32 devices in a mesh: blk: 8 (over z, y), rep: 4 (over x, core).
Axes of the slice: x: 2, y: 2, z: 4, core: 2. Of those that a mesh axis runs over, the one named last changes fastest.
Arguments:
- dense: bfloat16 [32768, 1024], P(('blk', 'rep')), may hold values from -6 to 6
- labels: int32 [32768], P(('blk', 'rep')), may hold values 0 or 1
- tile_values: bfloat16 [1024, 64, 128], P(('blk', 'rep')), may hold values from -1.1953125 to 1.1953125
- tile_block: int32 [1024, 64], P(('blk', 'rep')), may hold values from 0 to 1023
- tile_example: int32 [1024, 64], P(('blk', 'rep')), may hold values from 0 to 1023
- tile_count: int32 [1024], P(('blk', 'rep')), may hold values from 16 to 64, as said below
- z_state: float32 [32768, 128], P(('blk', 'rep')), may hold values from -6 to 6
- n_state: float32 [32768, 128], P(('blk', 'rep')), may hold values from 0.01 to 4
- w_one: bfloat16 [1024, 512], replicated, may hold values from -0.1875 to 0.1875
- b_one: float32 [512], replicated, may hold values from -3 to 3
- w_two: bfloat16 [512, 256], replicated, may hold values from -0.25 to 0.25
- b_two: float32 [256], replicated, may hold values from -3 to 3
- head: bfloat16 [256], replicated, may hold values from -0.375 to 0.375
Outputs:
- probability: float32 [32768], P(('blk', 'rep'))
- z_new: float32 [32768, 128], P(('blk', 'rep'))
- n_new: float32 [32768, 128], P(('blk', 'rep'))
- grad_w_one: float32 [1024, 512], replicated
- grad_b_one: float32 [512], replicated
- grad_w_two: float32 [512, 256], replicated
- grad_b_two: float32 [256], replicated
- grad_head: float32 [256], replicated
The draws below stay inside these ranges and needn't reach their ends.
Inputs may be any that keep to these rules, and one draw needn't show every extreme that they name: `tile_count`: slots at or beyond a list's count are padding; in every draw some owners receive 64 live slots from every device.
All inputs are finite; a program needn't handle non-finite values. No bound on the sum of `labels` on one device may be relied on, other than what follows from the above.
Results may differ from the reference program's by a relative error of at most 0.013.
Values may be sent and summed in bfloat16 or wider, within the bound.
No kernel may reach another device: no remote copies, remote signals or barrier semaphores. Data moves between devices by JAX's collectives and lax.ppermute only.
A program may use at most 64 MiB of HBM per device.

```python
import math
import jax
import jax.numpy as jnp
from jax import lax

W = 128
DIN = 1024
H1 = 512
H2 = 256
B_DEV = 1024
BLK_DEV = 1024
CAP = 64
OWNERS = 32
EXAMPLES = 32768
BLOCKS = 32768


def draw_tile_count(key, part):
    hot_key, base_key = jax.random.split(jax.random.fold_in(key, 11))
    order = jax.random.permutation(hot_key, OWNERS)
    hot = order < max(OWNERS // 16, 1)
    base = jax.random.randint(base_key, (OWNERS, OWNERS), CAP // 4, CAP // 2 + 1)
    counts = jnp.where(hot[None, :], CAP, base)
    return counts.reshape(OWNERS * OWNERS).astype(jnp.int32)


def draw_tile_block(key, part):
    first_key, second_key, table_key = jax.random.split(jax.random.fold_in(key, 23), 3)
    first = jax.random.randint(first_key, (OWNERS * OWNERS, CAP), 0, BLK_DEV)
    second = jax.random.randint(second_key, (OWNERS * OWNERS, CAP), 0, BLK_DEV)
    skewed = jnp.minimum(first * (second + 1) // BLK_DEV, BLK_DEV - 1)
    table = jax.random.permutation(table_key, BLK_DEV)
    return jnp.take(table, skewed).astype(jnp.int32)


def draw_tile_example(key, part):
    example_key = jax.random.fold_in(key, 37)
    return jax.random.randint(example_key, (OWNERS * OWNERS, CAP), 0, B_DEV).astype(jnp.int32)


def touch_ends(result, key, smallest, largest):
    longest = result.shape.index(max(result.shape))
    spots = []
    for shift in (0, 1):
        where = [jax.random.randint(jax.random.fold_in(key, axis), (), 0, length) for axis, length in enumerate(result.shape)]
        where[longest] = (where[longest] + shift) % result.shape[longest]
        spots.append(tuple(where))
    return result.at[spots[0]].set(smallest).at[spots[1]].set(largest)


def steps_of(key, shape, cuts, least, largest):
    gain, own = 1.0, jax.random.fold_in(key, 6)
    for axis_at, shards_of in cuts:
        heights = jnp.exp(jax.random.uniform(jax.random.fold_in(own, axis_at), (shards_of,), jnp.float32, least / len(cuts), largest / len(cuts)))
        gain = gain * jnp.repeat(heights, shape[axis_at] // shards_of).reshape([-1 if axis == axis_at else 1 for axis in range(len(shape))])
    return gain


def gaussian(rng, dims, deviation, limit, pieces=(), kind=jnp.bfloat16):
    level = steps_of(rng, dims, pieces, -0.22, 0.18) if pieces else 1.0
    entries = jax.random.normal(rng, dims, jnp.float32) * deviation * level
    return jnp.minimum(jnp.maximum(entries, -limit), limit).astype(kind)


def setup_inputs(seed: int = 0) -> dict:
    splits = jax.random.split(jax.random.key(seed), 14)
    dense = gaussian(splits[0], (EXAMPLES, DIN), 1.0, 6.0, ((0, 32),))
    labels = touch_ends((jax.random.randint(splits[1], (EXAMPLES,), 0, 4) < 1).astype(jnp.int32), jax.random.fold_in(splits[1], 1), 0, 1)
    tile_values = gaussian(splits[2], (OWNERS * OWNERS, CAP, W), 0.2, 1.1953125, ((0, 32),))
    tile_block = draw_tile_block(jax.random.fold_in(splits[13], 71), 0)
    tile_example = draw_tile_example(jax.random.fold_in(splits[13], 71), 0)
    tile_count = draw_tile_count(jax.random.fold_in(splits[13], 71), 0)
    z_state = gaussian(splits[6], (BLOCKS, W), 1.0, 6.0, ((0, 32),), jnp.float32)
    n_state = jnp.clip(jnp.exp(math.log(4.0) - 5.9914646 * jax.random.uniform(splits[7], (BLOCKS, W), jnp.float32) ** steps_of(splits[7], (BLOCKS, W), ((0, 32),), -0.2, 0.2)), 0.01, 4.0)
    w_one = gaussian(splits[8], (DIN, H1), DIN ** -0.5, 0.1875)
    b_one = gaussian(splits[9], (H1,), 0.5, 3.0, (), jnp.float32)
    w_two = gaussian(splits[10], (H1, H2), H1 ** -0.5, 0.25)
    b_two = gaussian(splits[11], (H2,), 0.5, 3.0, (), jnp.float32)
    head = gaussian(splits[12], (H2,), H2 ** -0.5, 0.375)
    return {"dense": dense, "labels": labels, "tile_values": tile_values, "tile_block": tile_block, "tile_example": tile_example, "tile_count": tile_count, "z_state": z_state, "n_state": n_state, "w_one": w_one, "b_one": b_one, "w_two": w_two, "b_two": b_two, "head": head}


alpha_rate = 0.5
beta_shift = 1.0
lasso_term = 0.5
ridge_term = 0.1

def wide_weight(z_state, n_state):
    shrunk = z_state - jnp.sign(z_state) * lasso_term
    denominator = (beta_shift + jnp.sqrt(n_state)) / alpha_rate + ridge_term
    return jnp.where(jnp.abs(z_state) > lasso_term, -shrunk / denominator, jnp.zeros_like(z_state))

def silu_slope(pre):
    gate = jax.nn.sigmoid(pre)
    return gate * (1.0 + pre * (1.0 - gate))

def live_values(values, counts):
    slots = jnp.arange(values.shape[1], dtype=jnp.int32)
    live = slots[None, :] < counts[:, None]
    return jnp.where(live[:, :, None], values, jnp.zeros_like(values))

def reference(dense, labels, tile_values, tile_block, tile_example, tile_count, z_state, n_state, w_one, b_one, w_two, b_two, head):
    weight = wide_weight(z_state, n_state)
    owner_base = (jnp.arange(OWNERS, dtype=jnp.int32) * BLK_DEV)[:, None]
    sources = jnp.arange(OWNERS, dtype=jnp.int32)

    def source_rows(src):
        start = (src * OWNERS).astype(jnp.int32)
        values = live_values(lax.dynamic_slice_in_dim(tile_values, start, OWNERS, 0), lax.dynamic_slice_in_dim(tile_count, start, OWNERS, 0))
        blocks = (lax.dynamic_slice_in_dim(tile_block, start, OWNERS, 0) + owner_base).astype(jnp.int32)
        examples = lax.dynamic_slice_in_dim(tile_example, start, OWNERS, 0).astype(jnp.int32)
        return (values, blocks, examples)

    def source_logits(src):
        values, blocks, examples = source_rows(src)
        picked = jnp.take(weight, blocks.reshape(-1), axis=0)
        tile_logit = lax.optimization_barrier(jnp.sum(values.reshape(-1, W).astype(jnp.float32) * picked, axis=1))
        return jax.ops.segment_sum(tile_logit, examples.reshape(-1), num_segments=B_DEV)
    wide = lax.map(source_logits, sources).reshape(EXAMPLES)
    pre_one = jnp.dot(dense, w_one, preferred_element_type=jnp.float32) + b_one
    hid_one = jax.nn.silu(pre_one).astype(jnp.bfloat16)
    pre_two = jnp.dot(hid_one, w_two, preferred_element_type=jnp.float32) + b_two
    hid_two = jax.nn.silu(pre_two).astype(jnp.bfloat16)
    deep = jnp.dot(hid_two, head, preferred_element_type=jnp.float32)
    probability = jax.nn.sigmoid(wide + deep)
    residual = probability - labels.astype(jnp.float32)

    def add_source(total, src):
        values, blocks, examples = source_rows(src)
        own = lax.dynamic_slice_in_dim(residual, (src * B_DEV).astype(jnp.int32), B_DEV, 0)
        tile_residual = jnp.take(own, examples.reshape(-1))
        contrib = values.reshape(-1, W).astype(jnp.float32) * tile_residual[:, None]
        return (total.at[blocks.reshape(-1)].add(contrib), None)
    grad_block, _ = lax.scan(add_source, jnp.zeros((BLOCKS, W), jnp.float32), sources)
    n_new = n_state + grad_block * grad_block
    sigma = (jnp.sqrt(n_new) - jnp.sqrt(n_state)) / alpha_rate
    z_new = z_state + grad_block - sigma * weight
    dlogit = residual.astype(jnp.bfloat16)
    grad_head = jnp.dot(dlogit, hid_two, preferred_element_type=jnp.float32)
    d_two = (dlogit.astype(jnp.float32)[:, None] * head.astype(jnp.float32)[None, :] * silu_slope(pre_two)).astype(jnp.bfloat16)
    grad_w_two = lax.dot_general(hid_one, d_two, (((0,), (0,)), ((), ())), preferred_element_type=jnp.float32)
    grad_b_two = lax.optimization_barrier(jnp.sum(d_two.astype(jnp.float32), axis=0))
    back_one = lax.dot_general(d_two, w_two, (((1,), (1,)), ((), ())), preferred_element_type=jnp.float32)
    d_one = (back_one * silu_slope(pre_one)).astype(jnp.bfloat16)
    grad_w_one = lax.dot_general(dense, d_one, (((0,), (0,)), ((), ())), preferred_element_type=jnp.float32)
    grad_b_one = lax.optimization_barrier(jnp.sum(d_one.astype(jnp.float32), axis=0))
    return (probability, z_new, n_new, grad_w_one, grad_b_one, grad_w_two, grad_b_two, grad_head)
```

```python
import functools
import jax
import jax.numpy as jnp
from jax import lax
from jax.experimental import pallas as pl
from jax.experimental.pallas import tpu as pltpu
from jax.sharding import PartitionSpec as P

alpha_rate = 0.5
beta_shift = 1.0
lasso_term = 0.5
ridge_term = 0.1

AXES = ("blk", "rep")
LANES = 128
f32 = jnp.float32
bf16 = jnp.bfloat16
NT = (((1,), (1,)), ((), ()))
NN = (((1,), (0,)), ((), ()))


def dot(a, b, dims=NN):
    return lax.dot_general(a, b, dims, preferred_element_type=f32)


def iota(shape, axis):
    return lax.broadcasted_iota(jnp.int32, shape, axis)


def split_two(x):
    top = x.astype(bf16)
    return top, (x - top.astype(f32)).astype(bf16)


def wide_weight(z, n):
    sign = jnp.where(z > 0, 1.0, jnp.where(z < 0, -1.0, 0.0))
    shrunk = z - sign * lasso_term
    denominator = (beta_shift + jnp.sqrt(n)) / alpha_rate + ridge_term
    return jnp.where(jnp.abs(z) > lasso_term, -shrunk / denominator, jnp.zeros_like(z))


def params(megabytes=40):
    return pltpu.CompilerParams(vmem_limit_bytes=megabytes << 20)


VM = pl.BlockSpec(memory_space=pltpu.VMEM)
ANY = pl.BlockSpec(memory_space=pl.ANY)


def pack_kernel(values_ref, block_ref, count_ref, out_ref):
    lists, cap = block_ref.shape
    dead_index = 64
    counts = jnp.sum(
        jnp.where(iota((lists, lists), 0) == iota((lists, lists), 1), count_ref[...], 0),
        axis=1,
        keepdims=True,
    )
    block = block_ref[...]
    high = jnp.where(iota((lists, cap), 1) < counts, block >> 5, dead_index)
    low = block & 31
    high = jnp.concatenate([high, high], axis=1).astype(f32)
    low = jnp.concatenate([low, low], axis=1).astype(f32)
    row = iota((8, LANES), 0)
    for k in range(lists):
        out_ref[k, 0:cap, :] = values_ref[k]
        tail = jnp.where(row == 0, high[k : k + 1], jnp.where(row == 1, low[k : k + 1], 0.0))
        out_ref[k, cap : cap + 8, :] = tail.astype(bf16)


def pack(values, block, count):
    lists, cap, width = values.shape
    return pl.pallas_call(
        pack_kernel,
        out_shape=jax.ShapeDtypeStruct((lists, cap + 8, width), bf16),
        in_specs=[VM, VM, VM],
        out_specs=VM,
        compiler_params=params(),
        name="pack",
    )(values, block, count.reshape(1, lists))


def to_column(row):
    return jnp.transpose(jnp.broadcast_to(row, (8, row.shape[1])))[:, 0:1]


def tower_kernel(
    dense_ref, w1_ref, b1_ref, w2_ref, b2_ref, head_ref, z_ref, n_ref,
    dense_t_ref, h1_ref, h2_ref, s2_ref, q_ref, deep_ref, wcat_ref,
    w1t, w2t,
):
    @pl.when(pl.program_id(0) == 0)
    def _():
        w1t[...] = jnp.transpose(w1_ref[...])
        w2t[...] = jnp.transpose(w2_ref[...])

    dense_t = jnp.transpose(dense_ref[...])
    dense_t_ref[...] = dense_t
    pre1 = dot(w1t[...], dense_t) + to_column(b1_ref[...])
    gate1 = jax.nn.sigmoid(pre1)
    h1 = (pre1 * gate1).astype(bf16)
    h1_ref[...] = h1
    slope1 = gate1 * (1.0 + pre1 * (1.0 - gate1))
    pre2 = dot(w2t[...], h1) + to_column(b2_ref[...])
    gate2 = jax.nn.sigmoid(pre2)
    h2 = (pre2 * gate2).astype(bf16)
    h2_ref[...] = h2
    head = head_ref[...]
    deep_ref[...] = dot(jnp.broadcast_to(head, (16, head.shape[1])), h2)[0:1]
    s2 = to_column(head.astype(f32)) * (gate2 * (1.0 + pre2 * (1.0 - gate2)))
    s2_ref[...] = s2
    q_ref[...] = dot(w2_ref[...], s2.astype(bf16)) * slope1
    wcat_ref[...] = jnp.concatenate(split_two(wide_weight(z_ref[...], n_ref[...])), axis=1)


def tower(dense, w1, b1, w2, b2, head, z, n):
    ex, din = dense.shape
    h1, h2 = w2.shape
    blocks, width = z.shape
    steps = 4
    be, bb = ex // steps, blocks // steps
    whole = lambda a: pl.BlockSpec(a.shape, lambda i: (0, 0))
    cols = lambda rows: pl.BlockSpec((rows, be), lambda i: (0, i))
    b1, b2, head = b1.reshape(1, h1), b2.reshape(1, h2), head.reshape(1, h2)
    return pl.pallas_call(
        tower_kernel,
        grid=(steps,),
        out_shape=(
            jax.ShapeDtypeStruct((din, ex), bf16),
            jax.ShapeDtypeStruct((h1, ex), bf16),
            jax.ShapeDtypeStruct((h2, ex), bf16),
            jax.ShapeDtypeStruct((h2, ex), f32),
            jax.ShapeDtypeStruct((h1, ex), f32),
            jax.ShapeDtypeStruct((1, ex), f32),
            jax.ShapeDtypeStruct((blocks, 2 * width), bf16),
        ),
        in_specs=[
            pl.BlockSpec((be, din), lambda i: (i, 0)),
            whole(w1), whole(b1), whole(w2), whole(b2), whole(head),
            pl.BlockSpec((bb, width), lambda i: (i, 0)),
            pl.BlockSpec((bb, width), lambda i: (i, 0)),
        ],
        out_specs=(
            cols(din), cols(h1), cols(h2), cols(h2), cols(h1), cols(1),
            pl.BlockSpec((bb, 2 * width), lambda i: (i, 0)),
        ),
        scratch_shapes=[pltpu.VMEM((h1, din), bf16), pltpu.VMEM((h2, h1), bf16)],
        compiler_params=params(),
        cost_estimate=pl.CostEstimate(
            flops=2 * ex * (din * h1 + 2 * h1 * h2), bytes_accessed=12 << 20, transcendentals=ex * (h1 + h2)
        ),
        name="tower",
    )(dense, w1, b1, w2, b2, head, z, n)


def four_lists(got_ref, at, cap):
    planes = [got_ref[at + k] for k in range(4)]
    values = jnp.concatenate([p[0:cap] for p in planes], axis=0)
    index = [p[cap : cap + 1].astype(f32) * 32.0 + p[cap + 1 : cap + 2].astype(f32) for p in planes]
    left = iota((1, LANES), 1) < cap
    pairs = [jnp.where(left, index[0], index[1]), jnp.where(left, index[2], index[3])]
    return values, jnp.concatenate(pairs, axis=1).astype(jnp.int32)


def logit_kernel(got_ref, wcat_ref, out_ref):
    lists = got_ref.shape[0]
    cap = got_ref.shape[1] - 8
    blocks = wcat_ref.shape[0]
    for at in range(0, lists, 4):
        values, index = four_lists(got_ref, at, cap)
        every = dot(wcat_ref[...], jnp.concatenate([values, values], axis=1), NT)
        picked = jnp.where(iota((blocks, 4 * cap), 0) == index, every, 0.0)
        logit = jnp.sum(picked, axis=0, keepdims=True)
        for k in range(4):
            out_ref[at + k] = logit[:, (k // 2) * LANES : (k // 2 + 1) * LANES]


def slot_logits(got, wcat):
    lists = got.shape[0]
    return pl.pallas_call(
        logit_kernel,
        out_shape=jax.ShapeDtypeStruct((lists, 1, LANES), f32),
        in_specs=[VM, VM],
        out_specs=VM,
        compiler_params=params(),
        name="slot_logits",
    )(got, wcat)


def step_kernel(
    logit_ref, example_ref, deep_ref, label_ref, dense_any, h1_any, h2_any, s2_any, q_any,
    prob_ref, out_ref, send_ref, keep_ref,
    marks, spread, dense_t, h1, h2, s2, q, sems,
):
    lists, cap = example_ref.shape
    ex = deep_ref.shape[1]
    rows = ex // LANES
    core = lax.axis_index("rep") & 1
    copies = [
        pltpu.make_async_copy(src, dst, sems.at[k])
        for k, (src, dst) in enumerate(
            ((q_any, q), (s2_any, s2), (h2_any, h2), (dense_any, dense_t), (h1_any, h1))
        )
    ]
    for copy in copies:
        copy.start()
    example = jnp.concatenate([example_ref[...], example_ref[...]], axis=1)
    high, low = example >> 7, example & (LANES - 1)
    mine = (iota((lists, LANES), 1) >= cap) == (core == 1)
    high_mine = jnp.where(mine, high, -1)
    down = iota((rows, LANES), 0)
    down_all = iota((LANES, LANES), 0)
    for k in range(lists):
        at = slice(k * LANES, (k + 1) * LANES)
        part = jnp.where(high_mine[k : k + 1] == down, logit_ref[k], 0.0)
        spread[:, at] = jnp.concatenate(split_two(part), axis=0)
        marks[:, at] = jnp.where(low[k : k + 1] == down_all, 1.0, 0.0).astype(bf16)
    wide = dot(spread[...], marks[...], NT)
    wide = wide[0:rows] + wide[rows:]
    deep = jnp.concatenate([deep_ref[:, k * LANES : (k + 1) * LANES] for k in range(rows)], axis=0)
    prob = jax.nn.sigmoid(wide + deep)
    prob_ref[...] = prob
    residual = prob - label_ref[...].astype(f32)
    found = dot(jnp.concatenate(split_two(residual), axis=0), marks[...])
    found = found[0:rows] + found[rows:]
    for k in range(lists):
        part = found[:, k * LANES : (k + 1) * LANES]
        out_ref[k, 0:8, :] = jnp.broadcast_to(
            jnp.sum(jnp.where(high[k : k + 1] == down, part, 0.0), axis=0, keepdims=True), (8, LANES)
        )
    dlogit = jnp.concatenate([residual[k : k + 1] for k in range(rows)], axis=1)
    dlogit = dlogit.astype(bf16).astype(f32)
    for copy in copies[0:3]:
        copy.wait()
    d_one = (q[...] * dlogit).astype(bf16)
    d_two = (s2[...] * dlogit).astype(bf16)
    head_part = h2[...].astype(f32) * dlogit
    fold = lambda a: functools.reduce(
        jnp.add, [a[:, k * LANES : (k + 1) * LANES].astype(f32) for k in range(rows)]
    )
    small = jnp.concatenate([fold(d_one), fold(d_two), fold(head_part)], axis=0)
    ones = jnp.ones((16, 2 * LANES), bf16)
    sums = dot(ones, jnp.concatenate(split_two(small), axis=1), NT)[0:1]
    count = sums.shape[1] // LANES
    sums = jnp.concatenate([sums[:, k * LANES : (k + 1) * LANES] for k in range(count)], axis=0)
    for k in range(lists):
        out_ref[k, 8 : 8 + count, :] = sums
    for copy in copies[3:]:
        copy.wait()
    big, packed = dense_t.shape[0] // 2, h1.shape[0] // 4
    width = d_two.shape[0]
    for half, target in ((1 - core, send_ref), (core, keep_ref)):
        part = dense_t[pl.ds(pl.multiple_of(half * big, big), big), :]
        target[0:big, :] = dot(part, d_one, NT).astype(bf16)
        for side in range(2):
            at = pl.multiple_of(half * packed + side * 2 * packed, packed)
            target[big:, side * width : (side + 1) * width] = dot(h1[pl.ds(at, packed), :], d_two, NT).astype(bf16)


def step(logits, example, deep, labels, dense_t, h1, h2, s2, q):
    lists, cap = example.shape
    ex = deep.shape[1]
    rows = ex // LANES
    n1, n2 = h1.shape[0], h2.shape[0]
    half = dense_t.shape[0] // 2 + n1 // 4
    count = (n1 + 2 * n2) // LANES
    big = (dense_t, h1, h2, s2, q)
    return pl.pallas_call(
        step_kernel,
        out_shape=(
            jax.ShapeDtypeStruct((rows, LANES), f32),
            jax.ShapeDtypeStruct((lists, 8 + count, LANES), f32),
            jax.ShapeDtypeStruct((half, n1), bf16),
            jax.ShapeDtypeStruct((half, n1), bf16),
        ),
        in_specs=[VM, VM, VM, VM] + [ANY] * 5,
        out_specs=(VM, VM, VM, VM),
        scratch_shapes=[
            pltpu.VMEM((LANES, lists * LANES), bf16),
            pltpu.VMEM((2 * rows, lists * LANES), bf16),
        ]
        + [pltpu.VMEM(a.shape, a.dtype) for a in big]
        + [pltpu.SemaphoreType.DMA((5,))],
        compiler_params=params(),
        name="step",
    )(logits, example, deep, labels.reshape(rows, LANES), *big)


def state_kernel(got_ref, res_ref, z_ref, n_ref, z_out, n_out, small_ref):
    lists = got_ref.shape[0]
    cap = got_ref.shape[1] - 8
    blocks, width = z_ref.shape
    left = iota((1, LANES), 1) < cap
    grad = jnp.zeros((blocks, width), f32)
    for at in range(0, lists, 4):
        values, index = four_lists(got_ref, at, cap)
        res = [res_ref[at + k, 0:1, :] for k in range(4)]
        res = jnp.concatenate([jnp.where(left, res[0], res[1]), jnp.where(left, res[2], res[3])], axis=1)
        top, rest = split_two(jnp.where(iota((blocks, 4 * cap), 0) == index, res, 0.0))
        grad = grad + dot(jnp.concatenate([top, rest], axis=1), jnp.concatenate([values, values], axis=0))
    z, n = z_ref[...], n_ref[...]
    n_new = n + grad * grad
    sigma = (jnp.sqrt(n_new) - jnp.sqrt(n)) / alpha_rate
    n_out[...] = n_new
    z_out[...] = z + grad - sigma * wide_weight(z, n)
    small_ref[...] = functools.reduce(jnp.add, [res_ref[k, 8:, :] for k in range(lists)])


def new_states(got, res, z, n):
    count = res.shape[1] - 8
    return pl.pallas_call(
        state_kernel,
        out_shape=(
            jax.ShapeDtypeStruct(z.shape, f32),
            jax.ShapeDtypeStruct(z.shape, f32),
            jax.ShapeDtypeStruct((count, LANES), f32),
        ),
        in_specs=[VM] * 4,
        out_specs=(VM, VM, VM),
        compiler_params=params(),
        name="new_states",
    )(got, res, z, n)


def every_to_every(x):
    return lax.all_to_all(x, AXES, split_axis=0, concat_axis=0, tiled=True)


def swap(x, bit, devices):
    return lax.ppermute(x, AXES, [(i, i ^ bit) for i in range(devices)])


def add(a, b):
    return (a.astype(f32) + b.astype(f32)).astype(bf16)


def halves(x, side):
    rows = x.shape[0] // 2
    return lax.dynamic_slice_in_dim(x, side * rows, rows, 0)


def sum_everywhere(pieces, me, devices):
    bits = [1 << k for k in range(1, devices.bit_length() - 1)]
    inner, last = bits[:-1], bits[-1]
    orders = [inner, inner[-1:] + inner[:-1]]
    pieces = list(pieces)
    for k in range(len(inner)):
        got = []
        for p, order in zip(pieces, orders):
            side = (me // order[k]) % 2
            got.append(swap(halves(p, 1 - side), order[k], devices))
        pieces = [
            add(halves(p, (me // order[k]) % 2), g) for p, order, g in zip(pieces, orders, got)
        ]
    pieces = [add(p, g) for p, g in zip(pieces, [swap(p, last, devices) for p in pieces])]
    for k in reversed(range(len(inner))):
        got = [swap(p, order[k], devices) for p, order in zip(pieces, orders)]
        joined = []
        for p, order, g in zip(pieces, orders, got):
            side = (me // order[k]) % 2
            joined.append(jnp.concatenate([jnp.where(side == 0, p, g), jnp.where(side == 0, g, p)], axis=0))
        pieces = joined
    return pieces


def per_device(
    devices,
    dense,
    labels,
    tile_values,
    tile_block,
    tile_example,
    tile_count,
    z_state,
    n_state,
    w_one,
    b_one,
    w_two,
    b_two,
    head,
):
    n1, n2 = w_two.shape
    din = dense.shape[1]
    me = lax.axis_index(AXES)
    core = me % 2
    got = every_to_every(pack(tile_values, tile_block, tile_count))
    dense_t, h1, h2, s2, q, deep, wcat = tower(dense, w_one, b_one, w_two, b_two, head, z_state, n_state)
    logits = every_to_every(slot_logits(got, wcat))
    prob, res, send, keep = step(logits, tile_example, deep, labels, dense_t, h1, h2, s2, q)
    own = add(keep, swap(send, 1, devices))
    got_res = every_to_every(res)
    z_new, n_new, small = new_states(got, got_res, z_state, n_state)
    cut = own.shape[0] // 2
    own = jnp.concatenate(sum_everywhere((own[:cut], own[cut:]), me, devices), axis=0)
    other = swap(own, 1, devices)
    first, second = jnp.where(core == 0, own, other), jnp.where(core == 0, other, own)
    big = din // 2
    grad_w_one = jnp.concatenate([first[:big], second[:big]], axis=0).astype(f32)
    packed = jnp.concatenate([first[big:], second[big:]], axis=0).astype(f32)
    grad_w_two = jnp.concatenate([packed[:, :n2], packed[:, n2:]], axis=0)
    small = small.reshape(-1)
    return (
        prob.reshape(-1),
        z_new,
        n_new,
        grad_w_one,
        small[:n1],
        grad_w_two,
        small[n1 : n1 + n2],
        small[n1 + n2 :],
    )


def solution(mesh):
    placed = (
        P(AXES, None),
        P(AXES),
        P(AXES, None, None),
        P(AXES, None),
        P(AXES, None),
        P(AXES),
        P(AXES, None),
        P(AXES, None),
        P(),
        P(),
        P(),
        P(),
        P(),
    )
    devices = mesh.shape["blk"] * mesh.shape["rep"]
    return jax.shard_map(
        functools.partial(per_device, devices),
        mesh=mesh,
        in_specs=placed,
        out_specs=(P(AXES), P(AXES, None), P(AXES, None), P(), P(), P(), P(), P()),
        check_vma=False,
    )
```

```python
import functools
import jax
import jax.numpy as jnp
from jax import lax
from jax.experimental import pallas as pl
from jax.experimental.pallas import tpu as pltpu
from jax.sharding import PartitionSpec as P

alpha_rate = 0.5
beta_shift = 1.0
lasso_term = 0.5
ridge_term = 0.1

AXES = ("blk", "rep")
LANES = 128
f32 = jnp.float32
bf16 = jnp.bfloat16
NT = (((1,), (1,)), ((), ()))
NN = (((1,), (0,)), ((), ()))


def dot(a, b, dims=NN):
    return lax.dot_general(a, b, dims, preferred_element_type=f32)


def iota(shape, axis):
    return lax.broadcasted_iota(jnp.int32, shape, axis)


def split_two(x):
    top = x.astype(bf16)
    return top, (x - top.astype(f32)).astype(bf16)


def wide_weight(z, n):
    sign = jnp.where(z > 0, 1.0, jnp.where(z < 0, -1.0, 0.0))
    shrunk = z - sign * lasso_term
    denominator = (beta_shift + jnp.sqrt(n)) / alpha_rate + ridge_term
    return jnp.where(jnp.abs(z) > lasso_term, -shrunk / denominator, jnp.zeros_like(z))


def params(megabytes=40):
    return pltpu.CompilerParams(vmem_limit_bytes=megabytes << 20)


VM = pl.BlockSpec(memory_space=pltpu.VMEM)
ANY = pl.BlockSpec(memory_space=pl.ANY)
HBM = pl.BlockSpec(memory_space=pltpu.HBM)


def pack_kernel(values_any, block_any, count_any, out_any, block_ref, count_ref, buf, sems):
    lists, cap = block_ref.shape
    dead_index = 64
    parts = 4
    each = lists // parts
    small = [
        pltpu.make_async_copy(block_any, block_ref, sems.at[2 * parts]),
        pltpu.make_async_copy(count_any, count_ref, sems.at[2 * parts + 1]),
    ]
    spans = [pl.ds(k * each, each) for k in range(parts)]
    loads = [
        pltpu.make_async_copy(values_any.at[at], buf.at[at, pl.ds(0, cap)], sems.at[k])
        for k, at in enumerate(spans)
    ]
    stores = [
        pltpu.make_async_copy(buf.at[at], out_any.at[at], sems.at[parts + k]) for k, at in enumerate(spans)
    ]
    for copy in small + loads:
        copy.start()
    for copy in small:
        copy.wait()
    counts = jnp.sum(
        jnp.where(iota((lists, lists), 0) == iota((lists, lists), 1), count_ref[...], 0),
        axis=1,
        keepdims=True,
    )
    block = block_ref[...]
    high = jnp.where(iota((lists, cap), 1) < counts, block >> 5, dead_index)
    low = block & 31
    high = jnp.concatenate([high, high], axis=1).astype(f32)
    low = jnp.concatenate([low, low], axis=1).astype(f32)
    row = iota((8, LANES), 0)
    for k in range(lists):
        tail = jnp.where(row == 0, high[k : k + 1], jnp.where(row == 1, low[k : k + 1], 0.0))
        buf[k, cap : cap + 8, :] = tail.astype(bf16)
    for load, store in zip(loads, stores):
        load.wait()
        store.start()
    for store in stores:
        store.wait()


def pack(values, block, count):
    lists, cap, width = values.shape
    shape = (lists, cap + 8, width)
    return pl.pallas_call(
        pack_kernel,
        out_shape=jax.ShapeDtypeStruct(shape, bf16),
        in_specs=[ANY, ANY, ANY],
        out_specs=ANY,
        scratch_shapes=[
            pltpu.VMEM((lists, cap), jnp.int32),
            pltpu.VMEM((1, lists), jnp.int32),
            pltpu.VMEM(shape, bf16),
            pltpu.SemaphoreType.DMA((10,)),
        ],
        compiler_params=params(60),
        name="pack",
    )(values, block, count.reshape(1, lists))


def to_column(row):
    return jnp.transpose(jnp.broadcast_to(row, (8, row.shape[1])))[:, 0:1]


def tower_kernel(
    dense_ref, w1_ref, b1_ref, w2_ref, b2_ref, head_ref,
    big_ref, s2_ref, q_ref, deep_ref,
    w1t, w2t,
):
    @pl.when(pl.program_id(0) == 0)
    def _():
        w1t[...] = jnp.transpose(w1_ref[...])
        w2t[...] = jnp.transpose(w2_ref[...])

    din, n1, n2 = dense_ref.shape[1], w1t.shape[0], w2t.shape[0]
    dense_t = jnp.transpose(dense_ref[...])
    big_ref[0:din, :] = dense_t
    pre1 = dot(w1t[...], dense_t) + to_column(b1_ref[...])
    gate1 = jax.nn.sigmoid(pre1)
    h1 = (pre1 * gate1).astype(bf16)
    big_ref[din : din + n1, :] = h1
    slope1 = gate1 * (1.0 + pre1 * (1.0 - gate1))
    pre2 = dot(w2t[...], h1) + to_column(b2_ref[...])
    gate2 = jax.nn.sigmoid(pre2)
    h2 = (pre2 * gate2).astype(bf16)
    big_ref[din + n1 : din + n1 + n2, :] = h2
    head = head_ref[...]
    deep_ref[...] = dot(jnp.broadcast_to(head, (16, head.shape[1])), h2)[0:1]
    s2 = to_column(head.astype(f32)) * (gate2 * (1.0 + pre2 * (1.0 - gate2)))
    s2 = s2.astype(bf16)
    s2_ref[...] = s2
    q_ref[...] = (dot(w2_ref[...], s2) * slope1).astype(bf16)


def tower(dense, w1, b1, w2, b2, head):
    ex, din = dense.shape
    h1, h2 = w2.shape
    steps = 4
    be = ex // steps
    whole = lambda a: pl.BlockSpec(a.shape, lambda i: (0, 0))
    cols = lambda rows: pl.BlockSpec((rows, be), lambda i: (0, i))
    b1, b2, head = b1.reshape(1, h1), b2.reshape(1, h2), head.reshape(1, h2)
    return pl.pallas_call(
        tower_kernel,
        grid=(steps,),
        out_shape=(
            jax.ShapeDtypeStruct((din + h1 + h2, ex), bf16),
            jax.ShapeDtypeStruct((h2, ex), bf16),
            jax.ShapeDtypeStruct((h1, ex), bf16),
            jax.ShapeDtypeStruct((1, ex), f32),
        ),
        in_specs=[
            pl.BlockSpec((be, din), lambda i: (i, 0)),
            whole(w1), whole(b1), whole(w2), whole(b2), whole(head),
        ],
        out_specs=(cols(din + h1 + h2), cols(h2), cols(h1), cols(1)),
        scratch_shapes=[pltpu.VMEM((h1, din), bf16), pltpu.VMEM((h2, h1), bf16)],
        compiler_params=params(62),
        cost_estimate=pl.CostEstimate(
            flops=2 * ex * (din * h1 + 2 * h1 * h2), bytes_accessed=12 << 20, transcendentals=ex * (h1 + h2)
        ),
        name="tower",
    )(dense, w1, b1, w2, b2, head)


def weight_kernel(z_ref, n_ref, out_ref):
    out_ref[...] = jnp.concatenate(split_two(wide_weight(z_ref[...], n_ref[...])), axis=1)


def weights(z, n):
    blocks, width = z.shape
    return pl.pallas_call(
        weight_kernel,
        out_shape=jax.ShapeDtypeStruct((blocks, 2 * width), bf16),
        in_specs=[VM, VM],
        out_specs=VM,
        compiler_params=params(6),
        cost_estimate=pl.CostEstimate(flops=10 * z.size, bytes_accessed=12 * z.size, transcendentals=2 * z.size),
        name="weights",
    )(z, n)


def four_lists(got_ref, at, cap):
    planes = [got_ref[at + k] for k in range(4)]
    values = jnp.concatenate([p[0:cap] for p in planes], axis=0)
    index = [p[cap : cap + 1].astype(f32) * 32.0 + p[cap + 1 : cap + 2].astype(f32) for p in planes]
    left = iota((1, LANES), 1) < cap
    pairs = [jnp.where(left, index[0], index[1]), jnp.where(left, index[2], index[3])]
    return values, jnp.concatenate(pairs, axis=1).astype(jnp.int32)


def logit_kernel(got_ref, wcat_ref, out_ref):
    lists = got_ref.shape[0]
    cap = got_ref.shape[1] - 8
    blocks = wcat_ref.shape[0]
    for at in range(0, lists, 4):
        values, index = four_lists(got_ref, at, cap)
        every = dot(wcat_ref[...], jnp.concatenate([values, values], axis=1), NT)
        picked = jnp.where(iota((blocks, 4 * cap), 0) == index, every, 0.0)
        logit = jnp.sum(picked, axis=0, keepdims=True)
        for k in range(4):
            out_ref[at + k] = logit[:, (k // 2) * LANES : (k // 2 + 1) * LANES]


def slot_logits(got, wcat):
    lists = got.shape[0]
    return pl.pallas_call(
        logit_kernel,
        out_shape=jax.ShapeDtypeStruct((lists, 1, LANES), f32),
        in_specs=[VM, VM],
        out_specs=VM,
        compiler_params=params(16),
        name="slot_logits",
    )(got, wcat)


def doubled(example_ref):
    example = jnp.concatenate([example_ref[...], example_ref[...]], axis=1)
    return example >> 7, example & (LANES - 1)


def mark(low, marks):
    down = iota((LANES, LANES), 0)
    for k in range(low.shape[0]):
        marks[:, k * LANES : (k + 1) * LANES] = jnp.where(low[k : k + 1] == down, 1.0, 0.0).astype(bf16)


def marks_kernel(example_ref, marks_ref):
    mark(doubled(example_ref)[1], marks_ref)


def example_marks(example):
    lists = example.shape[0]
    return pl.pallas_call(
        marks_kernel,
        out_shape=jax.ShapeDtypeStruct((LANES, lists * LANES), bf16),
        in_specs=[VM],
        out_specs=VM,
        compiler_params=params(8),
        cost_estimate=pl.CostEstimate(flops=2 << 20, bytes_accessed=4 << 20, transcendentals=0),
        name="example_marks",
    )(example)


def half_copies(half, big_any, dense_t, h1, sems):
    each, packed = dense_t.shape[0], h1.shape[0] // 2
    copies = [
        pltpu.make_async_copy(big_any.at[pl.ds(pl.multiple_of(half * each, each), each)], dense_t, sems.at[0])
    ]
    for side in range(2):
        start = pl.multiple_of(2 * each + half * packed + side * 2 * packed, packed)
        copies.append(
            pltpu.make_async_copy(
                big_any.at[pl.ds(start, packed)], h1.at[pl.ds(side * packed, packed)], sems.at[1 + side]
            )
        )
    return copies


def half_gradients(residual, copies, s2, q, dense_t, h1, target):
    rows, half = residual.shape[0], dense_t.shape[0]
    packed, width = h1.shape[0] // 2, s2.shape[0]
    dlogit = jnp.concatenate([residual[k : k + 1] for k in range(rows)], axis=1)
    dlogit = dlogit.astype(bf16).astype(f32)
    d_two = (s2[...].astype(f32) * dlogit).astype(bf16)
    copies[1].wait()
    copies[2].wait()
    second = dot(h1[...], d_two, NT).astype(bf16)
    target[half:, 0:width] = second[0:packed]
    target[half:, width:] = second[packed:]
    d_one = (q[...].astype(f32) * dlogit).astype(bf16)
    copies[0].wait()
    target[0:half, :] = dot(dense_t[...], d_one, NT).astype(bf16)


def half_scratch(big, n1):
    half = (big.shape[0] - n1 - n1 // 2) // 2
    return [
        pltpu.VMEM((half, big.shape[1]), bf16),
        pltpu.VMEM((n1 // 2, big.shape[1]), bf16),
        pltpu.SemaphoreType.DMA((4,)),
    ]


def residual_kernel(
    logit_any, example_ref, deep_ref, label_ref, marks, s2, q, big_any,
    prob_ref, residual_ref, send_ref,
    spread, logit_ref, dense_t, h1, sems,
):
    lists, cap = example_ref.shape
    rows = label_ref.shape[0]
    core = lax.axis_index("rep") & 1
    first = pltpu.make_async_copy(logit_any, logit_ref, sems.at[3])
    first.start()
    copies = half_copies(1 - core, big_any, dense_t, h1, sems)
    for copy in copies:
        copy.start()
    high = doubled(example_ref)[0]
    mine = (iota((lists, LANES), 1) >= cap) == (core == 1)
    high = jnp.where(mine, high, -1)
    down = iota((rows, LANES), 0)
    first.wait()
    for k in range(lists):
        part = jnp.where(high[k : k + 1] == down, logit_ref[k], 0.0)
        spread[:, k * LANES : (k + 1) * LANES] = jnp.concatenate(split_two(part), axis=0)
    wide = dot(spread[...], marks[...], NT)
    wide = wide[0:rows] + wide[rows:]
    deep = jnp.concatenate([deep_ref[:, k * LANES : (k + 1) * LANES] for k in range(rows)], axis=0)
    prob = jax.nn.sigmoid(wide + deep)
    prob_ref[...] = prob
    residual = prob - label_ref[...].astype(f32)
    residual_ref[...] = residual
    half_gradients(residual, copies, s2, q, dense_t, h1, send_ref)


def residuals(logits, example, deep, labels, marks, s2, q, big):
    lists = example.shape[0]
    rows = deep.shape[1] // LANES
    n1 = q.shape[0]
    half = (big.shape[0] - n1 - s2.shape[0]) // 2 + n1 // 4
    return pl.pallas_call(
        residual_kernel,
        out_shape=(
            jax.ShapeDtypeStruct((rows, LANES), f32),
            jax.ShapeDtypeStruct((rows, LANES), f32),
            jax.ShapeDtypeStruct((half, n1), bf16),
        ),
        in_specs=[ANY] + [VM] * 6 + [HBM],
        out_specs=[VM, VM, VM],
        scratch_shapes=[pltpu.VMEM((2 * rows, lists * LANES), bf16), pltpu.VMEM(logits.shape, f32)]
        + half_scratch(big, n1),
        compiler_params=params(49),
        name="residuals",
    )(logits, example, deep, labels.reshape(rows, LANES), marks, s2, q, big)


def gradient_kernel(residual_ref, s2, q, big_any, keep_ref, dense_t, h1, sems):
    core = lax.axis_index("rep") & 1
    copies = half_copies(core, big_any, dense_t, h1, sems)
    for copy in copies:
        copy.start()
    half_gradients(residual_ref[...], copies, s2, q, dense_t, h1, keep_ref)


def gradients(residual, s2, q, big):
    n1, ex = q.shape
    half = (big.shape[0] - n1 - s2.shape[0]) // 2 + n1 // 4
    return pl.pallas_call(
        gradient_kernel,
        out_shape=jax.ShapeDtypeStruct((half, n1), bf16),
        in_specs=[VM] * 3 + [HBM],
        out_specs=VM,
        scratch_shapes=half_scratch(big, n1),
        compiler_params=params(49),
        cost_estimate=pl.CostEstimate(flops=2 * half * n1 * ex, bytes_accessed=6 << 20, transcendentals=0),
        name="gradients",
    )(residual, s2, q, big)


def slot_kernel(residual_ref, example_ref, s2_any, q_any, big_any, out_ref, marks, s2, q, h2, sems):
    h2_any = big_any.at[pl.ds(big_any.shape[0] - h2.shape[0], h2.shape[0])]
    copies = [
        pltpu.make_async_copy(src, dst, sems.at[k])
        for k, (src, dst) in enumerate(((q_any, q), (s2_any, s2), (h2_any, h2)))
    ]
    for copy in copies:
        copy.start()
    lists = example_ref.shape[0]
    rows = residual_ref.shape[0]
    high, low = doubled(example_ref)
    mark(low, marks)
    down = iota((rows, LANES), 0)
    residual = residual_ref[...]
    found = dot(jnp.concatenate(split_two(residual), axis=0), marks[...])
    found = found[0:rows] + found[rows:]
    for k in range(lists):
        part = found[:, k * LANES : (k + 1) * LANES]
        out_ref[k, 0:8, :] = jnp.broadcast_to(
            jnp.sum(jnp.where(high[k : k + 1] == down, part, 0.0), axis=0, keepdims=True), (8, LANES)
        )
    dlogit = jnp.concatenate([residual[k : k + 1] for k in range(rows)], axis=1)
    dlogit = dlogit.astype(bf16).astype(f32)

    def fold(a):
        return functools.reduce(
            jnp.add, [a[:, k * LANES : (k + 1) * LANES].astype(f32) for k in range(rows)]
        )

    for copy in copies:
        copy.wait()
    small = jnp.concatenate(
        [
            fold((q[...].astype(f32) * dlogit).astype(bf16)),
            fold((s2[...].astype(f32) * dlogit).astype(bf16)),
            fold(h2[...].astype(f32) * dlogit),
        ],
        axis=0,
    )
    ones = jnp.ones((16, 2 * LANES), bf16)
    sums = dot(ones, jnp.concatenate(split_two(small), axis=1), NT)[0:1]
    count = sums.shape[1] // LANES
    sums = jnp.concatenate([sums[:, k * LANES : (k + 1) * LANES] for k in range(count)], axis=0)
    for k in range(lists):
        out_ref[k, 8 : 8 + count, :] = sums


def slot_residuals(residual, example, s2, q, big):
    lists = example.shape[0]
    count = (q.shape[0] + 2 * s2.shape[0]) // LANES
    return pl.pallas_call(
        slot_kernel,
        out_shape=jax.ShapeDtypeStruct((lists, 8 + count, LANES), f32),
        in_specs=[VM] * 2 + [HBM] * 3,
        out_specs=VM,
        scratch_shapes=[
            pltpu.VMEM((LANES, lists * LANES), bf16),
            pltpu.VMEM(s2.shape, bf16),
            pltpu.VMEM(q.shape, bf16),
            pltpu.VMEM(s2.shape, bf16),
            pltpu.SemaphoreType.DMA((3,)),
        ],
        compiler_params=params(60),
        cost_estimate=pl.CostEstimate(flops=2 * q.size + (lists << 20), bytes_accessed=3 << 20, transcendentals=0),
        name="slot_residuals",
    )(residual, example, s2, q, big)


def state_kernel(got_ref, res_ref, z_ref, n_ref, z_out, n_out, small_ref):
    lists = got_ref.shape[0]
    cap = got_ref.shape[1] - 8
    blocks, width = z_ref.shape
    left = iota((1, LANES), 1) < cap
    grad = jnp.zeros((blocks, 2 * width), f32)
    for at in range(0, lists, 4):
        values, index = four_lists(got_ref, at, cap)
        res = [res_ref[at + k, 0:1, :] for k in range(4)]
        res = jnp.concatenate([jnp.where(left, res[0], res[1]), jnp.where(left, res[2], res[3])], axis=1)
        scaled = jnp.concatenate(split_two(values.astype(f32) * to_column(res)), axis=1)
        hit = jnp.where(iota((blocks, 4 * cap), 0) == index, 1.0, 0.0).astype(bf16)
        grad = grad + dot(hit, scaled)
    grad = grad[:, :width] + grad[:, width:]
    z, n = z_ref[...], n_ref[...]
    n_new = n + grad * grad
    sigma = (jnp.sqrt(n_new) - jnp.sqrt(n)) / alpha_rate
    n_out[...] = n_new
    z_out[...] = z + grad - sigma * wide_weight(z, n)
    small_ref[...] = functools.reduce(jnp.add, [res_ref[k, 8:, :] for k in range(lists)])


def new_states(got, res, z, n):
    count = res.shape[1] - 8
    return pl.pallas_call(
        state_kernel,
        out_shape=(
            jax.ShapeDtypeStruct(z.shape, f32),
            jax.ShapeDtypeStruct(z.shape, f32),
            jax.ShapeDtypeStruct((count, LANES), f32),
        ),
        in_specs=[VM] * 4,
        out_specs=(VM, VM, VM),
        compiler_params=params(16),
        cost_estimate=pl.CostEstimate(
            flops=4 * got.shape[0] * (got.shape[1] - 8) * z.size, bytes_accessed=4 << 20, transcendentals=2 * z.size
        ),
        name="new_states",
    )(got, res, z, n)


def every_to_every(x):
    return lax.all_to_all(x, AXES, split_axis=0, concat_axis=0, tiled=True)


def swap(x, bit, devices):
    return lax.ppermute(x, AXES, [(i, i ^ bit) for i in range(devices)])


def add(*terms):
    return functools.reduce(jnp.add, [t.astype(f32) for t in terms]).astype(bf16)


def halves(x, side):
    rows = x.shape[0] // 2
    return lax.dynamic_slice_in_dim(x, side * rows, rows, 0)


def hold(*values):
    return lax.optimization_barrier(values)


def sum_everywhere(x, me, devices, slots, states):
    bits = [1 << k for k in range(1, devices.bit_length() - 1)]
    quad, inner, last = bits[:2], bits[2:-1], bits[-1]
    at = (me // quad[0]) % 4
    others = [(3, quad[0] + quad[1]), (1, quad[0]), (2, quad[1])]
    rows = x.shape[0] // 4
    quarter = lambda k: lax.dynamic_slice_in_dim(x, (at ^ k) * rows, rows, 0)
    res = slots(x)
    x = add(quarter(0), *[swap(quarter(k), bit, devices) for k, bit in others])
    x, res = hold(x, res)
    res = every_to_every(res)
    for bit in inner:
        side = (me // bit) % 2
        x = add(halves(x, side), swap(halves(x, 1 - side), bit, devices))
    x, res = hold(x, res)
    made = states(res)
    x = add(x, swap(x, last, devices))
    x, *made = hold(x, *made)
    for bit in reversed(inner):
        side = (me // bit) % 2
        other = swap(x, bit, devices)
        x = jnp.concatenate([jnp.where(side == 0, x, other), jnp.where(side == 0, other, x)], axis=0)
    parts = [(0, x)] + [(k, swap(x, bit, devices)) for k, bit in others]
    whole = jnp.zeros((4 * x.shape[0], x.shape[1]), x.dtype)
    for k, part in parts:
        whole = lax.dynamic_update_slice_in_dim(whole, part, (at ^ k) * x.shape[0], 0)
    return whole, made


def per_device(
    devices,
    dense,
    labels,
    tile_values,
    tile_block,
    tile_example,
    tile_count,
    z_state,
    n_state,
    w_one,
    b_one,
    w_two,
    b_two,
    head,
):
    n1, n2 = w_two.shape
    din = dense.shape[1]
    me = lax.axis_index(AXES)
    core = me % 2
    got = every_to_every(pack(tile_values, tile_block, tile_count))
    big, s2, q, deep = tower(dense, w_one, b_one, w_two, b_two, head)
    wcat = weights(z_state, n_state)
    got, deep = lax.optimization_barrier((got, deep))
    logits = slot_logits(got, wcat)
    logits, example = hold(logits, tile_example)
    marks = example_marks(example)
    logits = every_to_every(logits)
    prob, residual, send = residuals(logits, tile_example, deep, labels, marks, s2, q, big)
    keep = gradients(residual, s2, q, big)
    own = add(keep, swap(send, 1, devices))

    def slots(x):
        seen = hold(x, residual)[1]
        return slot_residuals(seen, tile_example, s2, q, big)

    def states(res):
        return new_states(got, res, z_state, n_state)

    own, (z_new, n_new, small) = sum_everywhere(own, me, devices, slots, states)
    other = swap(own, 1, devices)
    first, second = jnp.where(core == 0, own, other), jnp.where(core == 0, other, own)
    big = din // 2
    grad_w_one = jnp.concatenate([first[:big], second[:big]], axis=0).astype(f32)
    packed = jnp.concatenate([first[big:], second[big:]], axis=0).astype(f32)
    grad_w_two = jnp.concatenate([packed[:, :n2], packed[:, n2:]], axis=0)
    small = small.reshape(-1)
    return (
        prob.reshape(-1),
        z_new,
        n_new,
        grad_w_one,
        small[:n1],
        grad_w_two,
        small[n1 : n1 + n2],
        small[n1 + n2 :],
    )


def solution(mesh):
    placed = (
        P(AXES, None),
        P(AXES),
        P(AXES, None, None),
        P(AXES, None),
        P(AXES, None),
        P(AXES),
        P(AXES, None),
        P(AXES, None),
        P(),
        P(),
        P(),
        P(),
        P(),
    )
    devices = mesh.shape["blk"] * mesh.shape["rep"]
    return jax.shard_map(
        functools.partial(per_device, devices),
        mesh=mesh,
        in_specs=placed,
        out_specs=(P(AXES), P(AXES, None), P(AXES, None), P(), P(), P(), P(), P()),
        check_vma=False,
    )
```

```python
import functools
import jax
import jax.numpy as jnp
from jax import lax
from jax.experimental import pallas as pl
from jax.experimental.pallas import tpu as pltpu
from jax.sharding import PartitionSpec as P

alpha_rate = 0.5
beta_shift = 1.0
lasso_term = 0.5
ridge_term = 0.1

AXES = ("blk", "rep")
LANES = 128
f32 = jnp.float32
bf16 = jnp.bfloat16
NT = (((1,), (1,)), ((), ()))
NN = (((1,), (0,)), ((), ()))


def dot(a, b, dims=NN):
    return lax.dot_general(a, b, dims, preferred_element_type=f32)


def iota(shape, axis):
    return lax.broadcasted_iota(jnp.int32, shape, axis)


def split_two(x):
    top = x.astype(bf16)
    return top, (x - top.astype(f32)).astype(bf16)


def wide_weight(z, n):
    sign = jnp.where(z > 0, 1.0, jnp.where(z < 0, -1.0, 0.0))
    shrunk = z - sign * lasso_term
    denominator = (beta_shift + jnp.sqrt(n)) / alpha_rate + ridge_term
    return jnp.where(jnp.abs(z) > lasso_term, -shrunk / denominator, jnp.zeros_like(z))


def params(megabytes=40):
    return pltpu.CompilerParams(vmem_limit_bytes=megabytes << 20)


VM = pl.BlockSpec(memory_space=pltpu.VMEM)
ANY = pl.BlockSpec(memory_space=pl.ANY)
HBM = pl.BlockSpec(memory_space=pltpu.HBM)


def pack_kernel(values_any, block_any, count_any, out_any, block_ref, count_ref, buf, sems):
    lists, cap = block_ref.shape
    dead_index = 64
    parts = 4
    each = lists // parts
    small = [
        pltpu.make_async_copy(block_any, block_ref, sems.at[2 * parts]),
        pltpu.make_async_copy(count_any, count_ref, sems.at[2 * parts + 1]),
    ]
    spans = [pl.ds(k * each, each) for k in range(parts)]
    loads = [
        pltpu.make_async_copy(values_any.at[at], buf.at[at, pl.ds(0, cap)], sems.at[k])
        for k, at in enumerate(spans)
    ]
    stores = [
        pltpu.make_async_copy(buf.at[at], out_any.at[at], sems.at[parts + k]) for k, at in enumerate(spans)
    ]
    for copy in small + loads:
        copy.start()
    for copy in small:
        copy.wait()
    counts = jnp.sum(
        jnp.where(iota((lists, lists), 0) == iota((lists, lists), 1), count_ref[...], 0),
        axis=1,
        keepdims=True,
    )
    block = block_ref[...]
    high = jnp.where(iota((lists, cap), 1) < counts, block >> 5, dead_index)
    low = block & 31
    high = jnp.concatenate([high, high], axis=1).astype(f32)
    low = jnp.concatenate([low, low], axis=1).astype(f32)
    row = iota((8, LANES), 0)
    for k in range(lists):
        tail = jnp.where(row == 0, high[k : k + 1], jnp.where(row == 1, low[k : k + 1], 0.0))
        buf[k, cap : cap + 8, :] = tail.astype(bf16)
    for load, store in zip(loads, stores):
        load.wait()
        store.start()
    for store in stores:
        store.wait()


def pack(values, block, count):
    lists, cap, width = values.shape
    shape = (lists, cap + 8, width)
    return pl.pallas_call(
        pack_kernel,
        out_shape=jax.ShapeDtypeStruct(shape, bf16),
        in_specs=[ANY, ANY, ANY],
        out_specs=ANY,
        scratch_shapes=[
            pltpu.VMEM((lists, cap), jnp.int32),
            pltpu.VMEM((1, lists), jnp.int32),
            pltpu.VMEM(shape, bf16),
            pltpu.SemaphoreType.DMA((10,)),
        ],
        compiler_params=params(60),
        name="pack",
    )(values, block, count.reshape(1, lists))


def to_column(row):
    return jnp.transpose(jnp.broadcast_to(row, (8, row.shape[1])))[:, 0:1]


def tower_kernel(
    dense_ref, w1_ref, b1_ref, w2_ref, b2_ref, head_ref,
    big_ref, s2_ref, q_ref, deep_ref,
    w1t, w2t,
):
    @pl.when(pl.program_id(0) == 0)
    def _():
        w1t[...] = jnp.transpose(w1_ref[...])
        w2t[...] = jnp.transpose(w2_ref[...])

    din, n1, n2 = dense_ref.shape[1], w1t.shape[0], w2t.shape[0]
    dense_t = jnp.transpose(dense_ref[...])
    big_ref[0:din, :] = dense_t
    pre1 = dot(w1t[...], dense_t) + to_column(b1_ref[...])
    gate1 = jax.nn.sigmoid(pre1)
    h1 = (pre1 * gate1).astype(bf16)
    big_ref[din : din + n1, :] = h1
    slope1 = gate1 * (1.0 + pre1 * (1.0 - gate1))
    pre2 = dot(w2t[...], h1) + to_column(b2_ref[...])
    gate2 = jax.nn.sigmoid(pre2)
    h2 = (pre2 * gate2).astype(bf16)
    big_ref[din + n1 : din + n1 + n2, :] = h2
    head = head_ref[...]
    deep_ref[...] = dot(jnp.broadcast_to(head, (16, head.shape[1])), h2)[0:1]
    s2 = to_column(head.astype(f32)) * (gate2 * (1.0 + pre2 * (1.0 - gate2)))
    s2 = s2.astype(bf16)
    s2_ref[...] = s2
    q_ref[...] = (dot(w2_ref[...], s2) * slope1).astype(bf16)


def tower(dense, w1, b1, w2, b2, head):
    ex, din = dense.shape
    h1, h2 = w2.shape
    steps = 4
    be = ex // steps
    whole = lambda a: pl.BlockSpec(a.shape, lambda i: (0, 0))
    cols = lambda rows: pl.BlockSpec((rows, be), lambda i: (0, i))
    b1, b2, head = b1.reshape(1, h1), b2.reshape(1, h2), head.reshape(1, h2)
    return pl.pallas_call(
        tower_kernel,
        grid=(steps,),
        out_shape=(
            jax.ShapeDtypeStruct((din + h1 + h2, ex), bf16),
            jax.ShapeDtypeStruct((h2, ex), bf16),
            jax.ShapeDtypeStruct((h1, ex), bf16),
            jax.ShapeDtypeStruct((1, ex), f32),
        ),
        in_specs=[
            pl.BlockSpec((be, din), lambda i: (i, 0)),
            whole(w1), whole(b1), whole(w2), whole(b2), whole(head),
        ],
        out_specs=(cols(din + h1 + h2), cols(h2), cols(h1), cols(1)),
        scratch_shapes=[pltpu.VMEM((h1, din), bf16), pltpu.VMEM((h2, h1), bf16)],
        compiler_params=params(62),
        cost_estimate=pl.CostEstimate(
            flops=2 * ex * (din * h1 + 2 * h1 * h2), bytes_accessed=12 << 20, transcendentals=ex * (h1 + h2)
        ),
        name="tower",
    )(dense, w1, b1, w2, b2, head)


def weight_kernel(z_ref, n_ref, out_ref):
    out_ref[...] = jnp.concatenate(split_two(wide_weight(z_ref[...], n_ref[...])), axis=1)


def weights(z, n):
    blocks, width = z.shape
    return pl.pallas_call(
        weight_kernel,
        out_shape=jax.ShapeDtypeStruct((blocks, 2 * width), bf16),
        in_specs=[VM, VM],
        out_specs=VM,
        compiler_params=params(6),
        cost_estimate=pl.CostEstimate(flops=10 * z.size, bytes_accessed=12 * z.size, transcendentals=2 * z.size),
        name="weights",
    )(z, n)


def four_lists(got_ref, at, cap):
    planes = [got_ref[at + k] for k in range(4)]
    values = jnp.concatenate([p[0:cap] for p in planes], axis=0)
    index = [p[cap : cap + 1].astype(f32) * 32.0 + p[cap + 1 : cap + 2].astype(f32) for p in planes]
    left = iota((1, LANES), 1) < cap
    pairs = [jnp.where(left, index[0], index[1]), jnp.where(left, index[2], index[3])]
    return values, jnp.concatenate(pairs, axis=1).astype(jnp.int32)


def logit_kernel(got_ref, wcat_ref, out_ref):
    lists = got_ref.shape[0]
    cap = got_ref.shape[1] - 8
    blocks = wcat_ref.shape[0]
    for at in range(0, lists, 4):
        values, index = four_lists(got_ref, at, cap)
        every = dot(wcat_ref[...], jnp.concatenate([values, values], axis=1), NT)
        picked = jnp.where(iota((blocks, 4 * cap), 0) == index, every, 0.0)
        logit = jnp.sum(picked, axis=0, keepdims=True)
        for k in range(4):
            out_ref[at + k] = logit[:, (k // 2) * LANES : (k // 2 + 1) * LANES]


def slot_logits(got, wcat):
    lists = got.shape[0]
    return pl.pallas_call(
        logit_kernel,
        out_shape=jax.ShapeDtypeStruct((lists, 1, LANES), f32),
        in_specs=[VM, VM],
        out_specs=VM,
        compiler_params=params(16),
        name="slot_logits",
    )(got, wcat)


def doubled(example_ref):
    example = jnp.concatenate([example_ref[...], example_ref[...]], axis=1)
    return example >> 7, example & (LANES - 1)


def mark(low, marks):
    down = iota((LANES, LANES), 0)
    for k in range(low.shape[0]):
        marks[:, k * LANES : (k + 1) * LANES] = jnp.where(low[k : k + 1] == down, 1.0, 0.0).astype(bf16)


def marks_kernel(example_ref, marks_ref):
    mark(doubled(example_ref)[1], marks_ref)


def example_marks(example):
    lists = example.shape[0]
    return pl.pallas_call(
        marks_kernel,
        out_shape=jax.ShapeDtypeStruct((LANES, lists * LANES), bf16),
        in_specs=[VM],
        out_specs=VM,
        compiler_params=params(8),
        cost_estimate=pl.CostEstimate(flops=2 << 20, bytes_accessed=4 << 20, transcendentals=0),
        name="example_marks",
    )(example)


def half_copies(half, big_any, dense_t, h1, sems):
    each, packed = dense_t.shape[0], h1.shape[0] // 2
    copies = [
        pltpu.make_async_copy(big_any.at[pl.ds(pl.multiple_of(half * each, each), each)], dense_t, sems.at[0])
    ]
    for side in range(2):
        start = pl.multiple_of(2 * each + half * packed + side * 2 * packed, packed)
        copies.append(
            pltpu.make_async_copy(
                big_any.at[pl.ds(start, packed)], h1.at[pl.ds(side * packed, packed)], sems.at[1 + side]
            )
        )
    return copies


def half_gradients(residual, copies, s2, q, dense_t, h1, target):
    rows, first = residual.shape[0], dense_t.shape[0] // 4
    packed, width = h1.shape[0] // 8, s2.shape[0]
    each = first + packed
    dlogit = jnp.concatenate([residual[k : k + 1] for k in range(rows)], axis=1)
    dlogit = dlogit.astype(bf16).astype(f32)
    d_two = (s2[...].astype(f32) * dlogit).astype(bf16)
    copies[1].wait()
    copies[2].wait()
    second = dot(h1[...], d_two, NT).astype(bf16)
    for k in range(4):
        at = k * packed
        target[k * each + first : (k + 1) * each, 0:width] = second[at : at + packed]
        target[k * each + first : (k + 1) * each, width:] = second[4 * packed + at : 5 * packed + at]
    d_one = (q[...].astype(f32) * dlogit).astype(bf16)
    copies[0].wait()
    made = dot(dense_t[...], d_one, NT).astype(bf16)
    for k in range(4):
        target[k * each : k * each + first, :] = made[k * first : (k + 1) * first]


def half_scratch(big, n1):
    half = (big.shape[0] - n1 - n1 // 2) // 2
    return [
        pltpu.VMEM((half, big.shape[1]), bf16),
        pltpu.VMEM((n1 // 2, big.shape[1]), bf16),
        pltpu.SemaphoreType.DMA((4,)),
    ]


def position():
    return lax.axis_index("blk") * lax.axis_size("rep") + lax.axis_index("rep")


def residual_kernel(
    logit_any, example_ref, deep_ref, label_ref, marks, s2, q, big_any,
    prob_ref, residual_ref, send_ref, slot_ref,
    spread, logit_ref, apart, dense_t, h1, sems,
):
    lists, cap = example_ref.shape
    rows = label_ref.shape[0]
    me = position()
    core = me & 1
    first = pltpu.make_async_copy(logit_any, logit_ref, sems.at[3])
    first.start()
    copies = half_copies(1 - core, big_any, dense_t, h1, sems)
    for copy in copies:
        copy.start()
    high = doubled(example_ref)[0]
    mine = (iota((lists, LANES), 1) >= cap) == (core == 1)
    high_mine = jnp.where(mine, high, -1)
    down = iota((rows, LANES), 0)
    first.wait()
    for k in range(lists):
        part = jnp.where(high_mine[k : k + 1] == down, logit_ref[k], 0.0)
        spread[:, k * LANES : (k + 1) * LANES] = jnp.concatenate(split_two(part), axis=0)
    wide = dot(spread[...], marks[...], NT)
    wide = wide[0:rows] + wide[rows:]
    deep = jnp.concatenate([deep_ref[:, k * LANES : (k + 1) * LANES] for k in range(rows)], axis=0)
    prob = jax.nn.sigmoid(wide + deep)
    prob_ref[...] = prob
    residual = prob - label_ref[...].astype(f32)
    residual_ref[...] = residual
    half_gradients(residual, copies, s2, q, dense_t, h1, send_ref)
    found = dot(jnp.concatenate(split_two(residual), axis=0), marks[...])
    found = found[0:rows] + found[rows:]
    for k in range(lists):
        part = jnp.where(high[k : k + 1] == down, found[:, k * LANES : (k + 1) * LANES], 0.0)
        top, rest = split_two(jnp.sum(part, axis=0, keepdims=True))
        apart[me ^ k] = jnp.concatenate([top.astype(f32), rest.astype(f32)], axis=0)
    for k in range(lists):
        for side in range(2):
            at = (k % 2) * 2 * LANES + side * LANES
            slot_ref[k // 2 : k // 2 + 1, at : at + LANES] = apart[k, side : side + 1, :]


def residuals(logits, example, deep, labels, marks, s2, q, big):
    lists = example.shape[0]
    rows = deep.shape[1] // LANES
    n1 = q.shape[0]
    half = (big.shape[0] - n1 - s2.shape[0]) // 2 + n1 // 4
    return pl.pallas_call(
        residual_kernel,
        out_shape=(
            jax.ShapeDtypeStruct((rows, LANES), f32),
            jax.ShapeDtypeStruct((rows, LANES), f32),
            jax.ShapeDtypeStruct((half, n1), bf16),
            jax.ShapeDtypeStruct((lists // 2, 4 * LANES), f32),
        ),
        in_specs=[ANY] + [VM] * 6 + [HBM],
        out_specs=[VM, VM, VM, VM],
        scratch_shapes=[pltpu.VMEM((2 * rows, lists * LANES), bf16), pltpu.VMEM(logits.shape, f32), pltpu.VMEM((lists, 2, LANES), f32)]
        + half_scratch(big, n1),
        compiler_params=params(49),
        name="residuals",
    )(logits, example, deep, labels.reshape(rows, LANES), marks, s2, q, big)


def gradient_kernel(residual_ref, s2, q, big_any, keep_ref, dense_t, h1, sems):
    core = lax.axis_index("rep") & 1
    copies = half_copies(core, big_any, dense_t, h1, sems)
    for copy in copies:
        copy.start()
    half_gradients(residual_ref[...], copies, s2, q, dense_t, h1, keep_ref)


def gradients(residual, s2, q, big):
    n1, ex = q.shape
    half = (big.shape[0] - n1 - s2.shape[0]) // 2 + n1 // 4
    return pl.pallas_call(
        gradient_kernel,
        out_shape=jax.ShapeDtypeStruct((half, n1), bf16),
        in_specs=[VM] * 3 + [HBM],
        out_specs=VM,
        scratch_shapes=half_scratch(big, n1),
        compiler_params=params(49),
        cost_estimate=pl.CostEstimate(flops=2 * half * n1 * ex, bytes_accessed=6 << 20, transcendentals=0),
        name="gradients",
    )(residual, s2, q, big)


def small_kernel(residual_ref, s2_any, q_any, big_any, out_ref, s2, q, h2, sems):
    h2_any = big_any.at[pl.ds(big_any.shape[0] - h2.shape[0], h2.shape[0])]
    copies = [
        pltpu.make_async_copy(src, dst, sems.at[k])
        for k, (src, dst) in enumerate(((q_any, q), (s2_any, s2), (h2_any, h2)))
    ]
    for copy in copies:
        copy.start()
    residual = residual_ref[...]
    rows = residual.shape[0]
    dlogit = jnp.concatenate([residual[k : k + 1] for k in range(rows)], axis=1)
    dlogit = dlogit.astype(bf16).astype(f32)

    def fold(a):
        return functools.reduce(
            jnp.add, [a[:, k * LANES : (k + 1) * LANES].astype(f32) for k in range(rows)]
        )

    for copy in copies:
        copy.wait()
    small = jnp.concatenate(
        [
            fold((q[...].astype(f32) * dlogit).astype(bf16)),
            fold((s2[...].astype(f32) * dlogit).astype(bf16)),
            fold(h2[...].astype(f32) * dlogit),
        ],
        axis=0,
    )
    ones = jnp.ones((16, 2 * LANES), bf16)
    sums = dot(ones, jnp.concatenate(split_two(small), axis=1), NT)[0:1]
    width = out_ref.shape[1]
    sums = jnp.concatenate([sums[:, k * width : (k + 1) * width] for k in range(sums.shape[1] // width)], axis=0)
    out_ref[...] = jnp.concatenate(split_two(sums), axis=0).astype(f32)


def small_gradients(residual, s2, q, big):
    count = (q.shape[0] + 2 * s2.shape[0]) // q.shape[0]
    return pl.pallas_call(
        small_kernel,
        out_shape=jax.ShapeDtypeStruct((2 * count, q.shape[0]), f32),
        in_specs=[VM] + [HBM] * 3,
        out_specs=VM,
        scratch_shapes=[
            pltpu.VMEM(s2.shape, bf16),
            pltpu.VMEM(q.shape, bf16),
            pltpu.VMEM(s2.shape, bf16),
            pltpu.SemaphoreType.DMA((3,)),
        ],
        compiler_params=params(60),
        cost_estimate=pl.CostEstimate(flops=8 * q.size, bytes_accessed=8 << 20, transcendentals=0),
        name="small_gradients",
    )(residual, s2, q, big)


def state_kernel(got_ref, res_ref, z_ref, n_ref, z_out, n_out):
    lists = got_ref.shape[0]
    me = position()
    cap = got_ref.shape[1] - 8
    blocks, width = z_ref.shape
    left = iota((1, LANES), 1) < cap
    grad = jnp.zeros((blocks, 2 * width), f32)
    for at in range(0, lists, 4):
        values, index = four_lists(got_ref, at, cap)
        apart = [me ^ (at + k) for k in range(4)]
        res = [res_ref[pl.ds((a & 1) * (lists // 2) + (a >> 1), 1), :] for a in apart]
        res = jnp.concatenate([jnp.where(left, res[0], res[1]), jnp.where(left, res[2], res[3])], axis=1)
        scaled = jnp.concatenate(split_two(values.astype(f32) * to_column(res)), axis=1)
        hit = jnp.where(iota((blocks, 4 * cap), 0) == index, 1.0, 0.0).astype(bf16)
        grad = grad + dot(hit, scaled)
    grad = grad[:, :width] + grad[:, width:]
    z, n = z_ref[...], n_ref[...]
    n_new = n + grad * grad
    sigma = (jnp.sqrt(n_new) - jnp.sqrt(n)) / alpha_rate
    n_out[...] = n_new
    z_out[...] = z + grad - sigma * wide_weight(z, n)


def new_states(got, res, z, n):
    return pl.pallas_call(
        state_kernel,
        out_shape=(jax.ShapeDtypeStruct(z.shape, f32), jax.ShapeDtypeStruct(z.shape, f32)),
        in_specs=[VM] * 4,
        out_specs=(VM, VM),
        compiler_params=params(16),
        cost_estimate=pl.CostEstimate(
            flops=4 * got.shape[0] * (got.shape[1] - 8) * z.size, bytes_accessed=4 << 20, transcendentals=2 * z.size
        ),
        name="new_states",
    )(got, res, z, n)


def place_half(half, quad, parts, w1_any, w2_any, wide, narrow, sems):
    each, width = parts[0].shape
    first, packed = wide.shape[0] // 4, narrow.shape[1] // 4
    copies = []
    for k, part in enumerate(parts):
        quarter = quad ^ k
        span = pl.ds(k * first, first)
        wide[span, :] = part[0:first, :].astype(f32)
        start = pl.multiple_of((half * 4 + quarter) * first, first)
        copies.append(pltpu.make_async_copy(wide.at[span], w1_any.at[pl.ds(start, first)], sems.at[3 * k]))
        copies[-1].start()
        for side in range(2):
            span = pl.ds(k * packed, packed)
            narrow[side, span, :] = part[first:each, side * (width // 2) : (side + 1) * (width // 2)].astype(f32)
            start = pl.multiple_of((side * 8 + half * 4 + quarter) * packed, packed)
            copies.append(
                pltpu.make_async_copy(narrow.at[side, span], w2_any.at[pl.ds(start, packed)], sems.at[3 * k + 1 + side])
            )
            copies[-1].start()
    for copy in copies:
        copy.wait()


def place_kernel(swapped, *refs):
    parts, (w1_any, w2_any, wide, narrow, sems) = refs[:4], refs[-5:]
    me = position()
    place_half((me & 1) ^ swapped, (me >> 1) & 3, parts, w1_any, w2_any, wide, narrow, sems)


def place(swapped, parts, first, packed, before=()):
    width = parts[0].shape[1]
    shapes = (
        jax.ShapeDtypeStruct((8 * first, width), f32),
        jax.ShapeDtypeStruct((16 * packed, width // 2), f32),
    )
    return pl.pallas_call(
        functools.partial(place_kernel, swapped),
        out_shape=shapes,
        in_specs=[VM] * 4 + [ANY] * len(before),
        out_specs=[ANY, ANY],
        input_output_aliases={4 + k: k for k in range(len(before))},
        scratch_shapes=[
            pltpu.VMEM((4 * first, width), f32),
            pltpu.VMEM((2, 4 * packed, width // 2), f32),
            pltpu.SemaphoreType.DMA((12,)),
        ],
        compiler_params=params(16),
        cost_estimate=pl.CostEstimate(flops=first * width, bytes_accessed=40 * first * width, transcendentals=0),
        name="place_other" if swapped else "place_own",
    )(*parts, *before)


def every_to_every(x):
    return lax.all_to_all(x, AXES, split_axis=0, concat_axis=0, tiled=True)


def swap(x, bit, devices):
    return lax.ppermute(x, AXES, [(i, i ^ bit) for i in range(devices)])


def add(*terms):
    return functools.reduce(jnp.add, [t.astype(f32) for t in terms]).astype(bf16)


def halves(x, side):
    rows = x.shape[0] // 2
    return lax.dynamic_slice_in_dim(x, side * rows, rows, 0)


def hold(*values):
    return lax.optimization_barrier(values)


def pair(x):
    top = lax.reduce_precision(x, 8, 7)
    return jnp.concatenate([top, x - top], axis=0).astype(bf16)


def whole(p):
    rows = p.shape[0] // 2
    return p[:rows].astype(f32) + p[rows:].astype(f32)


def sum_everywhere(x, slots, me, devices, small, states):
    bits = [1 << k for k in range(1, devices.bit_length() - 1)]
    quad, inner, last = bits[:2], bits[2:-1], bits[-1]
    at = (me // quad[0]) % 4
    others = [(3, quad[0] + quad[1]), (1, quad[0]), (2, quad[1])]
    join = lambda *parts: jnp.concatenate(parts, axis=0)
    wide = x.shape[1]
    slots = slots.astype(bf16).reshape(-1, 4, wide)
    rows = x.shape[0] // 4
    quarter = lambda k: lax.dynamic_slice_in_dim(x, (at ^ k) * rows, rows, 0)
    sums = small(x)
    got = {k: swap(join(quarter(k), slots[:, k]), bit, devices) for k, bit in others}
    slots = jnp.stack([slots[:, 0]] + [got[k][rows:] for k in (1, 2, 3)], axis=1)
    x = add(quarter(0), *[got[k][:rows] for k in (1, 2, 3)])
    x, sums = hold(x, sums)
    sums = whole(sums)
    for bit in inner + [last]:
        side = (me // bit) % 2
        mine, theirs = (x, x) if bit == last else (halves(x, side), halves(x, 1 - side))
        slots = slots.reshape(slots.shape[0] // 2, 2, -1, wide)
        ride, extra = slots[:, 1].reshape(-1, wide), pair(sums)
        got = swap(join(theirs, ride, extra), bit, devices)
        n, m = theirs.shape[0], ride.shape[0]
        x = add(mine, got[:n])
        slots = jnp.stack([slots[:, 0], got[n : n + m].reshape(slots[:, 0].shape)], axis=1)
        slots = slots.reshape(slots.shape[0], -1, wide)
        sums = sums + whole(got[n + m :])
    slots = slots.reshape(-1, 2, wide // 2)
    far = swap(slots[:, 1], 1, devices)
    made = states(whole(jnp.stack([*jnp.split(join(slots[:, 0], far), 2, axis=1)]).reshape(-1, wide // 4)))
    for bit in reversed(inner):
        side = (me // bit) % 2
        other = swap(x, bit, devices)
        x = join(jnp.where(side == 0, x, other), jnp.where(side == 0, other, x))
    n = x.shape[0]
    message = join(x, pair(sums))
    got = {k: swap(message, bit, devices) for k, bit in others}
    parts = [x] + [got[k][:n] for k in (1, 2, 3)]
    sums = sums + sum(whole(got[k][n:]) for k in (1, 2, 3))
    parts[0], *made = hold(parts[0], *made)
    return parts, sums, made


def per_device(
    devices,
    dense,
    labels,
    tile_values,
    tile_block,
    tile_example,
    tile_count,
    z_state,
    n_state,
    w_one,
    b_one,
    w_two,
    b_two,
    head,
):
    n1, n2 = w_two.shape
    din = dense.shape[1]
    me = lax.axis_index(AXES)
    got = every_to_every(pack(tile_values, tile_block, tile_count))
    big, s2, q, deep = tower(dense, w_one, b_one, w_two, b_two, head)
    wcat = weights(z_state, n_state)
    got, deep = lax.optimization_barrier((got, deep))
    logits = slot_logits(got, wcat)
    logits, example = hold(logits, tile_example)
    marks = example_marks(example)
    logits = every_to_every(logits)
    prob, residual, send, slots = residuals(logits, tile_example, deep, labels, marks, s2, q, big)
    keep = gradients(residual, s2, q, big)
    own = add(keep, swap(send, 1, devices))

    def small(x):
        return small_gradients(hold(x, residual)[1], s2, q, big)

    def states(res):
        return new_states(got, res, z_state, n_state)

    parts, sums, (z_new, n_new) = sum_everywhere(own, slots, me, devices, small, states)
    first, packed = din // 8, n1 // 16
    order = (3, 1, 2, 0)
    others = {k: swap(parts[k], 1, devices) for k in order[:-1]}
    rows = parts[0].shape[0]
    final = swap(jnp.concatenate([parts[0], pair(sums)], axis=0), 1, devices)
    sums = (sums + whole(final[rows:])).reshape(-1)
    others[0] = final[:rows]
    placed = place(0, parts, first, packed)
    grad_w_one, grad_w_two = place(1, [others[k] for k in range(4)], first, packed, placed)
    return (
        prob.reshape(-1),
        z_new,
        n_new,
        grad_w_one,
        sums[:n1],
        grad_w_two,
        sums[n1 : n1 + n2],
        sums[n1 + n2 :],
    )


def solution(mesh):
    placed = (
        P(AXES, None),
        P(AXES),
        P(AXES, None, None),
        P(AXES, None),
        P(AXES, None),
        P(AXES),
        P(AXES, None),
        P(AXES, None),
        P(),
        P(),
        P(),
        P(),
        P(),
    )
    devices = mesh.shape["blk"] * mesh.shape["rep"]
    return jax.shard_map(
        functools.partial(per_device, devices),
        mesh=mesh,
        in_specs=placed,
        out_specs=(P(AXES), P(AXES, None), P(AXES, None), P(), P(), P(), P(), P()),
        check_vma=False,
    )
```

```python
import functools
import jax
import jax.numpy as jnp
from jax import lax
from jax.experimental import pallas as pl
from jax.experimental.pallas import tpu as pltpu
from jax.sharding import PartitionSpec as P

alpha_rate = 0.5
beta_shift = 1.0
lasso_term = 0.5
ridge_term = 0.1

AXES = ("blk", "rep")
LANES = 128
EIGHTHS = 8
ONES = 16
f32 = jnp.float32
bf16 = jnp.bfloat16
NT = (((1,), (1,)), ((), ()))
NN = (((1,), (0,)), ((), ()))


def dot(a, b, dims=NN):
    return lax.dot_general(a, b, dims, preferred_element_type=f32)


def iota(shape, axis):
    return lax.broadcasted_iota(jnp.int32, shape, axis)


def split_two(x):
    top = x.astype(bf16)
    return top, (x - top.astype(f32)).astype(bf16)


def wide_weight(z, n):
    sign = jnp.where(z > 0, 1.0, jnp.where(z < 0, -1.0, 0.0))
    shrunk = z - sign * lasso_term
    denominator = (beta_shift + jnp.sqrt(n)) / alpha_rate + ridge_term
    return jnp.where(jnp.abs(z) > lasso_term, -shrunk / denominator, jnp.zeros_like(z))


def params(megabytes=40):
    return pltpu.CompilerParams(vmem_limit_bytes=megabytes << 20)


VM = pl.BlockSpec(memory_space=pltpu.VMEM)
ANY = pl.BlockSpec(memory_space=pl.ANY)
HBM = pl.BlockSpec(memory_space=pltpu.HBM)


def pack_kernel(values_any, block_any, count_any, out_any, block_ref, count_ref, buf, sems):
    lists, cap = block_ref.shape
    dead_index = 64
    parts = 4
    each = lists // parts
    small = [
        pltpu.make_async_copy(block_any, block_ref, sems.at[2 * parts]),
        pltpu.make_async_copy(count_any, count_ref, sems.at[2 * parts + 1]),
    ]
    spans = [pl.ds(k * each, each) for k in range(parts)]
    loads = [
        pltpu.make_async_copy(values_any.at[at], buf.at[at, pl.ds(0, cap)], sems.at[k])
        for k, at in enumerate(spans)
    ]
    stores = [
        pltpu.make_async_copy(buf.at[at], out_any.at[at], sems.at[parts + k]) for k, at in enumerate(spans)
    ]
    for copy in small + loads:
        copy.start()
    for copy in small:
        copy.wait()
    counts = jnp.sum(
        jnp.where(iota((lists, lists), 0) == iota((lists, lists), 1), count_ref[...], 0),
        axis=1,
        keepdims=True,
    )
    block = block_ref[...]
    high = jnp.where(iota((lists, cap), 1) < counts, block >> 5, dead_index)
    low = block & 31
    high = jnp.concatenate([high, high], axis=1).astype(f32)
    low = jnp.concatenate([low, low], axis=1).astype(f32)
    row = iota((8, LANES), 0)
    for k in range(lists):
        tail = jnp.where(row == 0, high[k : k + 1], jnp.where(row == 1, low[k : k + 1], 0.0))
        buf[k, cap : cap + 8, :] = tail.astype(bf16)
    for load, store in zip(loads, stores):
        load.wait()
        store.start()
    for store in stores:
        store.wait()


def pack(values, block, count):
    lists, cap, width = values.shape
    shape = (lists, cap + 8, width)
    return pl.pallas_call(
        pack_kernel,
        out_shape=jax.ShapeDtypeStruct(shape, bf16),
        in_specs=[ANY, ANY, ANY],
        out_specs=ANY,
        scratch_shapes=[
            pltpu.VMEM((lists, cap), jnp.int32),
            pltpu.VMEM((1, lists), jnp.int32),
            pltpu.VMEM(shape, bf16),
            pltpu.SemaphoreType.DMA((10,)),
        ],
        compiler_params=params(60),
        name="pack",
    )(values, block, count.reshape(1, lists))


def to_column(row):
    return jnp.transpose(jnp.broadcast_to(row, (8, row.shape[1])))[:, 0:1]


def tower_kernel(
    dense_ref, w1_ref, b1_ref, w2_ref, b2_ref, head_ref,
    big_ref, s2_ref, q_ref, deep_ref,
    w1t, w2t,
):
    @pl.when(pl.program_id(0) == 0)
    def _():
        w1t[...] = jnp.transpose(w1_ref[...])
        w2t[...] = jnp.transpose(w2_ref[...])

    din, n1, n2 = dense_ref.shape[1], w1t.shape[0], w2t.shape[0]
    dense_t = jnp.transpose(dense_ref[...])
    big_ref[0:din, :] = dense_t
    pre1 = dot(w1t[...], dense_t) + to_column(b1_ref[...])
    gate1 = jax.nn.sigmoid(pre1)
    h1 = (pre1 * gate1).astype(bf16)
    big_ref[din : din + n1, :] = h1
    slope1 = gate1 * (1.0 + pre1 * (1.0 - gate1))
    pre2 = dot(w2t[...], h1) + to_column(b2_ref[...])
    gate2 = jax.nn.sigmoid(pre2)
    h2 = (pre2 * gate2).astype(bf16)
    big_ref[din + n1 : din + n1 + n2, :] = h2
    head = head_ref[...]
    deep_ref[...] = dot(jnp.broadcast_to(head, (16, head.shape[1])), h2)[0:1]
    s2 = to_column(head.astype(f32)) * (gate2 * (1.0 + pre2 * (1.0 - gate2)))
    s2 = s2.astype(bf16)
    s2_ref[...] = s2
    q_ref[...] = (dot(w2_ref[...], s2) * slope1).astype(bf16)


def tower(dense, w1, b1, w2, b2, head):
    ex, din = dense.shape
    h1, h2 = w2.shape
    steps = 4
    be = ex // steps
    whole = lambda a: pl.BlockSpec(a.shape, lambda i: (0, 0))
    cols = lambda rows: pl.BlockSpec((rows, be), lambda i: (0, i))
    b1, b2, head = b1.reshape(1, h1), b2.reshape(1, h2), head.reshape(1, h2)
    return pl.pallas_call(
        tower_kernel,
        grid=(steps,),
        out_shape=(
            jax.ShapeDtypeStruct((din + h1 + h2, ex), bf16),
            jax.ShapeDtypeStruct((h2, ex), bf16),
            jax.ShapeDtypeStruct((h1, ex), bf16),
            jax.ShapeDtypeStruct((1, ex), f32),
        ),
        in_specs=[
            pl.BlockSpec((be, din), lambda i: (i, 0)),
            whole(w1), whole(b1), whole(w2), whole(b2), whole(head),
        ],
        out_specs=(cols(din + h1 + h2), cols(h2), cols(h1), cols(1)),
        scratch_shapes=[pltpu.VMEM((h1, din), bf16), pltpu.VMEM((h2, h1), bf16)],
        compiler_params=params(62),
        cost_estimate=pl.CostEstimate(
            flops=2 * ex * (din * h1 + 2 * h1 * h2), bytes_accessed=12 << 20, transcendentals=ex * (h1 + h2)
        ),
        name="tower",
    )(dense, w1, b1, w2, b2, head)


def weight_kernel(z_ref, n_ref, out_ref):
    out_ref[...] = jnp.concatenate(split_two(wide_weight(z_ref[...], n_ref[...])), axis=1)


def weights(z, n):
    blocks, width = z.shape
    return pl.pallas_call(
        weight_kernel,
        out_shape=jax.ShapeDtypeStruct((blocks, 2 * width), bf16),
        in_specs=[VM, VM],
        out_specs=VM,
        compiler_params=params(6),
        cost_estimate=pl.CostEstimate(flops=10 * z.size, bytes_accessed=12 * z.size, transcendentals=2 * z.size),
        name="weights",
    )(z, n)


def four_lists(got_ref, at, cap):
    planes = [got_ref[at + k] for k in range(4)]
    values = jnp.concatenate([p[0:cap] for p in planes], axis=0)
    index = [p[cap : cap + 1].astype(f32) * 32.0 + p[cap + 1 : cap + 2].astype(f32) for p in planes]
    left = iota((1, LANES), 1) < cap
    pairs = [jnp.where(left, index[0], index[1]), jnp.where(left, index[2], index[3])]
    return values, jnp.concatenate(pairs, axis=1).astype(jnp.int32)


def logit_kernel(got_ref, wcat_ref, out_ref):
    lists = got_ref.shape[0]
    cap = got_ref.shape[1] - 8
    blocks = wcat_ref.shape[0]
    for at in range(0, lists, 4):
        values, index = four_lists(got_ref, at, cap)
        every = dot(wcat_ref[...], jnp.concatenate([values, values], axis=1), NT)
        picked = jnp.where(iota((blocks, 4 * cap), 0) == index, every, 0.0)
        logit = jnp.sum(picked, axis=0, keepdims=True)
        for k in range(4):
            out_ref[at + k] = logit[:, (k // 2) * LANES : (k // 2 + 1) * LANES]


def slot_logits(got, wcat):
    lists = got.shape[0]
    return pl.pallas_call(
        logit_kernel,
        out_shape=jax.ShapeDtypeStruct((lists, 1, LANES), f32),
        in_specs=[VM, VM],
        out_specs=VM,
        compiler_params=params(16),
        name="slot_logits",
    )(got, wcat)


def doubled(example_ref):
    example = jnp.concatenate([example_ref[...], example_ref[...]], axis=1)
    return example >> 7, example & (LANES - 1)


def mark(low, marks):
    down = iota((LANES, LANES), 0)
    for k in range(low.shape[0]):
        marks[:, k * LANES : (k + 1) * LANES] = jnp.where(low[k : k + 1] == down, 1.0, 0.0).astype(bf16)


def marks_kernel(example_ref, marks_ref):
    mark(doubled(example_ref)[1], marks_ref)


def example_marks(example):
    lists = example.shape[0]
    return pl.pallas_call(
        marks_kernel,
        out_shape=jax.ShapeDtypeStruct((LANES, lists * LANES), bf16),
        in_specs=[VM],
        out_specs=VM,
        compiler_params=params(8),
        cost_estimate=pl.CostEstimate(flops=2 << 20, bytes_accessed=4 << 20, transcendentals=0),
        name="example_marks",
    )(example)


def half_copies(half, big_any, dense_t, h1, sems):
    n1 = 2 * (h1.shape[0] - ONES)
    each, packed = dense_t.shape[0] - ONES, n1 // 4
    span = pl.ds(pl.multiple_of(half * each, each), each)
    copies = [pltpu.make_async_copy(big_any.at[span], dense_t.at[pl.ds(0, each)], sems.at[0])]
    for side in range(2):
        span = pl.ds(pl.multiple_of(2 * each + half * packed + side * 2 * packed, packed), packed)
        copies.append(
            pltpu.make_async_copy(big_any.at[span], h1.at[pl.ds(side * packed, packed)], sems.at[1 + side])
        )
    return copies


def half_gradients(residual, copies, s2, q, dense_t, h1, target):
    rows, first = residual.shape[0], (dense_t.shape[0] - ONES) // EIGHTHS
    packed, width = (h1.shape[0] - ONES) // 2 // EIGHTHS, s2.shape[0]
    each = first + packed
    dense_t[EIGHTHS * first :, :] = jnp.ones((ONES, dense_t.shape[1]), bf16)
    h1[2 * EIGHTHS * packed :, :] = jnp.ones((ONES, h1.shape[1]), bf16)
    dlogit = jnp.concatenate([residual[k : k + 1] for k in range(rows)], axis=1).astype(bf16)
    scale = dlogit.astype(f32)
    d_two = (s2[...].astype(f32) * scale).astype(bf16)
    copies[1].wait()
    copies[2].wait()
    second = dot(h1[...], d_two, NT)
    b_two = second[2 * EIGHTHS * packed : 2 * EIGHTHS * packed + 1]
    second = second.astype(bf16)
    for k in range(EIGHTHS):
        at, low = k * packed, (k + EIGHTHS) * packed
        target[k * each + first : (k + 1) * each, 0:width] = second[at : at + packed]
        target[k * each + first : (k + 1) * each, width:] = second[low : low + packed]
    d_one = (q[...].astype(f32) * scale).astype(bf16)
    copies[0].wait()
    made = dot(dense_t[...], d_one, NT)
    b_one = made[EIGHTHS * first : EIGHTHS * first + 1]
    made = made.astype(bf16)
    for k in range(EIGHTHS):
        target[k * each : k * each + first, :] = made[k * first : (k + 1) * first]
    return dlogit, b_one, b_two


def half_scratch(big, n1):
    half = (big.shape[0] - n1 - n1 // 2) // 2
    return [
        pltpu.VMEM((half + ONES, big.shape[1]), bf16),
        pltpu.VMEM((n1 // 2 + ONES, big.shape[1]), bf16),
        pltpu.SemaphoreType.DMA((4,)),
    ]


def position():
    return lax.axis_index("blk") * lax.axis_size("rep") + lax.axis_index("rep")


def residual_kernel(
    logit_any, example_ref, deep_ref, label_ref, marks, s2, q, big_any,
    prob_ref, residual_ref, send_ref, slot_ref,
    spread, logit_ref, apart, dense_t, h1, sems,
):
    lists, cap = example_ref.shape
    rows = label_ref.shape[0]
    me = position()
    core = me & 1
    first = pltpu.make_async_copy(logit_any, logit_ref, sems.at[3])
    first.start()
    copies = half_copies(1 - core, big_any, dense_t, h1, sems)
    for copy in copies:
        copy.start()
    high = doubled(example_ref)[0]
    mine = (iota((lists, LANES), 1) >= cap) == (core == 1)
    high_mine = jnp.where(mine, high, -1)
    down = iota((rows, LANES), 0)
    first.wait()
    for k in range(lists):
        part = jnp.where(high_mine[k : k + 1] == down, logit_ref[k], 0.0)
        spread[:, k * LANES : (k + 1) * LANES] = jnp.concatenate(split_two(part), axis=0)
    wide = dot(spread[...], marks[...], NT)
    wide = wide[0:rows] + wide[rows:]
    deep = jnp.concatenate([deep_ref[:, k * LANES : (k + 1) * LANES] for k in range(rows)], axis=0)
    prob = jax.nn.sigmoid(wide + deep)
    prob_ref[...] = prob
    residual = prob - label_ref[...].astype(f32)
    residual_ref[...] = residual
    half_gradients(residual, copies, s2, q, dense_t, h1, send_ref)
    found = dot(jnp.concatenate(split_two(residual), axis=0), marks[...])
    found = found[0:rows] + found[rows:]
    for k in range(lists):
        part = jnp.where(high[k : k + 1] == down, found[:, k * LANES : (k + 1) * LANES], 0.0)
        top, rest = split_two(jnp.sum(part, axis=0, keepdims=True))
        apart[me ^ k] = jnp.concatenate([top.astype(f32), rest.astype(f32)], axis=0)
    lines = [
        jnp.concatenate([apart[k + c, s : s + 1, :] for c in range(2) for s in range(2)], axis=1)
        for k in range(0, lists, 2)
    ]
    slot_ref[...] = jnp.concatenate(lines, axis=0).astype(bf16)


def residuals(logits, example, deep, labels, marks, s2, q, big):
    lists = example.shape[0]
    rows = deep.shape[1] // LANES
    n1 = q.shape[0]
    half = (big.shape[0] - n1 - s2.shape[0]) // 2 + n1 // 4
    return pl.pallas_call(
        residual_kernel,
        out_shape=(
            jax.ShapeDtypeStruct((rows, LANES), f32),
            jax.ShapeDtypeStruct((rows, LANES), f32),
            jax.ShapeDtypeStruct((half, n1), bf16),
            jax.ShapeDtypeStruct((lists // 2, 4 * LANES), bf16),
        ),
        in_specs=[ANY] + [VM] * 6 + [HBM],
        out_specs=[VM, VM, VM, VM],
        scratch_shapes=[pltpu.VMEM((2 * rows, lists * LANES), bf16), pltpu.VMEM(logits.shape, f32), pltpu.VMEM((lists, 2, LANES), f32)]
        + half_scratch(big, n1),
        compiler_params=params(49),
        name="residuals",
    )(logits, example, deep, labels.reshape(rows, LANES), marks, s2, q, big)


def gradient_kernel(residual_ref, s2, q, big_any, keep_ref, small_ref, h2, dense_t, h1, sems):
    core = lax.axis_index("rep") & 1
    span = pl.ds(big_any.shape[0] - h2.shape[0], h2.shape[0])
    copies = [pltpu.make_async_copy(big_any.at[span], h2, sems.at[3])]
    copies = half_copies(core, big_any, dense_t, h1, sems) + copies
    for copy in copies:
        copy.start()
    dlogit, b_one, b_two = half_gradients(residual_ref[...], copies, s2, q, dense_t, h1, keep_ref)
    copies[3].wait()
    head = dot(jnp.broadcast_to(dlogit, (ONES, dlogit.shape[1])), h2[...], NT)[0:1]
    small = jnp.concatenate([b_one, jnp.concatenate([b_two, head], axis=1)], axis=0)
    small_ref[...] = jnp.concatenate(split_two(small), axis=0)


def gradients(residual, s2, q, big):
    n1, ex = q.shape
    half = (big.shape[0] - n1 - s2.shape[0]) // 2 + n1 // 4
    return pl.pallas_call(
        gradient_kernel,
        out_shape=(jax.ShapeDtypeStruct((half, n1), bf16), jax.ShapeDtypeStruct((4, n1), bf16)),
        in_specs=[VM] * 3 + [HBM],
        out_specs=[VM, VM],
        scratch_shapes=[pltpu.VMEM(s2.shape, bf16)] + half_scratch(big, n1),
        compiler_params=params(49),
        cost_estimate=pl.CostEstimate(flops=2 * half * n1 * ex, bytes_accessed=6 << 20, transcendentals=0),
        name="gradients",
    )(residual, s2, q, big)


def state_kernel(got_ref, res_ref, z_ref, n_ref, z_out, n_out):
    lists = got_ref.shape[0]
    me = position()
    cap = got_ref.shape[1] - 8
    blocks, width = z_ref.shape
    left = iota((1, LANES), 1) < cap
    grad = jnp.zeros((blocks, 2 * width), f32)
    for at in range(0, lists, 4):
        values, index = four_lists(got_ref, at, cap)
        apart = [me ^ (at + k) for k in range(4)]
        res = [res_ref[pl.ds((a & 1) * (lists // 2) + (a >> 1), 1), :] for a in apart]
        res = jnp.concatenate([jnp.where(left, res[0], res[1]), jnp.where(left, res[2], res[3])], axis=1)
        scaled = jnp.concatenate(split_two(values.astype(f32) * to_column(res)), axis=1)
        hit = jnp.where(iota((blocks, 4 * cap), 0) == index, 1.0, 0.0).astype(bf16)
        grad = grad + dot(hit, scaled)
    grad = grad[:, :width] + grad[:, width:]
    z, n = z_ref[...], n_ref[...]
    n_new = n + grad * grad
    sigma = (jnp.sqrt(n_new) - jnp.sqrt(n)) / alpha_rate
    n_out[...] = n_new
    z_out[...] = z + grad - sigma * wide_weight(z, n)


def new_states(got, res, z, n):
    return pl.pallas_call(
        state_kernel,
        out_shape=(jax.ShapeDtypeStruct(z.shape, f32), jax.ShapeDtypeStruct(z.shape, f32)),
        in_specs=[VM] * 4,
        out_specs=(VM, VM),
        compiler_params=params(16),
        cost_estimate=pl.CostEstimate(
            flops=4 * got.shape[0] * (got.shape[1] - 8) * z.size, bytes_accessed=4 << 20, transcendentals=2 * z.size
        ),
        name="new_states",
    )(got, res, z, n)


def place_kernel(swapped, *refs):
    parts, refs = refs[:4], refs[4:]
    before, refs = (refs[:3], refs[3:]) if swapped else (None, refs)
    w1_any, w2_any, *outs = refs[:-3]
    wide, narrow, sems = refs[-3:]
    me = position()
    half, quad = (me & 1) ^ swapped, (me >> 1) & 3
    first, packed = wide.shape[0] // EIGHTHS, narrow.shape[1] // EIGHTHS
    each, width = first + packed, parts[0].shape[1]
    copies, total = [], before[2][...] if swapped else 0.0
    for k, part in enumerate(parts):
        for t in range(2):
            at, slot = t * each, 2 * k + t
            place = (half * 4 + (quad ^ k)) * 2 + t
            span = pl.ds(slot * first, first)
            wide[span, :] = part[at : at + first, :].astype(f32)
            target = w1_any.at[pl.ds(pl.multiple_of(place * first, first), first)]
            copies.append(pltpu.make_async_copy(wide.at[span], target, sems.at[3 * slot]))
            copies[-1].start()
            for c in range(2):
                span = pl.ds(slot * packed, packed)
                lanes = slice(c * (width // 2), (c + 1) * (width // 2))
                narrow[c, span, :] = part[at + first : at + each, lanes].astype(f32)
                target = w2_any.at[pl.ds(pl.multiple_of((c * 2 * EIGHTHS + place) * packed, packed), packed)]
                copies.append(pltpu.make_async_copy(narrow.at[c, span], target, sems.at[3 * slot + 1 + c]))
                copies[-1].start()
        extra = part[2 * each :, :].astype(f32)
        total = total + sum(extra[r : r + 2] for r in range(0, extra.shape[0], 2))
    if swapped:
        outs[0][...] = total[0:1]
        outs[1][...] = total[1:2, 0 : width // 2]
        outs[2][...] = total[1:2, width // 2 :]
    else:
        outs[0][...] = total
    for copy in copies:
        copy.wait()


def place(swapped, parts, first, packed, before=()):
    width = parts[0].shape[1]
    shapes = [(2 * EIGHTHS * first, width), (4 * EIGHTHS * packed, width // 2)]
    tail = [(1, width), (1, width // 2), (1, width // 2)] if swapped else [(2, width)]
    return pl.pallas_call(
        functools.partial(place_kernel, swapped),
        out_shape=[jax.ShapeDtypeStruct(t, f32) for t in shapes + tail],
        in_specs=[VM] * 4 + [ANY, ANY, VM] * swapped,
        out_specs=[ANY, ANY] + [VM] * len(tail),
        input_output_aliases={4: 0, 5: 1} if swapped else {},
        scratch_shapes=[
            pltpu.VMEM((EIGHTHS * first, width), f32),
            pltpu.VMEM((2, EIGHTHS * packed, width // 2), f32),
            pltpu.SemaphoreType.DMA((3 * EIGHTHS,)),
        ],
        compiler_params=params(16),
        cost_estimate=pl.CostEstimate(flops=first * width, bytes_accessed=80 * first * width, transcendentals=0),
        name="place_other" if swapped else "place_own",
    )(*parts, *before)


def every_to_every(x):
    return lax.all_to_all(x, AXES, split_axis=0, concat_axis=0, tiled=True)


def swap(x, bit, devices):
    return lax.ppermute(x, AXES, [(i, i ^ bit) for i in range(devices)])


def add(*terms):
    return functools.reduce(jnp.add, [t.astype(f32) for t in terms]).astype(bf16)


def halves(x, side):
    rows = x.shape[0] // 2
    return lax.dynamic_slice_in_dim(x, side * rows, rows, 0)


def hold(*values):
    return lax.optimization_barrier(values)


def join(*parts):
    return jnp.concatenate(parts, axis=0)


def whole(p):
    rows = p.shape[0] // 2
    return p[:rows].astype(f32) + p[rows:].astype(f32)


def sum_everywhere(x, slots, extra, me, devices, states):
    bits = [1 << k for k in range(1, devices.bit_length() - 1)]
    quad, inner, last = bits[:2], bits[2:-1], bits[-1]
    at = (me // quad[0]) % 4
    others = [(3, quad[0] + quad[1]), (1, quad[0]), (2, quad[1])]
    wide = x.shape[1]
    slots = slots.reshape(-1, 4, wide)
    rows = x.shape[0] // EIGHTHS
    side = (me // inner[0]) % 2
    quarters = lambda v: [v] + [swap(v, bit, devices) for k, bit in sorted(others)]
    eighth = lambda k, t: lax.dynamic_slice_in_dim(x, ((at ^ k) * 2 + t) * rows, rows, 0)
    away = {k: swap(join(eighth(k, 1 - side), slots[:, k]), bit, devices) for k, bit in others}
    stay = {k: swap(eighth(k, side), bit, devices) for k, bit in others}
    slots = jnp.stack([slots[:, 0]] + [away[k][rows:] for k in (1, 2, 3)], axis=1)
    mine = None
    theirs = add(eighth(0, 1 - side), *[away[k][:rows] for k in (1, 2, 3)])
    for bit in inner + [last]:
        if bit == last:
            mine = theirs = x
        elif bit != inner[0]:
            side_now = (me // bit) % 2
            mine, theirs = halves(x, side_now), halves(x, 1 - side_now)
        slots = slots.reshape(slots.shape[0] // 2, 2, -1, wide)
        ride = slots[:, 1].reshape(-1, wide)
        n, m = theirs.shape[0], ride.shape[0]
        got = swap(join(theirs, ride, *([extra] if bit == last else [])), bit, devices)
        if bit == inner[0]:
            mine = add(eighth(0, side), *[stay[k] for k in (1, 2, 3)])
        x = add(mine, got[:n])
        slots = jnp.stack([slots[:, 0], got[n : n + m].reshape(slots[:, 0].shape)], axis=1)
        slots = slots.reshape(slots.shape[0], -1, wide)
    extra = join(extra, got[n + m :])
    slots = slots.reshape(-1, 2, wide // 2)
    far = swap(slots[:, 1], 1, devices)
    made = states(whole(jnp.stack([*jnp.split(join(slots[:, 0], far), 2, axis=1)]).reshape(-1, wide // 4)))
    for bit in reversed(inner):
        side_now = (me // bit) % 2
        got = swap(join(x, extra), bit, devices)
        n = x.shape[0]
        other = got[:n]
        x = join(jnp.where(side_now == 0, x, other), jnp.where(side_now == 0, other, x))
        extra = join(extra, got[n:])
    parts = quarters(join(x, extra))
    parts[0], *made = hold(parts[0], *made)
    return parts, made


def per_device(
    devices,
    dense,
    labels,
    tile_values,
    tile_block,
    tile_example,
    tile_count,
    z_state,
    n_state,
    w_one,
    b_one,
    w_two,
    b_two,
    head,
):
    n1, n2 = w_two.shape
    din = dense.shape[1]
    me = lax.axis_index(AXES)
    got = every_to_every(pack(tile_values, tile_block, tile_count))
    big, s2, q, deep = tower(dense, w_one, b_one, w_two, b_two, head)
    deep, z_then, n_then = hold(deep, z_state, n_state)
    wcat = weights(z_then, n_then)
    got, deep = hold(got, deep)
    logits = slot_logits(got, wcat)
    logits, example = hold(logits, tile_example)
    marks = example_marks(example)
    logits = every_to_every(logits)
    prob, residual, send, slots = residuals(logits, tile_example, deep, labels, marks, s2, q, big)
    keep, small = gradients(residual, s2, q, big)
    own = add(keep, swap(send, 1, devices))

    def states(res):
        return new_states(got, res, z_state, n_state)

    parts, (z_new, n_new) = sum_everywhere(own, slots, small, me, devices, states)
    first, packed = din // 2 // EIGHTHS, n1 // 4 // EIGHTHS
    others = [swap(part, 1, devices) for part in parts]
    placed = place(0, parts, first, packed)
    grad_w_one, grad_w_two, grad_b_one, grad_b_two, grad_head = place(1, others, first, packed, placed)
    return (
        prob.reshape(-1),
        z_new,
        n_new,
        grad_w_one,
        grad_b_one.reshape(-1),
        grad_w_two,
        grad_b_two.reshape(-1),
        grad_head.reshape(-1),
    )


def solution(mesh):
    placed = (
        P(AXES, None),
        P(AXES),
        P(AXES, None, None),
        P(AXES, None),
        P(AXES, None),
        P(AXES),
        P(AXES, None),
        P(AXES, None),
        P(),
        P(),
        P(),
        P(),
        P(),
    )
    devices = mesh.shape["blk"] * mesh.shape["rep"]
    return jax.shard_map(
        functools.partial(per_device, devices),
        mesh=mesh,
        in_specs=placed,
        out_specs=(P(AXES), P(AXES, None), P(AXES, None), P(), P(), P(), P(), P()),
        check_vma=False,
    )
```

```python
import functools
import jax
import jax.numpy as jnp
from jax import lax
from jax.experimental import pallas as pl
from jax.experimental.pallas import tpu as pltpu
from jax.sharding import PartitionSpec as P

alpha_rate = 0.5
beta_shift = 1.0
lasso_term = 0.5
ridge_term = 0.1

AXES = ("blk", "rep")
LANES = 128
EIGHTHS = 8
ONES = 16
PIECES = 2
f32 = jnp.float32
bf16 = jnp.bfloat16
NT = (((1,), (1,)), ((), ()))
NN = (((1,), (0,)), ((), ()))


def dot(a, b, dims=NN):
    return lax.dot_general(a, b, dims, preferred_element_type=f32)


def iota(shape, axis):
    return lax.broadcasted_iota(jnp.int32, shape, axis)


def split_two(x):
    top = x.astype(bf16)
    return top, (x - top.astype(f32)).astype(bf16)


def wide_weight(z, n):
    sign = jnp.where(z > 0, 1.0, jnp.where(z < 0, -1.0, 0.0))
    shrunk = z - sign * lasso_term
    denominator = (beta_shift + jnp.sqrt(n)) / alpha_rate + ridge_term
    return jnp.where(jnp.abs(z) > lasso_term, -shrunk / denominator, jnp.zeros_like(z))


def params(megabytes=40):
    return pltpu.CompilerParams(vmem_limit_bytes=megabytes << 20)


VM = pl.BlockSpec(memory_space=pltpu.VMEM)
ANY = pl.BlockSpec(memory_space=pl.ANY)
HBM = pl.BlockSpec(memory_space=pltpu.HBM)


def pack_kernel(values_any, block_any, count_any, out_any, block_ref, count_ref, buf, sems):
    lists, cap = block_ref.shape
    dead_index = 64
    parts = 4
    each = lists // parts
    small = [
        pltpu.make_async_copy(block_any, block_ref, sems.at[2 * parts]),
        pltpu.make_async_copy(count_any, count_ref, sems.at[2 * parts + 1]),
    ]
    spans = [pl.ds(k * each, each) for k in range(parts)]
    loads = [
        pltpu.make_async_copy(values_any.at[at], buf.at[at, pl.ds(0, cap)], sems.at[k])
        for k, at in enumerate(spans)
    ]
    stores = [
        pltpu.make_async_copy(buf.at[at], out_any.at[at], sems.at[parts + k]) for k, at in enumerate(spans)
    ]
    for copy in small + loads:
        copy.start()
    for copy in small:
        copy.wait()
    counts = jnp.sum(
        jnp.where(iota((lists, lists), 0) == iota((lists, lists), 1), count_ref[...], 0),
        axis=1,
        keepdims=True,
    )
    block = block_ref[...]
    high = jnp.where(iota((lists, cap), 1) < counts, block >> 5, dead_index)
    low = block & 31
    high = jnp.concatenate([high, high], axis=1).astype(f32)
    low = jnp.concatenate([low, low], axis=1).astype(f32)
    row = iota((8, LANES), 0)
    for k in range(lists):
        tail = jnp.where(row == 0, high[k : k + 1], jnp.where(row == 1, low[k : k + 1], 0.0))
        buf[k, cap : cap + 8, :] = tail.astype(bf16)
    for load, store in zip(loads, stores):
        load.wait()
        store.start()
    for store in stores:
        store.wait()


def pack(values, block, count):
    lists, cap, width = values.shape
    shape = (lists, cap + 8, width)
    return pl.pallas_call(
        pack_kernel,
        out_shape=jax.ShapeDtypeStruct(shape, bf16),
        in_specs=[ANY, ANY, ANY],
        out_specs=ANY,
        scratch_shapes=[
            pltpu.VMEM((lists, cap), jnp.int32),
            pltpu.VMEM((1, lists), jnp.int32),
            pltpu.VMEM(shape, bf16),
            pltpu.SemaphoreType.DMA((10,)),
        ],
        compiler_params=params(60),
        name="pack",
    )(values, block, count.reshape(1, lists))


def to_column(row):
    return jnp.transpose(jnp.broadcast_to(row, (8, row.shape[1])))[:, 0:1]


def tower_kernel(
    dense_ref, w1_ref, b1_ref, w2_ref, b2_ref, head_ref,
    big_ref, h2_ref, s2_ref, q_ref, deep_ref,
    w1t, w2t,
):
    @pl.when(pl.program_id(0) == 0)
    def _():
        w1t[...] = jnp.transpose(w1_ref[...])
        w2t[...] = jnp.transpose(w2_ref[...])

    din, n1, n2 = dense_ref.shape[1], w1t.shape[0], w2t.shape[0]
    dense_t = jnp.transpose(dense_ref[...])
    big_ref[0:din, :] = dense_t
    pre1 = dot(w1t[...], dense_t) + to_column(b1_ref[...])
    gate1 = jax.nn.sigmoid(pre1)
    h1 = (pre1 * gate1).astype(bf16)
    big_ref[din : din + n1, :] = h1
    big_ref[din + n1 :, :] = jnp.zeros((n2, big_ref.shape[1]), bf16)
    slope1 = gate1 * (1.0 + pre1 * (1.0 - gate1))
    pre2 = dot(w2t[...], h1) + to_column(b2_ref[...])
    gate2 = jax.nn.sigmoid(pre2)
    h2 = (pre2 * gate2).astype(bf16)
    h2_ref[...] = h2
    head = head_ref[...]
    deep_ref[...] = dot(jnp.broadcast_to(head, (16, head.shape[1])), h2)[0:1]
    s2 = to_column(head.astype(f32)) * (gate2 * (1.0 + pre2 * (1.0 - gate2)))
    s2 = s2.astype(bf16)
    s2_ref[...] = s2
    q_ref[...] = (dot(w2_ref[...], s2) * slope1).astype(bf16)


def tower(dense, w1, b1, w2, b2, head):
    ex, din = dense.shape
    h1, h2 = w2.shape
    steps = 4
    be = ex // steps
    whole = lambda a: pl.BlockSpec(a.shape, lambda i: (0, 0))
    cols = lambda rows: pl.BlockSpec((rows, be), lambda i: (0, i))
    b1, b2, head = b1.reshape(1, h1), b2.reshape(1, h2), head.reshape(1, h2)
    return pl.pallas_call(
        tower_kernel,
        grid=(steps,),
        out_shape=(
            jax.ShapeDtypeStruct((din + h1 + h2, ex), bf16),
            jax.ShapeDtypeStruct((h2, ex), bf16),
            jax.ShapeDtypeStruct((h2, ex), bf16),
            jax.ShapeDtypeStruct((h1, ex), bf16),
            jax.ShapeDtypeStruct((1, ex), f32),
        ),
        in_specs=[
            pl.BlockSpec((be, din), lambda i: (i, 0)),
            whole(w1), whole(b1), whole(w2), whole(b2), whole(head),
        ],
        out_specs=(cols(din + h1 + h2), cols(h2), cols(h2), cols(h1), cols(1)),
        scratch_shapes=[pltpu.VMEM((h1, din), bf16), pltpu.VMEM((h2, h1), bf16)],
        compiler_params=params(62),
        cost_estimate=pl.CostEstimate(
            flops=2 * ex * (din * h1 + 2 * h1 * h2), bytes_accessed=12 << 20, transcendentals=ex * (h1 + h2)
        ),
        name="tower",
    )(dense, w1, b1, w2, b2, head)


def weight_kernel(z_ref, n_ref, out_ref):
    out_ref[...] = jnp.concatenate(split_two(wide_weight(z_ref[...], n_ref[...])), axis=1)


def weights(z, n):
    blocks, width = z.shape
    return pl.pallas_call(
        weight_kernel,
        out_shape=jax.ShapeDtypeStruct((blocks, 2 * width), bf16),
        in_specs=[VM, VM],
        out_specs=VM,
        compiler_params=params(6),
        cost_estimate=pl.CostEstimate(flops=10 * z.size, bytes_accessed=12 * z.size, transcendentals=2 * z.size),
        name="weights",
    )(z, n)


def four_lists(got_ref, at, cap):
    planes = [got_ref[at + k] for k in range(4)]
    values = jnp.concatenate([p[0:cap] for p in planes], axis=0)
    index = [p[cap : cap + 1].astype(f32) * 32.0 + p[cap + 1 : cap + 2].astype(f32) for p in planes]
    left = iota((1, LANES), 1) < cap
    pairs = [jnp.where(left, index[0], index[1]), jnp.where(left, index[2], index[3])]
    return values, jnp.concatenate(pairs, axis=1).astype(jnp.int32)


def logit_kernel(got_ref, wcat_ref, out_ref):
    lists = got_ref.shape[0]
    cap = got_ref.shape[1] - 8
    blocks = wcat_ref.shape[0]
    for at in range(0, lists, 4):
        values, index = four_lists(got_ref, at, cap)
        every = dot(wcat_ref[...], jnp.concatenate([values, values], axis=1), NT)
        picked = jnp.where(iota((blocks, 4 * cap), 0) == index, every, 0.0)
        logit = jnp.sum(picked, axis=0, keepdims=True)
        for k in range(4):
            out_ref[at + k] = logit[:, (k // 2) * LANES : (k // 2 + 1) * LANES]


def slot_logits(got, wcat):
    lists = got.shape[0]
    return pl.pallas_call(
        logit_kernel,
        out_shape=jax.ShapeDtypeStruct((lists, 1, LANES), f32),
        in_specs=[VM, VM],
        out_specs=VM,
        compiler_params=params(16),
        name="slot_logits",
    )(got, wcat)


def paired(example_ref):
    lists = example_ref.shape[0]
    example = [
        jnp.concatenate([example_ref[k : k + 1], example_ref[k + 1 : k + 2]], axis=1) for k in range(0, lists, 2)
    ]
    return [e >> 7 for e in example], [e & (LANES - 1) for e in example]


def marks_kernel(example_ref, marks_ref):
    down = iota((LANES, LANES), 0)
    for k, low in enumerate(paired(example_ref)[1]):
        marks_ref[:, k * LANES : (k + 1) * LANES] = jnp.where(low == down, 1.0, 0.0).astype(bf16)


def example_marks(example):
    lists, cap = example.shape
    return pl.pallas_call(
        marks_kernel,
        out_shape=jax.ShapeDtypeStruct((LANES, lists * cap), bf16),
        in_specs=[VM],
        out_specs=VM,
        compiler_params=params(8),
        cost_estimate=pl.CostEstimate(flops=2 << 20, bytes_accessed=4 << 20, transcendentals=0),
        name="example_marks",
    )(example)


def half_copies(half, big_any, dense_t, h1, sems):
    n1 = 2 * (h1.shape[0] - ONES)
    each, packed = dense_t.shape[0] - ONES, n1 // 4
    copies = []
    for side in range(2):
        span = pl.ds(pl.multiple_of(2 * each + half * packed + side * 2 * packed, packed), packed)
        copies.append(pltpu.make_async_copy(big_any.at[span], h1.at[pl.ds(side * packed, packed)], sems.at[side]))
    rows = each // PIECES
    for k in range(PIECES):
        span = pl.ds(pl.multiple_of(half * each + k * rows, rows), rows)
        copies.append(pltpu.make_async_copy(big_any.at[span], dense_t.at[pl.ds(k * rows, rows)], sems.at[2 + k]))
    return copies


def half_gradients(residual, copies, s2, q, dense_t, h1, target):
    rows, first = residual.shape[0], (dense_t.shape[0] - ONES) // EIGHTHS
    packed, width = (h1.shape[0] - ONES) // 2 // EIGHTHS, s2.shape[0]
    each = first + packed
    dense_t[EIGHTHS * first :, :] = jnp.ones((ONES, dense_t.shape[1]), bf16)
    h1[2 * EIGHTHS * packed :, :] = jnp.ones((ONES, h1.shape[1]), bf16)
    dlogit = jnp.concatenate([residual[k : k + 1] for k in range(rows)], axis=1).astype(bf16)
    scale = dlogit.astype(f32)
    d_two = (s2[...].astype(f32) * scale).astype(bf16)
    d_one = (q[...].astype(f32) * scale).astype(bf16)
    copies[0].wait()
    copies[1].wait()
    second = dot(h1[...], d_two, NT)
    b_two = second[2 * EIGHTHS * packed : 2 * EIGHTHS * packed + 1]
    second = second.astype(bf16)
    for k in range(EIGHTHS):
        at, low = k * packed, (k + EIGHTHS) * packed
        target[k * each + first : (k + 1) * each, 0:width] = second[at : at + packed]
        target[k * each + first : (k + 1) * each, width:] = second[low : low + packed]
    for copy in copies[2:]:
        copy.wait()
    made = dot(dense_t[...], d_one, NT)
    b_one = made[EIGHTHS * first : EIGHTHS * first + 1]
    made = made.astype(bf16)
    for k in range(EIGHTHS):
        target[k * each : k * each + first, :] = made[k * first : (k + 1) * first]
    return dlogit, b_one, b_two


def half_scratch(big, n1):
    half = (big.shape[0] - n1 - n1 // 2) // 2
    return [
        pltpu.VMEM((half + ONES, big.shape[1]), bf16),
        pltpu.VMEM((n1 // 2 + ONES, big.shape[1]), bf16),
        pltpu.SemaphoreType.DMA((4 + PIECES,)),
    ]


def position():
    return lax.axis_index("blk") * lax.axis_size("rep") + lax.axis_index("rep")


def residual_kernel(
    logit_any, example_ref, deep_ref, label_ref, marks, s2, q, big_any,
    prob_ref, residual_ref, send_ref, slot_ref,
    spread, logit_ref, apart, dense_t, h1, sems,
):
    lists, cap = example_ref.shape
    rows = label_ref.shape[0]
    me = position()
    core = me & 1
    first = pltpu.make_async_copy(logit_any, logit_ref, sems.at[2 + PIECES])
    first.start()
    copies = half_copies(1 - core, big_any, dense_t, h1, sems)
    for copy in copies:
        copy.start()
    high = paired(example_ref)[0]
    left = iota((1, LANES), 1) < cap
    down = iota((rows, LANES), 0)
    turned = lambda v: pltpu.roll(v, cap, 1)
    first.wait()
    for k in range(lists // 2):
        even, odd = logit_ref[2 * k], logit_ref[2 * k + 1]
        pair = jnp.where(core == 0, jnp.where(left, even, turned(odd)), jnp.where(left, turned(even), odd))
        part = jnp.where(high[k] == down, pair, 0.0)
        spread[:, k * LANES : (k + 1) * LANES] = jnp.concatenate(split_two(part), axis=0)
    wide = dot(spread[...], marks[...], NT)
    wide = wide[0:rows] + wide[rows:]
    deep = jnp.concatenate([deep_ref[:, k * LANES : (k + 1) * LANES] for k in range(rows)], axis=0)
    prob = jax.nn.sigmoid(wide + deep)
    prob_ref[...] = prob
    residual = prob - label_ref[...].astype(f32)
    residual_ref[...] = residual
    found = dot(jnp.concatenate(split_two(residual), axis=0), marks[...])
    found = found[0:rows] + found[rows:]
    for k in range(lists // 2):
        part = jnp.where(high[k] == down, found[:, k * LANES : (k + 1) * LANES], 0.0)
        both = jnp.sum(part, axis=0, keepdims=True)
        swapped = turned(both)
        for c, one in enumerate((jnp.where(left, both, swapped), jnp.where(left, swapped, both))):
            top, rest = split_two(one)
            apart[me ^ (2 * k + c)] = jnp.concatenate([top.astype(f32), rest.astype(f32)], axis=0)
    lines = [
        jnp.concatenate([apart[k + c, s : s + 1, :] for c in range(2) for s in range(2)], axis=1)
        for k in range(0, lists, 2)
    ]
    slot_ref[...] = jnp.concatenate(lines, axis=0).astype(bf16)
    half_gradients(residual, copies, s2, q, dense_t, h1, send_ref)


def residuals(logits, example, deep, labels, marks, s2, q, big):
    lists = example.shape[0]
    rows = deep.shape[1] // LANES
    n1 = q.shape[0]
    half = (big.shape[0] - n1 - s2.shape[0]) // 2 + n1 // 4
    return pl.pallas_call(
        residual_kernel,
        out_shape=(
            jax.ShapeDtypeStruct((rows, LANES), f32),
            jax.ShapeDtypeStruct((rows, LANES), f32),
            jax.ShapeDtypeStruct((half, n1), bf16),
            jax.ShapeDtypeStruct((lists // 2, 4 * LANES), bf16),
        ),
        in_specs=[ANY] + [VM] * 6 + [HBM],
        out_specs=[VM, VM, VM, VM],
        scratch_shapes=[pltpu.VMEM((2 * rows, marks.shape[1]), bf16), pltpu.VMEM(logits.shape, f32), pltpu.VMEM((lists, 2, LANES), f32)]
        + half_scratch(big, n1),
        compiler_params=params(49),
        name="residuals",
    )(logits, example, deep, labels.reshape(rows, LANES), marks, s2, q, big)


def gradient_kernel(residual_ref, s2, q, big_any, keep_ref, small_ref, dense_t, h1, sems):
    core = lax.axis_index("rep") & 1
    copies = half_copies(core, big_any, dense_t, h1, sems)
    for copy in copies:
        copy.start()
    _, b_one, b_two = half_gradients(residual_ref[...], copies, s2, q, dense_t, h1, keep_ref)
    small = jnp.concatenate([b_one, jnp.concatenate([b_two, jnp.zeros_like(b_two)], axis=1)], axis=0)
    small_ref[...] = jnp.concatenate(split_two(small), axis=0)


def gradients(residual, s2, q, big):
    n1, ex = q.shape
    half = (big.shape[0] - n1 - s2.shape[0]) // 2 + n1 // 4
    return pl.pallas_call(
        gradient_kernel,
        out_shape=(jax.ShapeDtypeStruct((half, n1), bf16), jax.ShapeDtypeStruct((4, n1), bf16)),
        in_specs=[VM] * 3 + [HBM],
        out_specs=[VM, VM],
        scratch_shapes=half_scratch(big, n1),
        compiler_params=params(49),
        cost_estimate=pl.CostEstimate(flops=2 * half * n1 * ex, bytes_accessed=6 << 20, transcendentals=0),
        name="gradients",
    )(residual, s2, q, big)


def head_kernel(residual_ref, small, h2, out_ref):
    residual = residual_ref[...]
    dlogit = jnp.concatenate([residual[k : k + 1] for k in range(residual.shape[0])], axis=1).astype(bf16)
    head = dot(jnp.broadcast_to(dlogit, (ONES, dlogit.shape[1])), h2[...], NT)[0:1]
    top, rest = split_two(jnp.concatenate([jnp.zeros_like(head), head], axis=1))
    zero = jnp.zeros_like(top)
    out_ref[...] = small[...] + jnp.concatenate([zero, top, zero, rest], axis=0)


def head_gradient(residual, small, h2):
    return pl.pallas_call(
        head_kernel,
        out_shape=jax.ShapeDtypeStruct(small.shape, bf16),
        in_specs=[VM] * 3,
        out_specs=VM,
        compiler_params=params(8),
        cost_estimate=pl.CostEstimate(flops=32 * h2.size, bytes_accessed=2 << 20, transcendentals=0),
        name="head_gradient",
    )(residual, small, h2)


def state_kernel(got_ref, res_ref, z_ref, n_ref, z_out, n_out):
    lists = got_ref.shape[0]
    me = position()
    cap = got_ref.shape[1] - 8
    blocks, width = z_ref.shape
    left = iota((1, LANES), 1) < cap
    grad = jnp.zeros((blocks, 2 * width), f32)
    for at in range(0, lists, 4):
        values, index = four_lists(got_ref, at, cap)
        apart = [me ^ (at + k) for k in range(4)]
        res = [res_ref[pl.ds((a & 1) * (lists // 2) + (a >> 1), 1), :] for a in apart]
        res = jnp.concatenate([jnp.where(left, res[0], res[1]), jnp.where(left, res[2], res[3])], axis=1)
        scaled = jnp.concatenate(split_two(values.astype(f32) * to_column(res)), axis=1)
        hit = jnp.where(iota((blocks, 4 * cap), 0) == index, 1.0, 0.0).astype(bf16)
        grad = grad + dot(hit, scaled)
    grad = grad[:, :width] + grad[:, width:]
    z, n = z_ref[...], n_ref[...]
    n_new = n + grad * grad
    sigma = (jnp.sqrt(n_new) - jnp.sqrt(n)) / alpha_rate
    n_out[...] = n_new
    z_out[...] = z + grad - sigma * wide_weight(z, n)


def new_states(got, res, z, n):
    return pl.pallas_call(
        state_kernel,
        out_shape=(jax.ShapeDtypeStruct(z.shape, f32), jax.ShapeDtypeStruct(z.shape, f32)),
        in_specs=[VM] * 4,
        out_specs=(VM, VM),
        compiler_params=params(16),
        cost_estimate=pl.CostEstimate(
            flops=4 * got.shape[0] * (got.shape[1] - 8) * z.size, bytes_accessed=4 << 20, transcendentals=2 * z.size
        ),
        name="new_states",
    )(got, res, z, n)


def place_kernel(items, follows, *refs):
    parts, refs = refs[: len(items)], refs[len(items) :]
    before, refs = (refs[:3], refs[3:]) if follows else (None, refs)
    w1_any, w2_any, *outs = refs[:-3]
    wide, narrow, sems = refs[-3:]
    me = position()
    quad = (me >> 1) & 3
    first, packed = wide.shape[1] // 2, narrow.shape[2] // 2
    each, width = first + packed, parts[0].shape[1]
    copies, total = [], before[2][...] if follows else 0.0
    for k, ((apart, swapped), part) in enumerate(zip(items, parts)):
        quarter = ((me & 1) ^ swapped) * 4 + (quad ^ apart)
        for t in range(2):
            at = t * each
            wide[k, t * first : (t + 1) * first, :] = part[at : at + first, :].astype(f32)
            for c in range(2):
                lanes = slice(c * (width // 2), (c + 1) * (width // 2))
                narrow[k, c, t * packed : (t + 1) * packed, :] = part[at + first : at + each, lanes].astype(f32)
        start = pl.multiple_of(quarter * 2 * first, 2 * first)
        copies.append(pltpu.make_async_copy(wide.at[k], w1_any.at[pl.ds(start, 2 * first)], sems.at[3 * k]))
        for c in range(2):
            start = pl.multiple_of((c * EIGHTHS + quarter) * 2 * packed, 2 * packed)
            target = w2_any.at[pl.ds(start, 2 * packed)]
            copies.append(pltpu.make_async_copy(narrow.at[k, c], target, sems.at[3 * k + 1 + c]))
        for copy in copies[-3:]:
            copy.start()
        extra = part[2 * each :, :].astype(f32)
        total = total + sum(extra[r : r + 2] for r in range(0, extra.shape[0], 2))
    if len(outs) > 1:
        outs[0][...] = total[0:1]
        outs[1][...] = total[1:2, 0 : width // 2]
        outs[2][...] = total[1:2, width // 2 :]
    else:
        outs[0][...] = total
    for copy in copies:
        copy.wait()


def place(items, parts, first, packed, before=(), final=False):
    width, count = parts[0].shape[1], len(items)
    shapes = [(2 * EIGHTHS * first, width), (4 * EIGHTHS * packed, width // 2)]
    tail = [(1, width), (1, width // 2), (1, width // 2)] if final else [(2, width)]
    return pl.pallas_call(
        functools.partial(place_kernel, items, bool(before)),
        out_shape=[jax.ShapeDtypeStruct(t, f32) for t in shapes + tail],
        in_specs=[VM] * count + ([ANY, ANY, VM] if before else []),
        out_specs=[ANY, ANY] + [VM] * len(tail),
        input_output_aliases={count: 0, count + 1: 1} if before else {},
        scratch_shapes=[
            pltpu.VMEM((count, 2 * first, width), f32),
            pltpu.VMEM((count, 2, 2 * packed, width // 2), f32),
            pltpu.SemaphoreType.DMA((3 * count,)),
        ],
        compiler_params=params(16),
        cost_estimate=pl.CostEstimate(
            flops=count * first * width, bytes_accessed=16 * count * first * width, transcendentals=0
        ),
        name="place",
    )(*parts, *before)


def every_to_every(x):
    return lax.all_to_all(x, AXES, split_axis=0, concat_axis=0, tiled=True)


def swap(x, bit, devices):
    return lax.ppermute(x, AXES, [(i, i ^ bit) for i in range(devices)])


def add(*terms):
    return functools.reduce(jnp.add, [t.astype(f32) for t in terms]).astype(bf16)


def halves(x, side):
    rows = x.shape[0] // 2
    return lax.dynamic_slice_in_dim(x, side * rows, rows, 0)


def hold(*values):
    return lax.optimization_barrier(values)


def join(*parts):
    return jnp.concatenate(parts, axis=0)


def whole(p):
    rows = p.shape[0] // 2
    return p[:rows].astype(f32) + p[rows:].astype(f32)


def sum_everywhere(x, slots, extra, me, devices, states):
    bits = [1 << k for k in range(1, devices.bit_length() - 1)]
    quad, inner, last = bits[:2], bits[2:-1], bits[-1]
    at = (me // quad[0]) % 4
    others = [(3, quad[0] + quad[1]), (1, quad[0]), (2, quad[1])]
    wide = x.shape[1]
    slots = slots.reshape(-1, 4, wide)
    rows = x.shape[0] // EIGHTHS
    side = (me // inner[0]) % 2
    quarters = lambda v: [v] + [swap(v, bit, devices) for k, bit in sorted(others)]
    eighth = lambda k, t: lax.dynamic_slice_in_dim(x, ((at ^ k) * 2 + t) * rows, rows, 0)
    away = {k: swap(join(eighth(k, 1 - side), slots[:, k]), bit, devices) for k, bit in others}
    stay = {k: swap(eighth(k, side), bit, devices) for k, bit in others}
    slots = jnp.stack([slots[:, 0]] + [away[k][rows:] for k in (1, 2, 3)], axis=1)
    mine = None
    theirs = add(eighth(0, 1 - side), *[away[k][:rows] for k in (1, 2, 3)])
    for bit in inner + [last]:
        if bit == last:
            mine = theirs = x
        elif bit != inner[0]:
            side_now = (me // bit) % 2
            mine, theirs = halves(x, side_now), halves(x, 1 - side_now)
        slots = slots.reshape(slots.shape[0] // 2, 2, -1, wide)
        ride = slots[:, 1].reshape(-1, wide)
        n, m = theirs.shape[0], ride.shape[0]
        got = swap(join(theirs, ride, *([extra] if bit == last else [])), bit, devices)
        if bit == inner[0]:
            mine = add(eighth(0, side), *[stay[k] for k in (1, 2, 3)])
        x = add(mine, got[:n])
        slots = jnp.stack([slots[:, 0], got[n : n + m].reshape(slots[:, 0].shape)], axis=1)
        slots = slots.reshape(slots.shape[0], -1, wide)
    extra = join(extra, got[n + m :])
    slots = slots.reshape(-1, 2, wide // 2)
    far = swap(slots[:, 1], 1, devices)
    made = states(whole(jnp.stack([*jnp.split(join(slots[:, 0], far), 2, axis=1)]).reshape(-1, wide // 4)))
    for bit in reversed(inner):
        side_now = (me // bit) % 2
        got = swap(join(x, extra), bit, devices)
        n = x.shape[0]
        other = got[:n]
        x = join(jnp.where(side_now == 0, x, other), jnp.where(side_now == 0, other, x))
        extra = join(extra, got[n:])
    parts = quarters(join(x, extra))
    parts[0], *made = hold(parts[0], *made)
    return parts, made


def per_device(
    devices,
    dense,
    labels,
    tile_values,
    tile_block,
    tile_example,
    tile_count,
    z_state,
    n_state,
    w_one,
    b_one,
    w_two,
    b_two,
    head,
):
    n1, n2 = w_two.shape
    din = dense.shape[1]
    me = lax.axis_index(AXES)
    got = every_to_every(pack(tile_values, tile_block, tile_count))
    big, h2, s2, q, deep = tower(dense, w_one, b_one, w_two, b_two, head)
    deep, z_then, n_then = hold(deep, z_state, n_state)
    wcat = weights(z_then, n_then)
    got, deep = hold(got, deep)
    logits = slot_logits(got, wcat)
    logits, example = hold(logits, tile_example)
    marks = example_marks(example)
    logits = every_to_every(logits)
    prob, residual, send, slots = residuals(logits, tile_example, deep, labels, marks, s2, q, big)
    keep, small = gradients(residual, s2, q, big)
    own = add(keep, swap(send, 1, devices))

    own, small, seen = hold(own, small, residual)
    small = head_gradient(seen, small, h2)

    def states(res):
        return new_states(got, res, z_state, n_state)

    parts, (z_new, n_new) = sum_everywhere(own, slots, small, me, devices, states)
    first, packed = din // 2 // EIGHTHS, n1 // 4 // EIGHTHS
    others = [swap(part, 1, devices) for part in parts]
    placed = place([(k, 0) for k in range(4)], parts, first, packed)
    grad_w_one, grad_w_two, grad_b_one, grad_b_two, grad_head = place(
        [(k, 1) for k in range(4)], others, first, packed, placed, True
    )
    return (
        prob.reshape(-1),
        z_new,
        n_new,
        grad_w_one,
        grad_b_one.reshape(-1),
        grad_w_two,
        grad_b_two.reshape(-1),
        grad_head.reshape(-1),
    )


def solution(mesh):
    placed = (
        P(AXES, None),
        P(AXES),
        P(AXES, None, None),
        P(AXES, None),
        P(AXES, None),
        P(AXES),
        P(AXES, None),
        P(AXES, None),
        P(),
        P(),
        P(),
        P(),
        P(),
    )
    devices = mesh.shape["blk"] * mesh.shape["rep"]
    return jax.shard_map(
        functools.partial(per_device, devices),
        mesh=mesh,
        in_specs=placed,
        out_specs=(P(AXES), P(AXES, None), P(AXES, None), P(), P(), P(), P(), P()),
        check_vma=False,
    )
```

```python
import functools
import jax
import jax.numpy as jnp
from jax import lax
from jax.experimental import pallas as pl
from jax.experimental.pallas import tpu as pltpu
from jax.sharding import PartitionSpec as P

alpha_rate = 0.5
beta_shift = 1.0
lasso_term = 0.5
ridge_term = 0.1

AXES = ("blk", "rep")
LANES = 128
EIGHTHS = 8
ONES = 16
PIECES = 2
f32 = jnp.float32
bf16 = jnp.bfloat16
NT = (((1,), (1,)), ((), ()))
NN = (((1,), (0,)), ((), ()))


def dot(a, b, dims=NN):
    return lax.dot_general(a, b, dims, preferred_element_type=f32)


def iota(shape, axis):
    return lax.broadcasted_iota(jnp.int32, shape, axis)


def split_two(x):
    top = x.astype(bf16)
    return top, (x - top.astype(f32)).astype(bf16)


def wide_weight(z, n):
    sign = jnp.where(z > 0, 1.0, jnp.where(z < 0, -1.0, 0.0))
    shrunk = z - sign * lasso_term
    denominator = (beta_shift + jnp.sqrt(n)) / alpha_rate + ridge_term
    return jnp.where(jnp.abs(z) > lasso_term, -shrunk / denominator, jnp.zeros_like(z))


def params(megabytes=40):
    return pltpu.CompilerParams(vmem_limit_bytes=megabytes << 20)


VM = pl.BlockSpec(memory_space=pltpu.VMEM)
ANY = pl.BlockSpec(memory_space=pl.ANY)
HBM = pl.BlockSpec(memory_space=pltpu.HBM)


def pack_kernel(values_any, block_any, count_any, out_any, block_ref, count_ref, buf, sems):
    lists, cap = block_ref.shape
    dead_index = 64
    parts = 4
    each = lists // parts
    small = [
        pltpu.make_async_copy(block_any, block_ref, sems.at[2 * parts]),
        pltpu.make_async_copy(count_any, count_ref, sems.at[2 * parts + 1]),
    ]
    spans = [pl.ds(k * each, each) for k in range(parts)]
    loads = [
        pltpu.make_async_copy(values_any.at[at], buf.at[at, pl.ds(0, cap)], sems.at[k])
        for k, at in enumerate(spans)
    ]
    stores = [
        pltpu.make_async_copy(buf.at[at], out_any.at[at], sems.at[parts + k]) for k, at in enumerate(spans)
    ]
    for copy in small + loads:
        copy.start()
    for copy in small:
        copy.wait()
    counts = jnp.sum(
        jnp.where(iota((lists, lists), 0) == iota((lists, lists), 1), count_ref[...], 0),
        axis=1,
        keepdims=True,
    )
    block = block_ref[...]
    high = jnp.where(iota((lists, cap), 1) < counts, block >> 5, dead_index)
    low = block & 31
    high = jnp.concatenate([high, high], axis=1).astype(f32)
    low = jnp.concatenate([low, low], axis=1).astype(f32)
    row = iota((8, LANES), 0)
    for k in range(lists):
        tail = jnp.where(row == 0, high[k : k + 1], jnp.where(row == 1, low[k : k + 1], 0.0))
        buf[k, cap : cap + 8, :] = tail.astype(bf16)
    for load, store in zip(loads, stores):
        load.wait()
        store.start()
    for store in stores:
        store.wait()


def pack(values, block, count):
    lists, cap, width = values.shape
    shape = (lists, cap + 8, width)
    return pl.pallas_call(
        pack_kernel,
        out_shape=jax.ShapeDtypeStruct(shape, bf16),
        in_specs=[ANY, ANY, ANY],
        out_specs=ANY,
        scratch_shapes=[
            pltpu.VMEM((lists, cap), jnp.int32),
            pltpu.VMEM((1, lists), jnp.int32),
            pltpu.VMEM(shape, bf16),
            pltpu.SemaphoreType.DMA((10,)),
        ],
        compiler_params=params(60),
        name="pack",
    )(values, block, count.reshape(1, lists))


def to_column(row):
    return jnp.transpose(jnp.broadcast_to(row, (8, row.shape[1])))[:, 0:1]


def tower_kernel(
    dense_ref, w1_ref, b1_ref, w2_ref, b2_ref, head_ref,
    big_ref, h2_ref, s2_ref, q_ref, deep_ref,
    w1t, w2t,
):
    @pl.when(pl.program_id(0) == 0)
    def _():
        w1t[...] = jnp.transpose(w1_ref[...])
        w2t[...] = jnp.transpose(w2_ref[...])

    din, n1, n2 = dense_ref.shape[1], w1t.shape[0], w2t.shape[0]
    dense_t = jnp.transpose(dense_ref[...])
    big_ref[0:din, :] = dense_t
    pre1 = dot(w1t[...], dense_t) + to_column(b1_ref[...])
    gate1 = jax.nn.sigmoid(pre1)
    h1 = (pre1 * gate1).astype(bf16)
    big_ref[din : din + n1, :] = h1
    big_ref[din + n1 :, :] = jnp.zeros((n2, big_ref.shape[1]), bf16)
    slope1 = gate1 * (1.0 + pre1 * (1.0 - gate1))
    pre2 = dot(w2t[...], h1) + to_column(b2_ref[...])
    gate2 = jax.nn.sigmoid(pre2)
    h2 = (pre2 * gate2).astype(bf16)
    h2_ref[...] = h2
    head = head_ref[...]
    deep_ref[...] = dot(jnp.broadcast_to(head, (16, head.shape[1])), h2)[0:1]
    s2 = to_column(head.astype(f32)) * (gate2 * (1.0 + pre2 * (1.0 - gate2)))
    s2 = s2.astype(bf16)
    s2_ref[...] = s2
    q_ref[...] = (dot(w2_ref[...], s2) * slope1).astype(bf16)


def tower(dense, w1, b1, w2, b2, head):
    ex, din = dense.shape
    h1, h2 = w2.shape
    steps = 4
    be = ex // steps
    whole = lambda a: pl.BlockSpec(a.shape, lambda i: (0, 0))
    cols = lambda rows: pl.BlockSpec((rows, be), lambda i: (0, i))
    b1, b2, head = b1.reshape(1, h1), b2.reshape(1, h2), head.reshape(1, h2)
    return pl.pallas_call(
        tower_kernel,
        grid=(steps,),
        out_shape=(
            jax.ShapeDtypeStruct((din + h1 + h2, ex), bf16),
            jax.ShapeDtypeStruct((h2, ex), bf16),
            jax.ShapeDtypeStruct((h2, ex), bf16),
            jax.ShapeDtypeStruct((h1, ex), bf16),
            jax.ShapeDtypeStruct((1, ex), f32),
        ),
        in_specs=[
            pl.BlockSpec((be, din), lambda i: (i, 0)),
            whole(w1), whole(b1), whole(w2), whole(b2), whole(head),
        ],
        out_specs=(cols(din + h1 + h2), cols(h2), cols(h2), cols(h1), cols(1)),
        scratch_shapes=[pltpu.VMEM((h1, din), bf16), pltpu.VMEM((h2, h1), bf16)],
        compiler_params=params(62),
        cost_estimate=pl.CostEstimate(
            flops=2 * ex * (din * h1 + 2 * h1 * h2), bytes_accessed=12 << 20, transcendentals=ex * (h1 + h2)
        ),
        name="tower",
    )(dense, w1, b1, w2, b2, head)


def weight_kernel(z_ref, n_ref, out_ref):
    out_ref[...] = jnp.concatenate(split_two(wide_weight(z_ref[...], n_ref[...])), axis=1)


def weights(z, n):
    blocks, width = z.shape
    return pl.pallas_call(
        weight_kernel,
        out_shape=jax.ShapeDtypeStruct((blocks, 2 * width), bf16),
        in_specs=[VM, VM],
        out_specs=VM,
        compiler_params=params(6),
        cost_estimate=pl.CostEstimate(flops=10 * z.size, bytes_accessed=12 * z.size, transcendentals=2 * z.size),
        name="weights",
    )(z, n)


def four_lists(got_ref, at, cap):
    planes = [got_ref[at + k] for k in range(4)]
    values = jnp.concatenate([p[0:cap] for p in planes], axis=0)
    index = [p[cap : cap + 1].astype(f32) * 32.0 + p[cap + 1 : cap + 2].astype(f32) for p in planes]
    left = iota((1, LANES), 1) < cap
    pairs = [jnp.where(left, index[0], index[1]), jnp.where(left, index[2], index[3])]
    return values, jnp.concatenate(pairs, axis=1).astype(jnp.int32)


def logit_kernel(got_ref, wcat_ref, out_ref):
    lists = got_ref.shape[0]
    cap = got_ref.shape[1] - 8
    blocks = wcat_ref.shape[0]
    for at in range(0, lists, 4):
        values, index = four_lists(got_ref, at, cap)
        every = dot(wcat_ref[...], jnp.concatenate([values, values], axis=1), NT)
        picked = jnp.where(iota((blocks, 4 * cap), 0) == index, every, 0.0)
        logit = jnp.sum(picked, axis=0, keepdims=True)
        for k in range(4):
            out_ref[at + k] = logit[:, (k // 2) * LANES : (k // 2 + 1) * LANES]


def slot_logits(got, wcat):
    lists = got.shape[0]
    return pl.pallas_call(
        logit_kernel,
        out_shape=jax.ShapeDtypeStruct((lists, 1, LANES), f32),
        in_specs=[VM, VM],
        out_specs=VM,
        compiler_params=params(16),
        name="slot_logits",
    )(got, wcat)


def paired(example_ref):
    lists = example_ref.shape[0]
    example = [
        jnp.concatenate([example_ref[k : k + 1], example_ref[k + 1 : k + 2]], axis=1) for k in range(0, lists, 2)
    ]
    return [e >> 7 for e in example], [e & (LANES - 1) for e in example]


def half_copies(half, big_any, dense_t, h1, sems):
    n1 = 2 * (h1.shape[0] - ONES)
    each, packed = dense_t.shape[0] - ONES, n1 // 4
    copies = []
    for side in range(2):
        span = pl.ds(pl.multiple_of(2 * each + half * packed + side * 2 * packed, packed), packed)
        copies.append(pltpu.make_async_copy(big_any.at[span], h1.at[pl.ds(side * packed, packed)], sems.at[side]))
    rows = each // PIECES
    for k in range(PIECES):
        span = pl.ds(pl.multiple_of(half * each + k * rows, rows), rows)
        copies.append(pltpu.make_async_copy(big_any.at[span], dense_t.at[pl.ds(k * rows, rows)], sems.at[2 + k]))
    return copies


def half_gradients(residual, copies, s2, q, dense_t, h1, target):
    rows, first = residual.shape[0], (dense_t.shape[0] - ONES) // EIGHTHS
    packed, width = (h1.shape[0] - ONES) // 2 // EIGHTHS, s2.shape[0]
    each = first + packed
    dense_t[EIGHTHS * first :, :] = jnp.ones((ONES, dense_t.shape[1]), bf16)
    h1[2 * EIGHTHS * packed :, :] = jnp.ones((ONES, h1.shape[1]), bf16)
    dlogit = jnp.concatenate([residual[k : k + 1] for k in range(rows)], axis=1).astype(bf16)
    scale = dlogit.astype(f32)
    d_two = (s2[...].astype(f32) * scale).astype(bf16)
    d_one = (q[...].astype(f32) * scale).astype(bf16)
    copies[0].wait()
    copies[1].wait()
    second = dot(h1[...], d_two, NT)
    b_two = second[2 * EIGHTHS * packed : 2 * EIGHTHS * packed + 1]
    second = second.astype(bf16)
    for k in range(EIGHTHS):
        at, low = k * packed, (k + EIGHTHS) * packed
        target[k * each + first : (k + 1) * each, 0:width] = second[at : at + packed]
        target[k * each + first : (k + 1) * each, width:] = second[low : low + packed]
    for copy in copies[2:]:
        copy.wait()
    made = dot(dense_t[...], d_one, NT)
    b_one = made[EIGHTHS * first : EIGHTHS * first + 1]
    made = made.astype(bf16)
    for k in range(EIGHTHS):
        target[k * each : k * each + first, :] = made[k * first : (k + 1) * first]
    return dlogit, b_one, b_two


def half_scratch(big, n1):
    half = (big.shape[0] - n1 - n1 // 2) // 2
    return [
        pltpu.VMEM((half + ONES, big.shape[1]), bf16),
        pltpu.VMEM((n1 // 2 + ONES, big.shape[1]), bf16),
        pltpu.SemaphoreType.DMA((4 + PIECES,)),
    ]


def position():
    return lax.axis_index("blk") * lax.axis_size("rep") + lax.axis_index("rep")


def residual_kernel(
    logit_any, example_ref, deep_ref, label_ref, s2, q, big_any,
    prob_ref, residual_ref, send_ref, slot_ref,
    spread, marks, logit_ref, apart, dense_t, h1, sems,
):
    lists, cap = example_ref.shape
    rows = label_ref.shape[0]
    me = position()
    core = me & 1
    first = pltpu.make_async_copy(logit_any, logit_ref, sems.at[2 + PIECES])
    first.start()
    copies = half_copies(1 - core, big_any, dense_t, h1, sems)
    for copy in copies:
        copy.start()
    high, low = paired(example_ref)
    down_all = iota((LANES, LANES), 0)
    for k in range(lists // 2):
        marks[:, k * LANES : (k + 1) * LANES] = jnp.where(low[k] == down_all, 1.0, 0.0).astype(bf16)
    left = iota((1, LANES), 1) < cap
    down = iota((rows, LANES), 0)
    turned = lambda v: pltpu.roll(v, cap, 1)
    first.wait()
    for k in range(lists // 2):
        even, odd = logit_ref[2 * k], logit_ref[2 * k + 1]
        pair = jnp.where(core == 0, jnp.where(left, even, turned(odd)), jnp.where(left, turned(even), odd))
        part = jnp.where(high[k] == down, pair, 0.0)
        spread[:, k * LANES : (k + 1) * LANES] = jnp.concatenate(split_two(part), axis=0)
    wide = dot(spread[...], marks[...], NT)
    wide = wide[0:rows] + wide[rows:]
    deep = jnp.concatenate([deep_ref[:, k * LANES : (k + 1) * LANES] for k in range(rows)], axis=0)
    prob = jax.nn.sigmoid(wide + deep)
    prob_ref[...] = prob
    residual = prob - label_ref[...].astype(f32)
    residual_ref[...] = residual
    found = dot(jnp.concatenate(split_two(residual), axis=0), marks[...])
    found = found[0:rows] + found[rows:]
    for k in range(lists // 2):
        part = jnp.where(high[k] == down, found[:, k * LANES : (k + 1) * LANES], 0.0)
        both = jnp.sum(part, axis=0, keepdims=True)
        swapped = turned(both)
        for c, one in enumerate((jnp.where(left, both, swapped), jnp.where(left, swapped, both))):
            top, rest = split_two(one)
            apart[me ^ (2 * k + c)] = jnp.concatenate([top.astype(f32), rest.astype(f32)], axis=0)
    lines = [
        jnp.concatenate([apart[k + c, s : s + 1, :] for c in range(2) for s in range(2)], axis=1)
        for k in range(0, lists, 2)
    ]
    slot_ref[...] = jnp.concatenate(lines, axis=0).astype(bf16)
    half_gradients(residual, copies, s2, q, dense_t, h1, send_ref)


def residuals(logits, example, deep, labels, s2, q, big):
    lists, cap = example.shape
    rows = deep.shape[1] // LANES
    n1 = q.shape[0]
    half = (big.shape[0] - n1 - s2.shape[0]) // 2 + n1 // 4
    return pl.pallas_call(
        residual_kernel,
        out_shape=(
            jax.ShapeDtypeStruct((rows, LANES), f32),
            jax.ShapeDtypeStruct((rows, LANES), f32),
            jax.ShapeDtypeStruct((half, n1), bf16),
            jax.ShapeDtypeStruct((lists // 2, 4 * LANES), bf16),
        ),
        in_specs=[ANY] + [VM] * 5 + [HBM],
        out_specs=[VM, VM, VM, VM],
        scratch_shapes=[
            pltpu.VMEM((2 * rows, lists * cap), bf16),
            pltpu.VMEM((LANES, lists * cap), bf16),
            pltpu.VMEM(logits.shape, f32),
            pltpu.VMEM((lists, 2, LANES), f32),
        ]
        + half_scratch(big, n1),
        compiler_params=params(49),
        name="residuals",
    )(logits, example, deep, labels.reshape(rows, LANES), s2, q, big)


def gradient_kernel(residual_ref, s2, q, big_any, keep_ref, small_ref, dense_t, h1, sems):
    core = lax.axis_index("rep") & 1
    copies = half_copies(core, big_any, dense_t, h1, sems)
    for copy in copies:
        copy.start()
    _, b_one, b_two = half_gradients(residual_ref[...], copies, s2, q, dense_t, h1, keep_ref)
    small = jnp.concatenate([b_one, jnp.concatenate([b_two, jnp.zeros_like(b_two)], axis=1)], axis=0)
    small_ref[...] = jnp.concatenate(split_two(small), axis=0)


def gradients(residual, s2, q, big):
    n1, ex = q.shape
    half = (big.shape[0] - n1 - s2.shape[0]) // 2 + n1 // 4
    return pl.pallas_call(
        gradient_kernel,
        out_shape=(jax.ShapeDtypeStruct((half, n1), bf16), jax.ShapeDtypeStruct((4, n1), bf16)),
        in_specs=[VM] * 3 + [HBM],
        out_specs=[VM, VM],
        scratch_shapes=half_scratch(big, n1),
        compiler_params=params(49),
        cost_estimate=pl.CostEstimate(flops=2 * half * n1 * ex, bytes_accessed=6 << 20, transcendentals=0),
        name="gradients",
    )(residual, s2, q, big)


def head_kernel(residual_ref, small, h2, out_ref):
    residual = residual_ref[...]
    dlogit = jnp.concatenate([residual[k : k + 1] for k in range(residual.shape[0])], axis=1).astype(bf16)
    head = dot(jnp.broadcast_to(dlogit, (ONES, dlogit.shape[1])), h2[...], NT)[0:1]
    top, rest = split_two(jnp.concatenate([jnp.zeros_like(head), head], axis=1))
    zero = jnp.zeros_like(top)
    out_ref[...] = small[...] + jnp.concatenate([zero, top, zero, rest], axis=0)


def head_gradient(residual, small, h2):
    return pl.pallas_call(
        head_kernel,
        out_shape=jax.ShapeDtypeStruct(small.shape, bf16),
        in_specs=[VM] * 3,
        out_specs=VM,
        compiler_params=params(8),
        cost_estimate=pl.CostEstimate(flops=32 * h2.size, bytes_accessed=2 << 20, transcendentals=0),
        name="head_gradient",
    )(residual, small, h2)


def state_kernel(got_ref, res_ref, z_ref, n_ref, z_out, n_out):
    lists = got_ref.shape[0]
    me = position()
    cap = got_ref.shape[1] - 8
    blocks, width = z_ref.shape
    left = iota((1, LANES), 1) < cap
    grad = jnp.zeros((blocks, 2 * width), f32)
    for at in range(0, lists, 4):
        values, index = four_lists(got_ref, at, cap)
        apart = [me ^ (at + k) for k in range(4)]
        res = [res_ref[pl.ds((a & 1) * (lists // 2) + (a >> 1), 1), :] for a in apart]
        res = jnp.concatenate([jnp.where(left, res[0], res[1]), jnp.where(left, res[2], res[3])], axis=1)
        scaled = jnp.concatenate(split_two(values.astype(f32) * to_column(res)), axis=1)
        hit = jnp.where(iota((blocks, 4 * cap), 0) == index, 1.0, 0.0).astype(bf16)
        grad = grad + dot(hit, scaled)
    grad = grad[:, :width] + grad[:, width:]
    z, n = z_ref[...], n_ref[...]
    n_new = n + grad * grad
    sigma = (jnp.sqrt(n_new) - jnp.sqrt(n)) / alpha_rate
    n_out[...] = n_new
    z_out[...] = z + grad - sigma * wide_weight(z, n)


def new_states(got, res, z, n):
    return pl.pallas_call(
        state_kernel,
        out_shape=(jax.ShapeDtypeStruct(z.shape, f32), jax.ShapeDtypeStruct(z.shape, f32)),
        in_specs=[VM] * 4,
        out_specs=(VM, VM),
        compiler_params=params(16),
        cost_estimate=pl.CostEstimate(
            flops=4 * got.shape[0] * (got.shape[1] - 8) * z.size, bytes_accessed=4 << 20, transcendentals=2 * z.size
        ),
        name="new_states",
    )(got, res, z, n)


def place_kernel(items, follows, *refs):
    parts, refs = refs[: len(items)], refs[len(items) :]
    before, refs = (refs[:3], refs[3:]) if follows else (None, refs)
    w1_any, w2_any, *outs = refs[:-4]
    wide, narrow, small, sems = refs[-4:]
    me = position()
    quad = (me >> 1) & 3
    first, packed = wide.shape[1] // 2, narrow.shape[2] // 2
    each, width = first + packed, parts[0].shape[1]
    copies, total = [], before[2][...] if follows else 0.0
    for k, ((apart, swapped), part) in enumerate(zip(items, parts)):
        quarter = ((me & 1) ^ swapped) * 4 + (quad ^ apart)
        for t in range(2):
            at = t * each
            wide[k, t * first : (t + 1) * first, :] = part[at : at + first, :].astype(f32)
            for c in range(2):
                lanes = slice(c * (width // 2), (c + 1) * (width // 2))
                narrow[k, c, t * packed : (t + 1) * packed, :] = part[at + first : at + each, lanes].astype(f32)
        start = pl.multiple_of(quarter * 2 * first, 2 * first)
        copies.append(pltpu.make_async_copy(wide.at[k], w1_any.at[pl.ds(start, 2 * first)], sems.at[3 * k]))
        for c in range(2):
            start = pl.multiple_of((c * EIGHTHS + quarter) * 2 * packed, 2 * packed)
            target = w2_any.at[pl.ds(start, 2 * packed)]
            copies.append(pltpu.make_async_copy(narrow.at[k, c], target, sems.at[3 * k + 1 + c]))
        for copy in copies[-3:]:
            copy.start()
        extra = part[2 * each :, :].astype(f32)
        total = total + sum(extra[r : r + 2] for r in range(0, extra.shape[0], 2))
    if len(outs) > 1:
        small[0:1, :] = total[0:1]
        small[8:9, :] = total[1:2]
        small[16:17, 0 : width // 2] = total[1:2, width // 2 :]
        spans = ((0, width), (8, width // 2), (16, width // 2))
        for n, (out, (row, size)) in enumerate(zip(outs, spans)):
            copies.append(
                pltpu.make_async_copy(small.at[pl.ds(row, 1), pl.ds(0, size)], out, sems.at[3 * len(items) + n])
            )
            copies[-1].start()
    else:
        outs[0][...] = total
    for copy in copies:
        copy.wait()


def place(items, parts, first, packed, before=(), final=False):
    width, count = parts[0].shape[1], len(items)
    shapes = [(2 * EIGHTHS * first, width), (4 * EIGHTHS * packed, width // 2)]
    tail = [(1, width), (1, width // 2), (1, width // 2)] if final else [(2, width)]
    return pl.pallas_call(
        functools.partial(place_kernel, items, bool(before)),
        out_shape=[jax.ShapeDtypeStruct(t, f32) for t in shapes + tail],
        in_specs=[VM] * count + ([ANY, ANY, VM] if before else []),
        out_specs=[ANY, ANY] + [ANY if final else VM] * len(tail),
        input_output_aliases={count: 0, count + 1: 1} if before else {},
        scratch_shapes=[
            pltpu.VMEM((count, 2 * first, width), f32),
            pltpu.VMEM((count, 2, 2 * packed, width // 2), f32),
            pltpu.VMEM((24, width), f32),
            pltpu.SemaphoreType.DMA((3 * count + 3,)),
        ],
        compiler_params=params(16),
        cost_estimate=pl.CostEstimate(
            flops=count * first * width, bytes_accessed=16 * count * first * width, transcendentals=0
        ),
        name="place",
    )(*parts, *before)


def every_to_every(x):
    return lax.all_to_all(x, AXES, split_axis=0, concat_axis=0, tiled=True)


def swap(x, bit, devices):
    return lax.ppermute(x, AXES, [(i, i ^ bit) for i in range(devices)])


def add(*terms):
    return functools.reduce(jnp.add, [t.astype(f32) for t in terms]).astype(bf16)


def halves(x, side):
    rows = x.shape[0] // 2
    return lax.dynamic_slice_in_dim(x, side * rows, rows, 0)


def hold(*values):
    return lax.optimization_barrier(values)


def join(*parts):
    return jnp.concatenate(parts, axis=0)


def whole(p):
    rows = p.shape[0] // 2
    return p[:rows].astype(f32) + p[rows:].astype(f32)


def sum_everywhere(x, slots, extra, me, devices, states):
    bits = [1 << k for k in range(1, devices.bit_length() - 1)]
    quad, inner, last = bits[:2], bits[2:-1], bits[-1]
    at = (me // quad[0]) % 4
    others = [(3, quad[0] + quad[1]), (1, quad[0]), (2, quad[1])]
    wide = x.shape[1]
    slots = slots.reshape(-1, 4, wide)
    rows = x.shape[0] // EIGHTHS
    side = (me // inner[0]) % 2
    quarters = lambda v: [v] + [swap(v, bit, devices) for k, bit in sorted(others)]
    eighth = lambda k, t: lax.dynamic_slice_in_dim(x, ((at ^ k) * 2 + t) * rows, rows, 0)
    away = {k: swap(join(eighth(k, 1 - side), slots[:, k]), bit, devices) for k, bit in others}
    stay = {k: swap(eighth(k, side), bit, devices) for k, bit in others}
    slots = jnp.stack([slots[:, 0]] + [away[k][rows:] for k in (1, 2, 3)], axis=1)
    mine = None
    theirs = add(eighth(0, 1 - side), *[away[k][:rows] for k in (1, 2, 3)])
    for bit in inner + [last]:
        if bit == last:
            mine = theirs = x
        elif bit != inner[0]:
            side_now = (me // bit) % 2
            mine, theirs = halves(x, side_now), halves(x, 1 - side_now)
        slots = slots.reshape(slots.shape[0] // 2, 2, -1, wide)
        ride = slots[:, 1].reshape(-1, wide)
        n, m = theirs.shape[0], ride.shape[0]
        got = swap(join(theirs, ride, *([extra] if bit == last else [])), bit, devices)
        if bit == inner[0]:
            mine = add(eighth(0, side), *[stay[k] for k in (1, 2, 3)])
        x = add(mine, got[:n])
        slots = jnp.stack([slots[:, 0], got[n : n + m].reshape(slots[:, 0].shape)], axis=1)
        slots = slots.reshape(slots.shape[0], -1, wide)
    extra = join(extra, got[n + m :])
    slots = slots.reshape(-1, 2, wide // 2)
    far = swap(slots[:, 1], 1, devices)
    made = states(whole(jnp.stack([*jnp.split(join(slots[:, 0], far), 2, axis=1)]).reshape(-1, wide // 4)))
    for bit in reversed(inner):
        side_now = (me // bit) % 2
        got = swap(join(x, extra), bit, devices)
        n = x.shape[0]
        other = got[:n]
        x = join(jnp.where(side_now == 0, x, other), jnp.where(side_now == 0, other, x))
        extra = join(extra, got[n:])
    parts = quarters(join(x, extra))
    parts[0], *made = hold(parts[0], *made)
    return parts, made


def per_device(
    devices,
    dense,
    labels,
    tile_values,
    tile_block,
    tile_example,
    tile_count,
    z_state,
    n_state,
    w_one,
    b_one,
    w_two,
    b_two,
    head,
):
    n1, n2 = w_two.shape
    din = dense.shape[1]
    me = lax.axis_index(AXES)
    got = every_to_every(pack(tile_values, tile_block, tile_count))
    big, h2, s2, q, deep = tower(dense, w_one, b_one, w_two, b_two, head)
    deep, z_then, n_then = hold(deep, z_state, n_state)
    wcat = weights(z_then, n_then)
    got, deep = hold(got, deep)
    logits = slot_logits(got, wcat)
    logits = every_to_every(logits)
    prob, residual, send, slots = residuals(logits, tile_example, deep, labels, s2, q, big)
    keep, small = gradients(residual, s2, q, big)
    own = add(keep, swap(send, 1, devices))

    own, small, seen = hold(own, small, residual)
    small = head_gradient(seen, small, h2)

    def states(res):
        return new_states(got, res, z_state, n_state)

    parts, (z_new, n_new) = sum_everywhere(own, slots, small, me, devices, states)
    first, packed = din // 2 // EIGHTHS, n1 // 4 // EIGHTHS
    others = [swap(part, 1, devices) for part in parts]
    placed = place([(k, 0) for k in range(4)], parts, first, packed)
    grad_w_one, grad_w_two, grad_b_one, grad_b_two, grad_head = place(
        [(k, 1) for k in range(4)], others, first, packed, placed, True
    )
    return (
        prob.reshape(-1),
        z_new,
        n_new,
        grad_w_one,
        grad_b_one.reshape(-1),
        grad_w_two,
        grad_b_two.reshape(-1),
        grad_head.reshape(-1),
    )


def solution(mesh):
    placed = (
        P(AXES, None),
        P(AXES),
        P(AXES, None, None),
        P(AXES, None),
        P(AXES, None),
        P(AXES),
        P(AXES, None),
        P(AXES, None),
        P(),
        P(),
        P(),
        P(),
        P(),
    )
    devices = mesh.shape["blk"] * mesh.shape["rep"]
    return jax.shard_map(
        functools.partial(per_device, devices),
        mesh=mesh,
        in_specs=placed,
        out_specs=(P(AXES), P(AXES, None), P(AXES, None), P(), P(), P(), P(), P()),
        check_vma=False,
    )
```

```python
import functools
import jax
import jax.numpy as jnp
from jax import lax
from jax.experimental import pallas as pl
from jax.experimental.pallas import tpu as pltpu
from jax.sharding import PartitionSpec as P

alpha_rate = 0.5
beta_shift = 1.0
lasso_term = 0.5
ridge_term = 0.1

AXES = ("blk", "rep")
LANES = 128
EIGHTHS = 8
ONES = 16
PIECES = 2
f32 = jnp.float32
bf16 = jnp.bfloat16
NT = (((1,), (1,)), ((), ()))
NN = (((1,), (0,)), ((), ()))


def dot(a, b, dims=NN):
    return lax.dot_general(a, b, dims, preferred_element_type=f32)


def iota(shape, axis):
    return lax.broadcasted_iota(jnp.int32, shape, axis)


def split_two(x):
    top = x.astype(bf16)
    return top, (x - top.astype(f32)).astype(bf16)


def wide_weight(z, n):
    sign = jnp.where(z > 0, 1.0, jnp.where(z < 0, -1.0, 0.0))
    shrunk = z - sign * lasso_term
    denominator = (beta_shift + jnp.sqrt(n)) / alpha_rate + ridge_term
    return jnp.where(jnp.abs(z) > lasso_term, -shrunk / denominator, jnp.zeros_like(z))


def params(megabytes=40):
    return pltpu.CompilerParams(vmem_limit_bytes=megabytes << 20)


VM = pl.BlockSpec(memory_space=pltpu.VMEM)
ANY = pl.BlockSpec(memory_space=pl.ANY)
HBM = pl.BlockSpec(memory_space=pltpu.HBM)


def pack_kernel(values_any, block_any, count_any, out_any, block_ref, count_ref, buf, sems):
    lists, cap = block_ref.shape
    dead_index = 64
    parts = 4
    each = lists // parts
    small = [
        pltpu.make_async_copy(block_any, block_ref, sems.at[2 * parts]),
        pltpu.make_async_copy(count_any, count_ref, sems.at[2 * parts + 1]),
    ]
    spans = [pl.ds(k * each, each) for k in range(parts)]
    loads = [
        pltpu.make_async_copy(values_any.at[at], buf.at[at, pl.ds(0, cap)], sems.at[k])
        for k, at in enumerate(spans)
    ]
    stores = [
        pltpu.make_async_copy(buf.at[at], out_any.at[at], sems.at[parts + k]) for k, at in enumerate(spans)
    ]
    for copy in small + loads:
        copy.start()
    for copy in small:
        copy.wait()
    counts = jnp.sum(
        jnp.where(iota((lists, lists), 0) == iota((lists, lists), 1), count_ref[...], 0),
        axis=1,
        keepdims=True,
    )
    block = block_ref[...]
    high = jnp.where(iota((lists, cap), 1) < counts, block >> 5, dead_index)
    low = block & 31
    high = jnp.concatenate([high, high], axis=1).astype(f32)
    low = jnp.concatenate([low, low], axis=1).astype(f32)
    row = iota((8, LANES), 0)
    for k in range(lists):
        tail = jnp.where(row == 0, high[k : k + 1], jnp.where(row == 1, low[k : k + 1], 0.0))
        buf[k, cap : cap + 8, :] = tail.astype(bf16)
    for load, store in zip(loads, stores):
        load.wait()
        store.start()
    for store in stores:
        store.wait()


def pack(values, block, count):
    lists, cap, width = values.shape
    shape = (lists, cap + 8, width)
    return pl.pallas_call(
        pack_kernel,
        out_shape=jax.ShapeDtypeStruct(shape, bf16),
        in_specs=[ANY, ANY, ANY],
        out_specs=ANY,
        scratch_shapes=[
            pltpu.VMEM((lists, cap), jnp.int32),
            pltpu.VMEM((1, lists), jnp.int32),
            pltpu.VMEM(shape, bf16),
            pltpu.SemaphoreType.DMA((10,)),
        ],
        compiler_params=params(60),
        name="pack",
    )(values, block, count.reshape(1, lists))


def to_column(row):
    return jnp.transpose(jnp.broadcast_to(row, (8, row.shape[1])))[:, 0:1]


def tower_kernel(
    dense_ref, w1_ref, b1_ref, w2_ref, b2_ref, head_ref,
    big_ref, h2_ref, s2_ref, q_ref, deep_ref,
    w1t, w2t,
):
    @pl.when(pl.program_id(0) == 0)
    def _():
        w1t[...] = jnp.transpose(w1_ref[...])
        w2t[...] = jnp.transpose(w2_ref[...])

    din, n1, n2 = dense_ref.shape[1], w1t.shape[0], w2t.shape[0]
    dense_t = jnp.transpose(dense_ref[...])
    big_ref[0:din, :] = dense_t
    pre1 = dot(w1t[...], dense_t) + to_column(b1_ref[...])
    gate1 = jax.nn.sigmoid(pre1)
    h1 = (pre1 * gate1).astype(bf16)
    big_ref[din : din + n1, :] = h1
    big_ref[din + n1 :, :] = jnp.zeros((n2, big_ref.shape[1]), bf16)
    slope1 = gate1 * (1.0 + pre1 * (1.0 - gate1))
    pre2 = dot(w2t[...], h1) + to_column(b2_ref[...])
    gate2 = jax.nn.sigmoid(pre2)
    h2 = (pre2 * gate2).astype(bf16)
    h2_ref[...] = h2
    head = head_ref[...]
    deep_ref[...] = dot(jnp.broadcast_to(head, (16, head.shape[1])), h2)[0:1]
    s2 = to_column(head.astype(f32)) * (gate2 * (1.0 + pre2 * (1.0 - gate2)))
    s2 = s2.astype(bf16)
    s2_ref[...] = jnp.transpose(s2)
    q_ref[...] = jnp.transpose((dot(w2_ref[...], s2) * slope1).astype(bf16))


def tower(dense, w1, b1, w2, b2, head):
    ex, din = dense.shape
    h1, h2 = w2.shape
    steps = 4
    be = ex // steps
    whole = lambda a: pl.BlockSpec(a.shape, lambda i: (0, 0))
    cols = lambda rows: pl.BlockSpec((rows, be), lambda i: (0, i))
    down = lambda width: pl.BlockSpec((be, width), lambda i: (i, 0))
    b1, b2, head = b1.reshape(1, h1), b2.reshape(1, h2), head.reshape(1, h2)
    return pl.pallas_call(
        tower_kernel,
        grid=(steps,),
        out_shape=(
            jax.ShapeDtypeStruct((din + h1 + h2, ex), bf16),
            jax.ShapeDtypeStruct((h2, ex), bf16),
            jax.ShapeDtypeStruct((ex, h2), bf16),
            jax.ShapeDtypeStruct((ex, h1), bf16),
            jax.ShapeDtypeStruct((1, ex), f32),
        ),
        in_specs=[
            pl.BlockSpec((be, din), lambda i: (i, 0)),
            whole(w1), whole(b1), whole(w2), whole(b2), whole(head),
        ],
        out_specs=(cols(din + h1 + h2), cols(h2), down(h2), down(h1), cols(1)),
        scratch_shapes=[pltpu.VMEM((h1, din), bf16), pltpu.VMEM((h2, h1), bf16)],
        compiler_params=params(62),
        cost_estimate=pl.CostEstimate(
            flops=2 * ex * (din * h1 + 2 * h1 * h2), bytes_accessed=12 << 20, transcendentals=ex * (h1 + h2)
        ),
        name="tower",
    )(dense, w1, b1, w2, b2, head)


def weight_kernel(z_ref, n_ref, out_ref):
    out_ref[...] = jnp.concatenate(split_two(wide_weight(z_ref[...], n_ref[...])), axis=1)


def weights(z, n):
    blocks, width = z.shape
    return pl.pallas_call(
        weight_kernel,
        out_shape=jax.ShapeDtypeStruct((blocks, 2 * width), bf16),
        in_specs=[VM, VM],
        out_specs=VM,
        compiler_params=params(6),
        cost_estimate=pl.CostEstimate(flops=10 * z.size, bytes_accessed=12 * z.size, transcendentals=2 * z.size),
        name="weights",
    )(z, n)


def four_lists(got_ref, at, cap):
    planes = [got_ref[at + k] for k in range(4)]
    values = jnp.concatenate([p[0:cap] for p in planes], axis=0)
    index = [p[cap : cap + 1].astype(f32) * 32.0 + p[cap + 1 : cap + 2].astype(f32) for p in planes]
    left = iota((1, LANES), 1) < cap
    pairs = [jnp.where(left, index[0], index[1]), jnp.where(left, index[2], index[3])]
    return values, jnp.concatenate(pairs, axis=1).astype(jnp.int32)


def logit_kernel(got_ref, wcat_ref, out_ref):
    lists = got_ref.shape[0]
    cap = got_ref.shape[1] - 8
    blocks = wcat_ref.shape[0]
    for at in range(0, lists, 4):
        values, index = four_lists(got_ref, at, cap)
        every = dot(wcat_ref[...], jnp.concatenate([values, values], axis=1), NT)
        picked = jnp.where(iota((blocks, 4 * cap), 0) == index, every, 0.0)
        logit = jnp.sum(picked, axis=0, keepdims=True)
        for k in range(4):
            out_ref[at + k] = logit[:, (k // 2) * LANES : (k // 2 + 1) * LANES]


def slot_logits(got, wcat):
    lists = got.shape[0]
    return pl.pallas_call(
        logit_kernel,
        out_shape=jax.ShapeDtypeStruct((lists, 1, LANES), f32),
        in_specs=[VM, VM],
        out_specs=VM,
        compiler_params=params(16),
        name="slot_logits",
    )(got, wcat)


def paired(example_ref):
    lists = example_ref.shape[0]
    example = [
        jnp.concatenate([example_ref[k : k + 1], example_ref[k + 1 : k + 2]], axis=1) for k in range(0, lists, 2)
    ]
    return [e >> 7 for e in example], [e & (LANES - 1) for e in example]


def half_copies(half, big_any, dense_t, h1, sems):
    n1 = 2 * (h1.shape[0] - ONES)
    each, packed = dense_t.shape[0] - ONES, n1 // 4
    copies = []
    for side in range(2):
        span = pl.ds(pl.multiple_of(2 * each + half * packed + side * 2 * packed, packed), packed)
        copies.append(pltpu.make_async_copy(big_any.at[span], h1.at[pl.ds(side * packed, packed)], sems.at[side]))
    rows = each // PIECES
    for k in range(PIECES):
        span = pl.ds(pl.multiple_of(half * each + k * rows, rows), rows)
        copies.append(pltpu.make_async_copy(big_any.at[span], dense_t.at[pl.ds(k * rows, rows)], sems.at[2 + k]))
    return copies


def half_gradients(residual, copies, s2, q, dense_t, h1, target):
    rows, first = residual.shape[0], (dense_t.shape[0] - ONES) // EIGHTHS
    packed, width = (h1.shape[0] - ONES) // 2 // EIGHTHS, s2.shape[1]
    each = first + packed
    dense_t[EIGHTHS * first :, :] = jnp.ones((ONES, dense_t.shape[1]), bf16)
    h1[2 * EIGHTHS * packed :, :] = jnp.ones((ONES, h1.shape[1]), bf16)
    scale = jnp.transpose(residual.astype(bf16).astype(f32))

    def scaled(a):
        parts = [
            (a[k * LANES : (k + 1) * LANES, :].astype(f32) * scale[:, k : k + 1]).astype(bf16) for k in range(rows)
        ]
        return jnp.concatenate(parts, axis=0)

    d_two, d_one = scaled(s2), scaled(q)
    copies[0].wait()
    copies[1].wait()
    second = dot(h1[...], d_two)
    b_two = second[2 * EIGHTHS * packed : 2 * EIGHTHS * packed + 1]
    second = second.astype(bf16)
    for k in range(EIGHTHS):
        at, low = k * packed, (k + EIGHTHS) * packed
        target[k * each + first : (k + 1) * each, 0:width] = second[at : at + packed]
        target[k * each + first : (k + 1) * each, width:] = second[low : low + packed]
    for copy in copies[2:]:
        copy.wait()
    made = dot(dense_t[...], d_one)
    b_one = made[EIGHTHS * first : EIGHTHS * first + 1]
    made = made.astype(bf16)
    for k in range(EIGHTHS):
        target[k * each : k * each + first, :] = made[k * first : (k + 1) * first]
    return b_one, b_two


def half_scratch(big, n1):
    half = (big.shape[0] - n1 - n1 // 2) // 2
    return [
        pltpu.VMEM((half + ONES, big.shape[1]), bf16),
        pltpu.VMEM((n1 // 2 + ONES, big.shape[1]), bf16),
        pltpu.SemaphoreType.DMA((4 + PIECES,)),
    ]


def position():
    return lax.axis_index("blk") * lax.axis_size("rep") + lax.axis_index("rep")


def residual_kernel(
    logit_any, example_ref, deep_ref, label_ref, s2, q, big_any,
    prob_ref, residual_ref, send_ref, slot_ref,
    spread, marks, logit_ref, apart, dense_t, h1, sems,
):
    lists, cap = example_ref.shape
    rows = label_ref.shape[0]
    me = position()
    core = me & 1
    first = pltpu.make_async_copy(logit_any, logit_ref, sems.at[2 + PIECES])
    first.start()
    copies = half_copies(1 - core, big_any, dense_t, h1, sems)
    for copy in copies:
        copy.start()
    high, low = paired(example_ref)
    down_all = iota((LANES, LANES), 0)
    for k in range(lists // 2):
        marks[:, k * LANES : (k + 1) * LANES] = jnp.where(low[k] == down_all, 1.0, 0.0).astype(bf16)
    left = iota((1, LANES), 1) < cap
    down = iota((rows, LANES), 0)
    turned = lambda v: pltpu.roll(v, cap, 1)
    first.wait()
    for k in range(lists // 2):
        even, odd = logit_ref[2 * k], logit_ref[2 * k + 1]
        pair = jnp.where(core == 0, jnp.where(left, even, turned(odd)), jnp.where(left, turned(even), odd))
        part = jnp.where(high[k] == down, pair, 0.0)
        spread[:, k * LANES : (k + 1) * LANES] = jnp.concatenate(split_two(part), axis=0)
    wide = dot(spread[...], marks[...], NT)
    wide = wide[0:rows] + wide[rows:]
    deep = jnp.concatenate([deep_ref[:, k * LANES : (k + 1) * LANES] for k in range(rows)], axis=0)
    prob = jax.nn.sigmoid(wide + deep)
    prob_ref[...] = prob
    residual = prob - label_ref[...].astype(f32)
    residual_ref[...] = residual
    found = dot(jnp.concatenate(split_two(residual), axis=0), marks[...])
    found = found[0:rows] + found[rows:]
    for k in range(lists // 2):
        part = jnp.where(high[k] == down, found[:, k * LANES : (k + 1) * LANES], 0.0)
        both = jnp.sum(part, axis=0, keepdims=True)
        swapped = turned(both)
        for c, one in enumerate((jnp.where(left, both, swapped), jnp.where(left, swapped, both))):
            top, rest = split_two(one)
            apart[me ^ (2 * k + c)] = jnp.concatenate([top.astype(f32), rest.astype(f32)], axis=0)
    lines = [
        jnp.concatenate([apart[k + c, s : s + 1, :] for c in range(2) for s in range(2)], axis=1)
        for k in range(0, lists, 2)
    ]
    slot_ref[...] = jnp.concatenate(lines, axis=0).astype(bf16)
    half_gradients(residual, copies, s2, q, dense_t, h1, send_ref)


def residuals(logits, example, deep, labels, s2, q, big):
    lists, cap = example.shape
    rows = deep.shape[1] // LANES
    n1 = q.shape[1]
    half = (big.shape[0] - n1 - s2.shape[1]) // 2 + n1 // 4
    return pl.pallas_call(
        residual_kernel,
        out_shape=(
            jax.ShapeDtypeStruct((rows, LANES), f32),
            jax.ShapeDtypeStruct((rows, LANES), f32),
            jax.ShapeDtypeStruct((half, n1), bf16),
            jax.ShapeDtypeStruct((lists // 2, 4 * LANES), bf16),
        ),
        in_specs=[ANY] + [VM] * 5 + [HBM],
        out_specs=[VM, VM, VM, VM],
        scratch_shapes=[
            pltpu.VMEM((2 * rows, lists * cap), bf16),
            pltpu.VMEM((LANES, lists * cap), bf16),
            pltpu.VMEM(logits.shape, f32),
            pltpu.VMEM((lists, 2, LANES), f32),
        ]
        + half_scratch(big, n1),
        compiler_params=params(49),
        name="residuals",
    )(logits, example, deep, labels.reshape(rows, LANES), s2, q, big)


def gradient_kernel(residual_ref, s2, q, big_any, keep_ref, small_ref, dense_t, h1, sems):
    core = lax.axis_index("rep") & 1
    copies = half_copies(core, big_any, dense_t, h1, sems)
    for copy in copies:
        copy.start()
    b_one, b_two = half_gradients(residual_ref[...], copies, s2, q, dense_t, h1, keep_ref)
    small = jnp.concatenate([b_one, jnp.concatenate([b_two, jnp.zeros_like(b_two)], axis=1)], axis=0)
    small_ref[...] = jnp.concatenate(split_two(small), axis=0)


def gradients(residual, s2, q, big):
    ex, n1 = q.shape
    half = (big.shape[0] - n1 - s2.shape[1]) // 2 + n1 // 4
    return pl.pallas_call(
        gradient_kernel,
        out_shape=(jax.ShapeDtypeStruct((half, n1), bf16), jax.ShapeDtypeStruct((4, n1), bf16)),
        in_specs=[VM] * 3 + [HBM],
        out_specs=[VM, VM],
        scratch_shapes=half_scratch(big, n1),
        compiler_params=params(49),
        cost_estimate=pl.CostEstimate(flops=2 * half * n1 * ex, bytes_accessed=6 << 20, transcendentals=0),
        name="gradients",
    )(residual, s2, q, big)


def head_kernel(residual_ref, small, h2, out_ref):
    residual = residual_ref[...]
    dlogit = jnp.concatenate([residual[k : k + 1] for k in range(residual.shape[0])], axis=1).astype(bf16)
    head = dot(jnp.broadcast_to(dlogit, (ONES, dlogit.shape[1])), h2[...], NT)[0:1]
    top, rest = split_two(jnp.concatenate([jnp.zeros_like(head), head], axis=1))
    zero = jnp.zeros_like(top)
    out_ref[...] = small[...] + jnp.concatenate([zero, top, zero, rest], axis=0)


def head_gradient(residual, small, h2):
    return pl.pallas_call(
        head_kernel,
        out_shape=jax.ShapeDtypeStruct(small.shape, bf16),
        in_specs=[VM] * 3,
        out_specs=VM,
        compiler_params=params(8),
        cost_estimate=pl.CostEstimate(flops=32 * h2.size, bytes_accessed=2 << 20, transcendentals=0),
        name="head_gradient",
    )(residual, small, h2)


def state_kernel(got_ref, res_ref, z_ref, n_ref, z_out, n_out):
    lists = got_ref.shape[0]
    me = position()
    cap = got_ref.shape[1] - 8
    blocks, width = z_ref.shape
    left = iota((1, LANES), 1) < cap
    grad = jnp.zeros((blocks, 2 * width), f32)
    for at in range(0, lists, 4):
        values, index = four_lists(got_ref, at, cap)
        apart = [me ^ (at + k) for k in range(4)]
        res = [res_ref[pl.ds((a & 1) * (lists // 2) + (a >> 1), 1), :] for a in apart]
        res = jnp.concatenate([jnp.where(left, res[0], res[1]), jnp.where(left, res[2], res[3])], axis=1)
        scaled = jnp.concatenate(split_two(values.astype(f32) * to_column(res)), axis=1)
        hit = jnp.where(iota((blocks, 4 * cap), 0) == index, 1.0, 0.0).astype(bf16)
        grad = grad + dot(hit, scaled)
    grad = grad[:, :width] + grad[:, width:]
    z, n = z_ref[...], n_ref[...]
    n_new = n + grad * grad
    sigma = (jnp.sqrt(n_new) - jnp.sqrt(n)) / alpha_rate
    n_out[...] = n_new
    z_out[...] = z + grad - sigma * wide_weight(z, n)


def new_states(got, res, z, n):
    return pl.pallas_call(
        state_kernel,
        out_shape=(jax.ShapeDtypeStruct(z.shape, f32), jax.ShapeDtypeStruct(z.shape, f32)),
        in_specs=[VM] * 4,
        out_specs=(VM, VM),
        compiler_params=params(16),
        cost_estimate=pl.CostEstimate(
            flops=4 * got.shape[0] * (got.shape[1] - 8) * z.size, bytes_accessed=4 << 20, transcendentals=2 * z.size
        ),
        name="new_states",
    )(got, res, z, n)


def place_kernel(items, follows, *refs):
    parts, refs = refs[: len(items)], refs[len(items) :]
    before, refs = (refs[:3], refs[3:]) if follows else (None, refs)
    w1_any, w2_any, *outs = refs[:-4]
    wide, narrow, small, sems = refs[-4:]
    me = position()
    quad = (me >> 1) & 3
    first, packed = wide.shape[1] // 2, narrow.shape[2] // 2
    each, width = first + packed, parts[0].shape[1]
    copies, total = [], before[2][...] if follows else 0.0
    for k, ((apart, swapped), part) in enumerate(zip(items, parts)):
        quarter = ((me & 1) ^ swapped) * 4 + (quad ^ apart)
        for t in range(2):
            at = t * each
            wide[k, t * first : (t + 1) * first, :] = part[at : at + first, :].astype(f32)
            for c in range(2):
                lanes = slice(c * (width // 2), (c + 1) * (width // 2))
                narrow[k, c, t * packed : (t + 1) * packed, :] = part[at + first : at + each, lanes].astype(f32)
        start = pl.multiple_of(quarter * 2 * first, 2 * first)
        copies.append(pltpu.make_async_copy(wide.at[k], w1_any.at[pl.ds(start, 2 * first)], sems.at[3 * k]))
        for c in range(2):
            start = pl.multiple_of((c * EIGHTHS + quarter) * 2 * packed, 2 * packed)
            target = w2_any.at[pl.ds(start, 2 * packed)]
            copies.append(pltpu.make_async_copy(narrow.at[k, c], target, sems.at[3 * k + 1 + c]))
        for copy in copies[-3:]:
            copy.start()
        extra = part[2 * each :, :].astype(f32)
        total = total + sum(extra[r : r + 2] for r in range(0, extra.shape[0], 2))
    if len(outs) > 1:
        small[0:1, :] = total[0:1]
        small[8:9, :] = total[1:2]
        small[16:17, 0 : width // 2] = total[1:2, width // 2 :]
        spans = ((0, width), (8, width // 2), (16, width // 2))
        for n, (out, (row, size)) in enumerate(zip(outs, spans)):
            copies.append(
                pltpu.make_async_copy(small.at[pl.ds(row, 1), pl.ds(0, size)], out, sems.at[3 * len(items) + n])
            )
            copies[-1].start()
    else:
        outs[0][...] = total
    for copy in copies:
        copy.wait()


def place(items, parts, first, packed, before=(), final=False):
    width, count = parts[0].shape[1], len(items)
    shapes = [(2 * EIGHTHS * first, width), (4 * EIGHTHS * packed, width // 2)]
    tail = [(1, width), (1, width // 2), (1, width // 2)] if final else [(2, width)]
    return pl.pallas_call(
        functools.partial(place_kernel, items, bool(before)),
        out_shape=[jax.ShapeDtypeStruct(t, f32) for t in shapes + tail],
        in_specs=[VM] * count + ([ANY, ANY, VM] if before else []),
        out_specs=[ANY, ANY] + [ANY if final else VM] * len(tail),
        input_output_aliases={count: 0, count + 1: 1} if before else {},
        scratch_shapes=[
            pltpu.VMEM((count, 2 * first, width), f32),
            pltpu.VMEM((count, 2, 2 * packed, width // 2), f32),
            pltpu.VMEM((24, width), f32),
            pltpu.SemaphoreType.DMA((3 * count + 3,)),
        ],
        compiler_params=params(16),
        cost_estimate=pl.CostEstimate(
            flops=count * first * width, bytes_accessed=16 * count * first * width, transcendentals=0
        ),
        name="place",
    )(*parts, *before)


def every_to_every(x):
    return lax.all_to_all(x, AXES, split_axis=0, concat_axis=0, tiled=True)


def swap(x, bit, devices):
    return lax.ppermute(x, AXES, [(i, i ^ bit) for i in range(devices)])


def add(*terms):
    return functools.reduce(jnp.add, [t.astype(f32) for t in terms]).astype(bf16)


def halves(x, side):
    rows = x.shape[0] // 2
    return lax.dynamic_slice_in_dim(x, side * rows, rows, 0)


def hold(*values):
    return lax.optimization_barrier(values)


def join(*parts):
    return jnp.concatenate(parts, axis=0)


def whole(p):
    rows = p.shape[0] // 2
    return p[:rows].astype(f32) + p[rows:].astype(f32)


def sum_everywhere(x, slots, extra, me, devices, states):
    bits = [1 << k for k in range(1, devices.bit_length() - 1)]
    quad, inner, last = bits[:2], bits[2:-1], bits[-1]
    at = (me // quad[0]) % 4
    others = [(3, quad[0] + quad[1]), (1, quad[0]), (2, quad[1])]
    wide = x.shape[1]
    slots = slots.reshape(-1, 4, wide)
    rows = x.shape[0] // EIGHTHS
    side = (me // inner[0]) % 2
    quarters = lambda v: [v] + [swap(v, bit, devices) for k, bit in sorted(others)]
    eighth = lambda k, t: lax.dynamic_slice_in_dim(x, ((at ^ k) * 2 + t) * rows, rows, 0)
    away = {k: swap(join(eighth(k, 1 - side), slots[:, k]), bit, devices) for k, bit in others}
    stay = {k: swap(eighth(k, side), bit, devices) for k, bit in others}
    slots = jnp.stack([slots[:, 0]] + [away[k][rows:] for k in (1, 2, 3)], axis=1)
    mine = None
    theirs = add(eighth(0, 1 - side), *[away[k][:rows] for k in (1, 2, 3)])
    for bit in inner + [last]:
        if bit == last:
            mine = theirs = x
        elif bit != inner[0]:
            side_now = (me // bit) % 2
            mine, theirs = halves(x, side_now), halves(x, 1 - side_now)
        slots = slots.reshape(slots.shape[0] // 2, 2, -1, wide)
        ride = slots[:, 1].reshape(-1, wide)
        n, m = theirs.shape[0], ride.shape[0]
        got = swap(join(theirs, ride, *([extra] if bit == last else [])), bit, devices)
        if bit == inner[0]:
            mine = add(eighth(0, side), *[stay[k] for k in (1, 2, 3)])
        x = add(mine, got[:n])
        slots = jnp.stack([slots[:, 0], got[n : n + m].reshape(slots[:, 0].shape)], axis=1)
        slots = slots.reshape(slots.shape[0], -1, wide)
    extra = join(extra, got[n + m :])
    slots = slots.reshape(-1, 2, wide // 2)
    far = swap(slots[:, 1], 1, devices)
    made = states(whole(jnp.stack([*jnp.split(join(slots[:, 0], far), 2, axis=1)]).reshape(-1, wide // 4)))
    for bit in reversed(inner):
        side_now = (me // bit) % 2
        got = swap(join(x, extra), bit, devices)
        n = x.shape[0]
        other = got[:n]
        x = join(jnp.where(side_now == 0, x, other), jnp.where(side_now == 0, other, x))
        extra = join(extra, got[n:])
    parts = quarters(join(x, extra))
    parts[0], *made = hold(parts[0], *made)
    return parts, made


def per_device(
    devices,
    dense,
    labels,
    tile_values,
    tile_block,
    tile_example,
    tile_count,
    z_state,
    n_state,
    w_one,
    b_one,
    w_two,
    b_two,
    head,
):
    n1, n2 = w_two.shape
    din = dense.shape[1]
    me = lax.axis_index(AXES)
    got = every_to_every(pack(tile_values, tile_block, tile_count))
    big, h2, s2, q, deep = tower(dense, w_one, b_one, w_two, b_two, head)
    deep, z_then, n_then = hold(deep, z_state, n_state)
    wcat = weights(z_then, n_then)
    got, deep = hold(got, deep)
    logits = slot_logits(got, wcat)
    logits = every_to_every(logits)
    prob, residual, send, slots = residuals(logits, tile_example, deep, labels, s2, q, big)
    keep, small = gradients(residual, s2, q, big)
    own = add(keep, swap(send, 1, devices))

    own, small, seen = hold(own, small, residual)
    small = head_gradient(seen, small, h2)

    def states(res):
        return new_states(got, res, z_state, n_state)

    parts, (z_new, n_new) = sum_everywhere(own, slots, small, me, devices, states)
    first, packed = din // 2 // EIGHTHS, n1 // 4 // EIGHTHS
    others = [swap(part, 1, devices) for part in parts]
    placed = place([(k, 0) for k in range(4)], parts, first, packed)
    grad_w_one, grad_w_two, grad_b_one, grad_b_two, grad_head = place(
        [(k, 1) for k in range(4)], others, first, packed, placed, True
    )
    return (
        prob.reshape(-1),
        z_new,
        n_new,
        grad_w_one,
        grad_b_one.reshape(-1),
        grad_w_two,
        grad_b_two.reshape(-1),
        grad_head.reshape(-1),
    )


def solution(mesh):
    placed = (
        P(AXES, None),
        P(AXES),
        P(AXES, None, None),
        P(AXES, None),
        P(AXES, None),
        P(AXES),
        P(AXES, None),
        P(AXES, None),
        P(),
        P(),
        P(),
        P(),
        P(),
    )
    devices = mesh.shape["blk"] * mesh.shape["rep"]
    return jax.shard_map(
        functools.partial(per_device, devices),
        mesh=mesh,
        in_specs=placed,
        out_specs=(P(AXES), P(AXES, None), P(AXES, None), P(), P(), P(), P(), P()),
        check_vma=False,
    )
```

```python
import functools
import jax
import jax.numpy as jnp
from jax import lax
from jax.experimental import pallas as pl
from jax.experimental.pallas import tpu as pltpu
from jax.sharding import PartitionSpec as P

alpha_rate = 0.5
beta_shift = 1.0
lasso_term = 0.5
ridge_term = 0.1

AXES = ("blk", "rep")
LANES = 128
EIGHTHS = 8
ONES = 16
PIECES = 2
f32 = jnp.float32
bf16 = jnp.bfloat16
NT = (((1,), (1,)), ((), ()))
NN = (((1,), (0,)), ((), ()))


def dot(a, b, dims=NN):
    return lax.dot_general(a, b, dims, preferred_element_type=f32)


def iota(shape, axis):
    return lax.broadcasted_iota(jnp.int32, shape, axis)


def split_two(x):
    top = x.astype(bf16)
    return top, (x - top.astype(f32)).astype(bf16)


def wide_weight(z, n):
    sign = jnp.where(z > 0, 1.0, jnp.where(z < 0, -1.0, 0.0))
    shrunk = z - sign * lasso_term
    denominator = (beta_shift + jnp.sqrt(n)) / alpha_rate + ridge_term
    return jnp.where(jnp.abs(z) > lasso_term, -shrunk / denominator, jnp.zeros_like(z))


def params(megabytes=40):
    return pltpu.CompilerParams(vmem_limit_bytes=megabytes << 20)


VM = pl.BlockSpec(memory_space=pltpu.VMEM)
ANY = pl.BlockSpec(memory_space=pl.ANY)
HBM = pl.BlockSpec(memory_space=pltpu.HBM)


def pack_kernel(values_any, block_any, count_any, out_any, block_ref, count_ref, buf, sems):
    lists, cap = block_ref.shape
    dead_index = 64
    parts = 4
    each = lists // parts
    small = [
        pltpu.make_async_copy(block_any, block_ref, sems.at[2 * parts]),
        pltpu.make_async_copy(count_any, count_ref, sems.at[2 * parts + 1]),
    ]
    spans = [pl.ds(k * each, each) for k in range(parts)]
    loads = [
        pltpu.make_async_copy(values_any.at[at], buf.at[at, pl.ds(0, cap)], sems.at[k])
        for k, at in enumerate(spans)
    ]
    stores = [
        pltpu.make_async_copy(buf.at[at], out_any.at[at], sems.at[parts + k]) for k, at in enumerate(spans)
    ]
    for copy in small + loads:
        copy.start()
    for copy in small:
        copy.wait()
    counts = jnp.sum(
        jnp.where(iota((lists, lists), 0) == iota((lists, lists), 1), count_ref[...], 0),
        axis=1,
        keepdims=True,
    )
    block = block_ref[...]
    high = jnp.where(iota((lists, cap), 1) < counts, block >> 5, dead_index)
    low = block & 31
    high = jnp.concatenate([high, high], axis=1).astype(f32)
    low = jnp.concatenate([low, low], axis=1).astype(f32)
    row = iota((8, LANES), 0)
    for k in range(lists):
        tail = jnp.where(row == 0, high[k : k + 1], jnp.where(row == 1, low[k : k + 1], 0.0))
        buf[k, cap : cap + 8, :] = tail.astype(bf16)
    for load, store in zip(loads, stores):
        load.wait()
        store.start()
    for store in stores:
        store.wait()


def pack(values, block, count):
    lists, cap, width = values.shape
    shape = (lists, cap + 8, width)
    return pl.pallas_call(
        pack_kernel,
        out_shape=jax.ShapeDtypeStruct(shape, bf16),
        in_specs=[ANY, ANY, ANY],
        out_specs=ANY,
        scratch_shapes=[
            pltpu.VMEM((lists, cap), jnp.int32),
            pltpu.VMEM((1, lists), jnp.int32),
            pltpu.VMEM(shape, bf16),
            pltpu.SemaphoreType.DMA((10,)),
        ],
        compiler_params=params(60),
        name="pack",
    )(values, block, count.reshape(1, lists))


def to_column(row):
    return jnp.transpose(jnp.broadcast_to(row, (8, row.shape[1])))[:, 0:1]


def tower_kernel(
    dense_ref, w1_ref, b1_ref, w2_ref, b2_ref, head_ref,
    big_ref, h2_ref, s2_ref, q_ref, deep_ref,
    w1t, w2t,
):
    @pl.when(pl.program_id(0) == 0)
    def _():
        w1t[...] = jnp.transpose(w1_ref[...])
        w2t[...] = jnp.transpose(w2_ref[...])

    din, n1, n2 = dense_ref.shape[1], w1t.shape[0], w2t.shape[0]
    dense_t = jnp.transpose(dense_ref[...])
    big_ref[0:din, :] = dense_t
    pre1 = dot(w1t[...], dense_t) + to_column(b1_ref[...])
    gate1 = jax.nn.sigmoid(pre1)
    h1 = (pre1 * gate1).astype(bf16)
    big_ref[din : din + n1, :] = h1
    big_ref[din + n1 :, :] = jnp.zeros((n2, big_ref.shape[1]), bf16)
    slope1 = gate1 * (1.0 + pre1 * (1.0 - gate1))
    pre2 = dot(w2t[...], h1) + to_column(b2_ref[...])
    gate2 = jax.nn.sigmoid(pre2)
    h2 = (pre2 * gate2).astype(bf16)
    h2_ref[...] = h2
    head = head_ref[...]
    deep_ref[...] = dot(jnp.broadcast_to(head, (16, head.shape[1])), h2)[0:1]
    s2 = to_column(head.astype(f32)) * (gate2 * (1.0 + pre2 * (1.0 - gate2)))
    s2 = s2.astype(bf16)
    s2_ref[...] = jnp.transpose(s2)
    q_ref[...] = jnp.transpose((dot(w2_ref[...], s2) * slope1).astype(bf16))


def tower(dense, w1, b1, w2, b2, head):
    ex, din = dense.shape
    h1, h2 = w2.shape
    steps = 4
    be = ex // steps
    whole = lambda a: pl.BlockSpec(a.shape, lambda i: (0, 0))
    cols = lambda rows: pl.BlockSpec((rows, be), lambda i: (0, i))
    down = lambda width: pl.BlockSpec((be, width), lambda i: (i, 0))
    b1, b2, head = b1.reshape(1, h1), b2.reshape(1, h2), head.reshape(1, h2)
    return pl.pallas_call(
        tower_kernel,
        grid=(steps,),
        out_shape=(
            jax.ShapeDtypeStruct((din + h1 + h2, ex), bf16),
            jax.ShapeDtypeStruct((h2, ex), bf16),
            jax.ShapeDtypeStruct((ex, h2), bf16),
            jax.ShapeDtypeStruct((ex, h1), bf16),
            jax.ShapeDtypeStruct((1, ex), f32),
        ),
        in_specs=[
            pl.BlockSpec((be, din), lambda i: (i, 0)),
            whole(w1), whole(b1), whole(w2), whole(b2), whole(head),
        ],
        out_specs=(cols(din + h1 + h2), cols(h2), down(h2), down(h1), cols(1)),
        scratch_shapes=[pltpu.VMEM((h1, din), bf16), pltpu.VMEM((h2, h1), bf16)],
        compiler_params=params(62),
        cost_estimate=pl.CostEstimate(
            flops=2 * ex * (din * h1 + 2 * h1 * h2), bytes_accessed=12 << 20, transcendentals=ex * (h1 + h2)
        ),
        name="tower",
    )(dense, w1, b1, w2, b2, head)


def weight_kernel(z_ref, n_ref, out_ref):
    out_ref[...] = jnp.concatenate(split_two(wide_weight(z_ref[...], n_ref[...])), axis=1)


def weights(z, n):
    blocks, width = z.shape
    return pl.pallas_call(
        weight_kernel,
        out_shape=jax.ShapeDtypeStruct((blocks, 2 * width), bf16),
        in_specs=[VM, VM],
        out_specs=VM,
        compiler_params=params(6),
        cost_estimate=pl.CostEstimate(flops=10 * z.size, bytes_accessed=12 * z.size, transcendentals=2 * z.size),
        name="weights",
    )(z, n)


def four_lists(got_ref, at, cap):
    planes = [got_ref[at + k] for k in range(4)]
    values = jnp.concatenate([p[0:cap] for p in planes], axis=0)
    index = [p[cap : cap + 1].astype(f32) * 32.0 + p[cap + 1 : cap + 2].astype(f32) for p in planes]
    left = iota((1, LANES), 1) < cap
    pairs = [jnp.where(left, index[0], index[1]), jnp.where(left, index[2], index[3])]
    return values, jnp.concatenate(pairs, axis=1).astype(jnp.int32)


def logit_kernel(got_ref, wcat_ref, out_ref):
    lists = got_ref.shape[0]
    cap = got_ref.shape[1] - 8
    blocks = wcat_ref.shape[0]
    for at in range(0, lists, 4):
        values, index = four_lists(got_ref, at, cap)
        every = dot(wcat_ref[...], jnp.concatenate([values, values], axis=1), NT)
        picked = jnp.where(iota((blocks, 4 * cap), 0) == index, every, 0.0)
        logit = jnp.sum(picked, axis=0, keepdims=True)
        for k in range(4):
            out_ref[at + k] = logit[:, (k // 2) * LANES : (k // 2 + 1) * LANES]


def slot_logits(got, wcat):
    lists = got.shape[0]
    return pl.pallas_call(
        logit_kernel,
        out_shape=jax.ShapeDtypeStruct((lists, 1, LANES), f32),
        in_specs=[VM, VM],
        out_specs=VM,
        compiler_params=params(16),
        name="slot_logits",
    )(got, wcat)


def paired(example_ref):
    lists = example_ref.shape[0]
    example = [
        jnp.concatenate([example_ref[k : k + 1], example_ref[k + 1 : k + 2]], axis=1) for k in range(0, lists, 2)
    ]
    return [e >> 7 for e in example], [e & (LANES - 1) for e in example]


def half_copies(half, big_any, dense_t, h1, sems):
    n1 = 2 * (h1.shape[0] - ONES)
    each, packed = dense_t.shape[0] - ONES, n1 // 4
    copies = []
    for side in range(2):
        span = pl.ds(pl.multiple_of(2 * each + half * packed + side * 2 * packed, packed), packed)
        copies.append(pltpu.make_async_copy(big_any.at[span], h1.at[pl.ds(side * packed, packed)], sems.at[side]))
    span = pl.ds(pl.multiple_of(half * each, each), each)
    columns = dense_t.shape[1] // PIECES
    for k in range(PIECES):
        lanes = pl.ds(k * columns, columns)
        copies.append(
            pltpu.make_async_copy(big_any.at[span, lanes], dense_t.at[pl.ds(0, each), lanes], sems.at[2 + k])
        )
    return copies


def half_gradients(residual, copies, s2, q, dense_t, h1, target):
    rows, first = residual.shape[0], (dense_t.shape[0] - ONES) // EIGHTHS
    packed, width = (h1.shape[0] - ONES) // 2 // EIGHTHS, s2.shape[1]
    each = first + packed
    dense_t[EIGHTHS * first :, :] = jnp.ones((ONES, dense_t.shape[1]), bf16)
    h1[2 * EIGHTHS * packed :, :] = jnp.ones((ONES, h1.shape[1]), bf16)
    scale = jnp.transpose(residual.astype(bf16).astype(f32))

    def scaled(a):
        parts = [
            (a[k * LANES : (k + 1) * LANES, :].astype(f32) * scale[:, k : k + 1]).astype(bf16) for k in range(rows)
        ]
        return jnp.concatenate(parts, axis=0)

    d_two, d_one = scaled(s2), scaled(q)
    copies[0].wait()
    copies[1].wait()
    second = dot(h1[...], d_two)
    b_two = second[2 * EIGHTHS * packed : 2 * EIGHTHS * packed + 1]
    second = second.astype(bf16)
    for k in range(EIGHTHS):
        at, low = k * packed, (k + EIGHTHS) * packed
        target[k * each + first : (k + 1) * each, 0:width] = second[at : at + packed]
        target[k * each + first : (k + 1) * each, width:] = second[low : low + packed]
    columns = dense_t.shape[1] // PIECES
    made = 0.0
    for k, copy in enumerate(copies[2:]):
        copy.wait()
        span = slice(k * columns, (k + 1) * columns)
        made = made + dot(dense_t[:, span], d_one[span, :])
    b_one = made[EIGHTHS * first : EIGHTHS * first + 1]
    made = made.astype(bf16)
    for k in range(EIGHTHS):
        target[k * each : k * each + first, :] = made[k * first : (k + 1) * first]
    return b_one, b_two


def half_scratch(big, n1):
    half = (big.shape[0] - n1 - n1 // 2) // 2
    return [
        pltpu.VMEM((half + ONES, big.shape[1]), bf16),
        pltpu.VMEM((n1 // 2 + ONES, big.shape[1]), bf16),
        pltpu.SemaphoreType.DMA((4 + PIECES,)),
    ]


def position():
    return lax.axis_index("blk") * lax.axis_size("rep") + lax.axis_index("rep")


def residual_kernel(
    logit_any, example_ref, deep_ref, label_ref, s2, q, big_any,
    prob_ref, residual_ref, send_ref, slot_ref,
    spread, marks, logit_ref, apart, dense_t, h1, sems,
):
    lists, cap = example_ref.shape
    rows = label_ref.shape[0]
    me = position()
    core = me & 1
    first = pltpu.make_async_copy(logit_any, logit_ref, sems.at[2 + PIECES])
    first.start()
    copies = half_copies(1 - core, big_any, dense_t, h1, sems)
    for copy in copies:
        copy.start()
    high, low = paired(example_ref)
    down_all = iota((LANES, LANES), 0)
    for k in range(lists // 2):
        marks[:, k * LANES : (k + 1) * LANES] = jnp.where(low[k] == down_all, 1.0, 0.0).astype(bf16)
    left = iota((1, LANES), 1) < cap
    down = iota((rows, LANES), 0)
    turned = lambda v: pltpu.roll(v, cap, 1)
    first.wait()
    for k in range(lists // 2):
        even, odd = logit_ref[2 * k], logit_ref[2 * k + 1]
        pair = jnp.where(core == 0, jnp.where(left, even, turned(odd)), jnp.where(left, turned(even), odd))
        part = jnp.where(high[k] == down, pair, 0.0)
        spread[:, k * LANES : (k + 1) * LANES] = jnp.concatenate(split_two(part), axis=0)
    wide = dot(spread[...], marks[...], NT)
    wide = wide[0:rows] + wide[rows:]
    deep = jnp.concatenate([deep_ref[:, k * LANES : (k + 1) * LANES] for k in range(rows)], axis=0)
    prob = jax.nn.sigmoid(wide + deep)
    prob_ref[...] = prob
    residual = prob - label_ref[...].astype(f32)
    residual_ref[...] = residual
    found = dot(jnp.concatenate(split_two(residual), axis=0), marks[...])
    found = found[0:rows] + found[rows:]
    for k in range(lists // 2):
        part = jnp.where(high[k] == down, found[:, k * LANES : (k + 1) * LANES], 0.0)
        both = jnp.sum(part, axis=0, keepdims=True)
        swapped = turned(both)
        for c, one in enumerate((jnp.where(left, both, swapped), jnp.where(left, swapped, both))):
            top, rest = split_two(one)
            apart[me ^ (2 * k + c)] = jnp.concatenate([top.astype(f32), rest.astype(f32)], axis=0)
    lines = [
        jnp.concatenate([apart[k + c, s : s + 1, :] for c in range(2) for s in range(2)], axis=1)
        for k in range(0, lists, 2)
    ]
    slot_ref[...] = jnp.concatenate(lines, axis=0).astype(bf16)
    half_gradients(residual, copies, s2, q, dense_t, h1, send_ref)


def residuals(logits, example, deep, labels, s2, q, big):
    lists, cap = example.shape
    rows = deep.shape[1] // LANES
    n1 = q.shape[1]
    half = (big.shape[0] - n1 - s2.shape[1]) // 2 + n1 // 4
    return pl.pallas_call(
        residual_kernel,
        out_shape=(
            jax.ShapeDtypeStruct((rows, LANES), f32),
            jax.ShapeDtypeStruct((rows, LANES), f32),
            jax.ShapeDtypeStruct((half, n1), bf16),
            jax.ShapeDtypeStruct((lists // 2, 4 * LANES), bf16),
        ),
        in_specs=[ANY] + [VM] * 5 + [HBM],
        out_specs=[VM, VM, VM, VM],
        scratch_shapes=[
            pltpu.VMEM((2 * rows, lists * cap), bf16),
            pltpu.VMEM((LANES, lists * cap), bf16),
            pltpu.VMEM(logits.shape, f32),
            pltpu.VMEM((lists, 2, LANES), f32),
        ]
        + half_scratch(big, n1),
        compiler_params=params(49),
        name="residuals",
    )(logits, example, deep, labels.reshape(rows, LANES), s2, q, big)


def gradient_kernel(residual_ref, s2, q, big_any, keep_ref, small_ref, dense_t, h1, sems):
    core = lax.axis_index("rep") & 1
    copies = half_copies(core, big_any, dense_t, h1, sems)
    for copy in copies:
        copy.start()
    b_one, b_two = half_gradients(residual_ref[...], copies, s2, q, dense_t, h1, keep_ref)
    small = jnp.concatenate([b_one, jnp.concatenate([b_two, jnp.zeros_like(b_two)], axis=1)], axis=0)
    small_ref[...] = jnp.concatenate(split_two(small), axis=0)


def gradients(residual, s2, q, big):
    ex, n1 = q.shape
    half = (big.shape[0] - n1 - s2.shape[1]) // 2 + n1 // 4
    return pl.pallas_call(
        gradient_kernel,
        out_shape=(jax.ShapeDtypeStruct((half, n1), bf16), jax.ShapeDtypeStruct((4, n1), bf16)),
        in_specs=[VM] * 3 + [HBM],
        out_specs=[VM, VM],
        scratch_shapes=half_scratch(big, n1),
        compiler_params=params(49),
        cost_estimate=pl.CostEstimate(flops=2 * half * n1 * ex, bytes_accessed=6 << 20, transcendentals=0),
        name="gradients",
    )(residual, s2, q, big)


def head_kernel(residual_ref, small, h2, out_ref):
    residual = residual_ref[...]
    dlogit = jnp.concatenate([residual[k : k + 1] for k in range(residual.shape[0])], axis=1).astype(bf16)
    head = dot(jnp.broadcast_to(dlogit, (ONES, dlogit.shape[1])), h2[...], NT)[0:1]
    top, rest = split_two(jnp.concatenate([jnp.zeros_like(head), head], axis=1))
    zero = jnp.zeros_like(top)
    out_ref[...] = small[...] + jnp.concatenate([zero, top, zero, rest], axis=0)


def head_gradient(residual, small, h2):
    return pl.pallas_call(
        head_kernel,
        out_shape=jax.ShapeDtypeStruct(small.shape, bf16),
        in_specs=[VM] * 3,
        out_specs=VM,
        compiler_params=params(8),
        cost_estimate=pl.CostEstimate(flops=32 * h2.size, bytes_accessed=2 << 20, transcendentals=0),
        name="head_gradient",
    )(residual, small, h2)


def state_kernel(got_ref, res_ref, z_ref, n_ref, z_out, n_out):
    lists = got_ref.shape[0]
    me = position()
    cap = got_ref.shape[1] - 8
    blocks, width = z_ref.shape
    left = iota((1, LANES), 1) < cap
    grad = jnp.zeros((blocks, 2 * width), f32)
    for at in range(0, lists, 4):
        values, index = four_lists(got_ref, at, cap)
        apart = [me ^ (at + k) for k in range(4)]
        res = [res_ref[pl.ds((a & 1) * (lists // 2) + (a >> 1), 1), :] for a in apart]
        res = jnp.concatenate([jnp.where(left, res[0], res[1]), jnp.where(left, res[2], res[3])], axis=1)
        scaled = jnp.concatenate(split_two(values.astype(f32) * to_column(res)), axis=1)
        hit = jnp.where(iota((blocks, 4 * cap), 0) == index, 1.0, 0.0).astype(bf16)
        grad = grad + dot(hit, scaled)
    grad = grad[:, :width] + grad[:, width:]
    z, n = z_ref[...], n_ref[...]
    n_new = n + grad * grad
    sigma = (jnp.sqrt(n_new) - jnp.sqrt(n)) / alpha_rate
    n_out[...] = n_new
    z_out[...] = z + grad - sigma * wide_weight(z, n)


def new_states(got, res, z, n):
    return pl.pallas_call(
        state_kernel,
        out_shape=(jax.ShapeDtypeStruct(z.shape, f32), jax.ShapeDtypeStruct(z.shape, f32)),
        in_specs=[VM] * 4,
        out_specs=(VM, VM),
        compiler_params=params(16),
        cost_estimate=pl.CostEstimate(
            flops=4 * got.shape[0] * (got.shape[1] - 8) * z.size, bytes_accessed=4 << 20, transcendentals=2 * z.size
        ),
        name="new_states",
    )(got, res, z, n)


def place_kernel(items, follows, *refs):
    parts, refs = refs[: len(items)], refs[len(items) :]
    before, refs = (refs[:3], refs[3:]) if follows else (None, refs)
    w1_any, w2_any, *outs = refs[:-4]
    wide, narrow, small, sems = refs[-4:]
    me = position()
    quad = (me >> 1) & 3
    first, packed = wide.shape[1] // 2, narrow.shape[2] // 2
    each, width = first + packed, parts[0].shape[1]
    copies, total = [], before[2][...] if follows else 0.0
    for k, ((apart, swapped), part) in enumerate(zip(items, parts)):
        quarter = ((me & 1) ^ swapped) * 4 + (quad ^ apart)
        for t in range(2):
            at = t * each
            wide[k, t * first : (t + 1) * first, :] = part[at : at + first, :].astype(f32)
            for c in range(2):
                lanes = slice(c * (width // 2), (c + 1) * (width // 2))
                narrow[k, c, t * packed : (t + 1) * packed, :] = part[at + first : at + each, lanes].astype(f32)
        start = pl.multiple_of(quarter * 2 * first, 2 * first)
        copies.append(pltpu.make_async_copy(wide.at[k], w1_any.at[pl.ds(start, 2 * first)], sems.at[3 * k]))
        for c in range(2):
            start = pl.multiple_of((c * EIGHTHS + quarter) * 2 * packed, 2 * packed)
            target = w2_any.at[pl.ds(start, 2 * packed)]
            copies.append(pltpu.make_async_copy(narrow.at[k, c], target, sems.at[3 * k + 1 + c]))
        for copy in copies[-3:]:
            copy.start()
        extra = part[2 * each :, :].astype(f32)
        total = total + sum(extra[r : r + 2] for r in range(0, extra.shape[0], 2))
    if len(outs) > 1:
        small[0:1, :] = total[0:1]
        small[8:9, :] = total[1:2]
        small[16:17, 0 : width // 2] = total[1:2, width // 2 :]
        spans = ((0, width), (8, width // 2), (16, width // 2))
        for n, (out, (row, size)) in enumerate(zip(outs, spans)):
            copies.append(
                pltpu.make_async_copy(small.at[pl.ds(row, 1), pl.ds(0, size)], out, sems.at[3 * len(items) + n])
            )
            copies[-1].start()
    else:
        outs[0][...] = total
    for copy in copies:
        copy.wait()


def place(items, parts, first, packed, before=(), final=False):
    width, count = parts[0].shape[1], len(items)
    shapes = [(2 * EIGHTHS * first, width), (4 * EIGHTHS * packed, width // 2)]
    tail = [(1, width), (1, width // 2), (1, width // 2)] if final else [(2, width)]
    return pl.pallas_call(
        functools.partial(place_kernel, items, bool(before)),
        out_shape=[jax.ShapeDtypeStruct(t, f32) for t in shapes + tail],
        in_specs=[VM] * count + ([ANY, ANY, VM] if before else []),
        out_specs=[ANY, ANY] + [ANY if final else VM] * len(tail),
        input_output_aliases={count: 0, count + 1: 1} if before else {},
        scratch_shapes=[
            pltpu.VMEM((count, 2 * first, width), f32),
            pltpu.VMEM((count, 2, 2 * packed, width // 2), f32),
            pltpu.VMEM((24, width), f32),
            pltpu.SemaphoreType.DMA((3 * count + 3,)),
        ],
        compiler_params=params(16),
        cost_estimate=pl.CostEstimate(
            flops=count * first * width, bytes_accessed=16 * count * first * width, transcendentals=0
        ),
        name="place",
    )(*parts, *before)


def every_to_every(x):
    return lax.all_to_all(x, AXES, split_axis=0, concat_axis=0, tiled=True)


def swap(x, bit, devices):
    return lax.ppermute(x, AXES, [(i, i ^ bit) for i in range(devices)])


def add(*terms):
    return functools.reduce(jnp.add, [t.astype(f32) for t in terms]).astype(bf16)


def halves(x, side):
    rows = x.shape[0] // 2
    return lax.dynamic_slice_in_dim(x, side * rows, rows, 0)


def hold(*values):
    return lax.optimization_barrier(values)


def join(*parts):
    return jnp.concatenate(parts, axis=0)


def whole(p):
    rows = p.shape[0] // 2
    return p[:rows].astype(f32) + p[rows:].astype(f32)


def sum_everywhere(x, slots, extra, me, devices, states):
    bits = [1 << k for k in range(1, devices.bit_length() - 1)]
    quad, inner, last = bits[:2], bits[2:-1], bits[-1]
    at = (me // quad[0]) % 4
    others = [(3, quad[0] + quad[1]), (1, quad[0]), (2, quad[1])]
    wide = x.shape[1]
    slots = slots.reshape(-1, 4, wide)
    rows = x.shape[0] // EIGHTHS
    side = (me // inner[0]) % 2
    quarters = lambda v: [v] + [swap(v, bit, devices) for k, bit in sorted(others)]
    eighth = lambda k, t: lax.dynamic_slice_in_dim(x, ((at ^ k) * 2 + t) * rows, rows, 0)
    away = {k: swap(join(eighth(k, 1 - side), slots[:, k]), bit, devices) for k, bit in others}
    stay = {k: swap(eighth(k, side), bit, devices) for k, bit in others}
    slots = jnp.stack([slots[:, 0]] + [away[k][rows:] for k in (1, 2, 3)], axis=1)
    mine = None
    theirs = add(eighth(0, 1 - side), *[away[k][:rows] for k in (1, 2, 3)])
    for bit in inner + [last]:
        if bit == last:
            mine = theirs = x
        elif bit != inner[0]:
            side_now = (me // bit) % 2
            mine, theirs = halves(x, side_now), halves(x, 1 - side_now)
        slots = slots.reshape(slots.shape[0] // 2, 2, -1, wide)
        ride = slots[:, 1].reshape(-1, wide)
        n, m = theirs.shape[0], ride.shape[0]
        got = swap(join(theirs, ride, *([extra] if bit == last else [])), bit, devices)
        if bit == inner[0]:
            mine = add(eighth(0, side), *[stay[k] for k in (1, 2, 3)])
        x = add(mine, got[:n])
        slots = jnp.stack([slots[:, 0], got[n : n + m].reshape(slots[:, 0].shape)], axis=1)
        slots = slots.reshape(slots.shape[0], -1, wide)
    extra = join(extra, got[n + m :])
    slots = slots.reshape(-1, 2, wide // 2)
    far = swap(slots[:, 1], 1, devices)
    made = states(whole(jnp.stack([*jnp.split(join(slots[:, 0], far), 2, axis=1)]).reshape(-1, wide // 4)))
    for bit in reversed(inner):
        side_now = (me // bit) % 2
        got = swap(join(x, extra), bit, devices)
        n = x.shape[0]
        other = got[:n]
        x = join(jnp.where(side_now == 0, x, other), jnp.where(side_now == 0, other, x))
        extra = join(extra, got[n:])
    parts = quarters(join(x, extra))
    parts[0], *made = hold(parts[0], *made)
    return parts, made


def per_device(
    devices,
    dense,
    labels,
    tile_values,
    tile_block,
    tile_example,
    tile_count,
    z_state,
    n_state,
    w_one,
    b_one,
    w_two,
    b_two,
    head,
):
    n1, n2 = w_two.shape
    din = dense.shape[1]
    me = lax.axis_index(AXES)
    got = every_to_every(pack(tile_values, tile_block, tile_count))
    big, h2, s2, q, deep = tower(dense, w_one, b_one, w_two, b_two, head)
    deep, z_then, n_then = hold(deep, z_state, n_state)
    wcat = weights(z_then, n_then)
    got, deep = hold(got, deep)
    logits = slot_logits(got, wcat)
    logits = every_to_every(logits)
    prob, residual, send, slots = residuals(logits, tile_example, deep, labels, s2, q, big)
    keep, small = gradients(residual, s2, q, big)
    own = add(keep, swap(send, 1, devices))

    own, small, seen = hold(own, small, residual)
    small = head_gradient(seen, small, h2)

    def states(res):
        return new_states(got, res, z_state, n_state)

    parts, (z_new, n_new) = sum_everywhere(own, slots, small, me, devices, states)
    first, packed = din // 2 // EIGHTHS, n1 // 4 // EIGHTHS
    others = [swap(part, 1, devices) for part in parts]
    placed = place([(k, 0) for k in range(4)], parts, first, packed)
    grad_w_one, grad_w_two, grad_b_one, grad_b_two, grad_head = place(
        [(k, 1) for k in range(4)], others, first, packed, placed, True
    )
    return (
        prob.reshape(-1),
        z_new,
        n_new,
        grad_w_one,
        grad_b_one.reshape(-1),
        grad_w_two,
        grad_b_two.reshape(-1),
        grad_head.reshape(-1),
    )


def solution(mesh):
    placed = (
        P(AXES, None),
        P(AXES),
        P(AXES, None, None),
        P(AXES, None),
        P(AXES, None),
        P(AXES),
        P(AXES, None),
        P(AXES, None),
        P(),
        P(),
        P(),
        P(),
        P(),
    )
    devices = mesh.shape["blk"] * mesh.shape["rep"]
    return jax.shard_map(
        functools.partial(per_device, devices),
        mesh=mesh,
        in_specs=placed,
        out_specs=(P(AXES), P(AXES, None), P(AXES, None), P(), P(), P(), P(), P()),
        check_vma=False,
    )
```
